128 devices in a mesh: dp: 16 (over x, y), head: 8 (over z, core).
Axes of the slice: x: 4, y: 4, z: 4, core: 2. Of those that a mesh axis runs over, the one named last changes fastest.
Arguments:
- inputs: bfloat16 [4096, 3072], P('dp'), may hold values from -6 to 6
- grad_y: bfloat16 [4096, 3072], P('dp'), may hold values from -1.5 to 1.5
- q_pre: bfloat16 [4096, 3072], P('dp', 'head'), may hold values from -6 to 6
- f_pre: bfloat16 [4096, 3072], P('dp', 'head'), may hold values from -6 to 10
- v_pre: bfloat16 [4096, 3072], P('dp', 'head'), may hold values from -6 to 6
- w_out: bfloat16 [3072, 3072], P('head'), may hold values from -0.109375 to 0.109375
- err_in: bfloat16 [16, 3, 3072, 3072], P('dp', None, None, 'head'), may hold values from -3 to 3
- err_out: bfloat16 [16, 3072, 3072], P('dp', 'head'), may hold values from -3 to 3
- basis_in: float32 [3, 64, 3072], P(None, None, 'head'), may hold values from -6 to 6
- basis_out: float32 [64, 3072], replicated, may hold values from -6 to 6
Outputs:
- new_err_in: bfloat16 [16, 3, 3072, 3072], P('dp', None, None, 'head')
- new_err_out: bfloat16 [16, 3072, 3072], P('dp', 'head')
- factor_in: float32 [3, 64, 3072], P(None, None, 'head')
- factor_out: float32 [64, 3072], replicated
The draws below stay inside these ranges and needn't reach their ends.
All inputs are finite; a program needn't handle non-finite values.
Results may differ from the reference program's by a relative error of at most 0.0072.
The reference program's roundings to bfloat16 on the way (of `grad_o` and `hidden`) count: a program that leaves them out, or rounds other values in their place, can miss the bound.
Values sent between devices are 32-bit elements; how exact they have to be, the bound alone decides.
No kernel may reach another device: no remote copies, remote signals or barrier semaphores. Data moves between devices by JAX's collectives and lax.ppermute only.
A program may use at most 128 MiB of HBM per device.

```python
import jax
import jax.numpy as jnp
from jax import lax

D = 3072
DK = 128
RANK = 64
SEQ = 256
INNER = 3072
TOK_DEV = 256
TOKEN_TOTAL = 4096
N_DP = 16


def draw_f_pre(key, part):
    key = jax.random.fold_in(key, 11)
    speed_random_key, jitter_random_key, spike_random_key = jax.random.split(key, 3)
    speed_draw = jnp.exp(jax.random.uniform(speed_random_key, (1, INNER), minval=jnp.log(0.5 / SEQ), maxval=jnp.log(1.0 / 20.0)))
    jitter_draw = 0.5 * jax.random.normal(jitter_random_key, (TOKEN_TOTAL, INNER))
    spike_draw = (jax.random.randint(spike_random_key, (TOKEN_TOTAL, 1), 0, 64) == 0).astype(jnp.float32)
    value_sample = jnp.log((1.0 - speed_draw) / speed_draw) + jitter_draw - 4.0 * spike_draw
    return jnp.clip(value_sample, -6.0, 10.0).astype(jnp.bfloat16)


def block_levels(stream_key, shape, cuts, least, top_value):
    factor_of = 1.0
    for position, blocks in cuts:
        draws = jax.random.uniform(jax.random.fold_in(jax.random.fold_in(stream_key, 6), position), (blocks,), jnp.float32, least / len(cuts), top_value / len(cuts))
        factor_of = factor_of * jnp.repeat(jnp.exp(draws), shape[position] // blocks).reshape((-1,) + (1,) * (len(shape) - 1 - position))
    return factor_of


def centred(own_key, dims, scale, bound, cuts=(), dtype=jnp.bfloat16):
    result = scale * jax.random.normal(own_key, dims, jnp.float32)
    if cuts:
        result = result * block_levels(own_key, dims, cuts, -0.22, 0.18)
    return jnp.clip(result, -bound, bound).astype(dtype)


def setup_inputs(seed: int = 0) -> dict:
    keys = jax.random.split(jax.random.key(seed), 11)
    inputs = centred(keys[0], (TOKEN_TOTAL, D), 1.0, 6.0, ((0, 16),))
    grad_y = centred(keys[1], (TOKEN_TOTAL, D), 0.25, 1.5, ((0, 16),))
    q_pre = centred(keys[2], (TOKEN_TOTAL, INNER), 1.0, 6.0, ((0, 16), (1, 8)))
    f_pre = draw_f_pre(jax.random.fold_in(keys[10], 71), 0)
    v_pre = centred(keys[4], (TOKEN_TOTAL, INNER), 1.0, 6.0, ((0, 16), (1, 8)))
    w_out = centred(keys[5], (INNER, D), INNER ** -0.5, 0.109375, ((0, 8),))
    err_in = centred(keys[6], (N_DP, 3, D, INNER), 0.5, 3.0, ((0, 16), (3, 8)))
    err_out = centred(keys[7], (N_DP, INNER, D), 0.5, 3.0, ((0, 16), (1, 8)))
    basis_in = centred(keys[8], (3, RANK, INNER), 1.0, 6.0, ((2, 8),), jnp.float32)
    basis_out = centred(keys[9], (RANK, D), 1.0, 6.0, (), jnp.float32)
    return dict(inputs=inputs, grad_y=grad_y, q_pre=q_pre, f_pre=f_pre, v_pre=v_pre, w_out=w_out, err_in=err_in, err_out=err_out, basis_in=basis_in, basis_out=basis_out)


EXACT = lax.Precision.HIGHEST

def sequence_grads(pieces):
    q_rows, f_rows, v_rows, cotangent = pieces
    heads_all = q_rows.shape[1] // DK

    def forward(q_part, f_part, v_part):
        queries = jax.nn.silu(q_part).reshape(-1, heads_all, DK)
        decays = jax.nn.sigmoid(f_part).reshape(-1, heads_all, DK)
        gate_keys = jax.nn.sigmoid(-f_part).reshape(-1, heads_all, DK)
        values = v_part.reshape(-1, heads_all, DK)

        def advance(state, items):
            query_now, decay_now, key_now, value_now = items
            state = decay_now[:, :, None] * state + key_now[:, :, None] * value_now[:, None, :]
            return (state, jnp.einsum('ha,hab->hb', query_now, state, precision=EXACT))
        initial = jnp.zeros((heads_all, DK, DK), jnp.float32)
        _, outputs = lax.scan(advance, initial, (queries, decays, gate_keys, values))
        return outputs.reshape(-1, heads_all * DK)
    hidden, pullback = jax.vjp(forward, q_rows, f_rows, v_rows)
    grad_q, grad_f, grad_v = pullback(cotangent)
    return (hidden, grad_q, grad_f, grad_v)

def orthonormal(rows):
    gram = jnp.dot(rows, rows.T, precision=EXACT)
    return jax.scipy.linalg.solve_triangular(jnp.linalg.cholesky(gram), rows, lower=True)

def reference(inputs, grad_y, q_pre, f_pre, v_pre, w_out, err_in, err_out, basis_in, basis_out):
    grad_o = jnp.dot(grad_y.astype(jnp.float32), w_out.T.astype(jnp.float32), preferred_element_type=jnp.float32).astype(jnp.bfloat16)
    count = q_pre.shape[0] // SEQ

    def shaped(array):
        return array.astype(jnp.float32).reshape(count, SEQ, array.shape[1])
    hidden, grad_q, grad_f, grad_v = lax.map(sequence_grads, (shaped(q_pre), shaped(f_pre), shaped(v_pre), shaped(grad_o)))
    hidden = hidden.reshape(N_DP, TOK_DEV, INNER).astype(jnp.bfloat16)
    grads_pre = jnp.stack([grad_q, grad_f, grad_v]).reshape(3, N_DP, TOK_DEV, INNER).astype(jnp.bfloat16)
    input_groups = inputs.reshape(N_DP, TOK_DEV, D)
    output_groups = grad_y.reshape(N_DP, TOK_DEV, D)

    def moments(index):
        x_rows = input_groups[index].astype(jnp.float32)
        g_rows = grads_pre[:, index].astype(jnp.float32)
        moment_in = jnp.einsum('td,ptc->pdc', x_rows, g_rows, precision=EXACT) + err_in[index].astype(jnp.float32)
        moment_out = jnp.einsum('tc,td->cd', hidden[index].astype(jnp.float32), output_groups[index].astype(jnp.float32), precision=EXACT) + err_out[index].astype(jnp.float32)
        return (moment_in, moment_out)

    def left_terms(index):
        moment_in, moment_out = moments(index)
        left_in = jnp.einsum('prc,pdc->prd', basis_in, moment_in, precision=EXACT)
        left_out = jnp.einsum('rd,cd->rc', basis_out, moment_out, precision=EXACT)
        return (left_in, left_out)
    indices = jnp.arange(N_DP)
    left_in, left_out = lax.map(left_terms, indices)
    ortho_in = jax.vmap(orthonormal)(lax.optimization_barrier(jnp.sum(left_in, axis=0)))
    ortho_out = orthonormal(lax.optimization_barrier(jnp.sum(left_out, axis=0)))

    def right_terms(index):
        moment_in, moment_out = moments(index)
        right_in = jnp.einsum('prd,pdc->prc', ortho_in, moment_in, precision=EXACT)
        right_out = jnp.einsum('rc,cd->rd', ortho_out, moment_out, precision=EXACT)
        return (right_in, right_out)
    right_in, right_out = lax.map(right_terms, indices)
    factor_in = lax.optimization_barrier(jnp.sum(right_in, axis=0)) / N_DP
    factor_out = lax.optimization_barrier(jnp.sum(right_out, axis=0)) / N_DP

    def remainders(index):
        moment_in, moment_out = moments(index)
        rest_in = moment_in - jnp.einsum('prd,prc->pdc', ortho_in, factor_in, precision=EXACT)
        rest_out = moment_out - jnp.einsum('rc,rd->cd', ortho_out, factor_out, precision=EXACT)
        return (rest_in.astype(jnp.bfloat16), rest_out.astype(jnp.bfloat16))
    new_err_in, new_err_out = lax.map(remainders, indices)
    return (new_err_in, new_err_out, factor_in, factor_out)
```

```python
import functools

import jax
import jax.numpy as jnp
from jax import lax
from jax.experimental import pallas as pl
from jax.experimental.pallas import tpu as pltpu
from jax.sharding import Mesh, PartitionSpec as P

TOK = 256
DK = 128
HEADS = 3
COLS = HEADS * DK
RANK = 64
D = 3072
HALF = D // 2
TILE = 512
STEPS = HALF // TILE
CT = TILE // 128
N_DP = 16
CHIPS = 64
L_ROWS = 12 * 3 * RANK
LO_ROWS = HEADS * RANK
ROWS1 = 2560
RI_ROWS = 9 * RANK
RO_ROWS = 12 * RANK
ROWS2 = 1536

f32 = jnp.float32
bf16 = jnp.bfloat16
EXACT = lax.Precision.HIGHEST
VMEM = 48 * 1024 * 1024
SHIFTS = ((0, 1), (0, 2), (0, 3))


def nn(a, b):
    return lax.dot_general(a, b, (((1,), (0,)), ((), ())), preferred_element_type=f32)


def nt(a, b):
    return lax.dot_general(a, b, (((1,), (1,)), ((), ())), preferred_element_type=f32)


def tn(a, b):
    return lax.dot_general(a, b, (((0,), (0,)), ((), ())), preferred_element_type=f32)


def exact_nn(a, b):
    return lax.dot_general(a, b, (((1,), (0,)), ((), ())), precision=EXACT, preferred_element_type=f32)


def exact_nt(a, b):
    return lax.dot_general(a, b, (((1,), (1,)), ((), ())), precision=EXACT, preferred_element_type=f32)


def split2(a):
    high = a.astype(bf16)
    return high, (a - high.astype(f32)).astype(bf16)


def split3(a):
    high = a.astype(bf16)
    rest = a - high.astype(f32)
    mid = rest.astype(bf16)
    return high, mid, (rest - mid.astype(f32)).astype(bf16)


def stacked(a):
    return jnp.concatenate(split2(a), axis=0)


def folded(a):
    half = a.shape[0] // 2
    return a[:half] + a[half:]


def recurrence_kernel(gy_ref, w_ref, q_ref, f_ref, v_ref, hid_ref, grad_ref):
    grad_o = nt(gy_ref[...], w_ref[...]).astype(bf16)
    q = q_ref[...].astype(f32)
    f = f_ref[...].astype(f32)
    v = v_ref[...]
    q_gate = 1.0 / (1.0 + jnp.exp(-q))
    query = q * q_gate
    small = jnp.exp(-jnp.abs(f))
    key = jnp.where(f >= 0, small, 1.0) / (1.0 + small)
    decay = jnp.where(f >= 0, 1.0, small) / (1.0 + small)
    log_decay = jnp.minimum(f, 0.0) - jnp.log1p(small)

    row = lax.broadcasted_iota(jnp.int32, (TOK, TOK), 0)
    col = lax.broadcasted_iota(jnp.int32, (TOK, TOK), 1)
    lower = jnp.where(row >= col, 1.0, 0.0).astype(bf16)
    upper = jnp.where(row <= col, 1.0, 0.0).astype(bf16)
    differ = row ^ col
    high, mid, low = split3(log_decay)
    running = nn(lower, high) + (nn(lower, mid) + nn(lower, low))

    scores = jnp.zeros((TOK, TOK), f32)
    grad_s = split2(nt(grad_o, v))
    grad_st = split2(nt(v, grad_o))
    grad_query = jnp.zeros((TOK, DK), f32)
    grad_key = jnp.zeros((TOK, DK), f32)
    for size in (128, 64, 32, 16, 8):
        blocks = running.reshape(TOK // (2 * size), 2 * size, DK)
        spread = (blocks - blocks[:, size - 1 : size, :]).reshape(TOK, DK)
        if size > 8:
            q_scale = jnp.exp(jnp.minimum(spread, 0.0))
            k_scale = jnp.exp(jnp.minimum(-spread, 0.0))
            within = (differ >= size) & (differ < 2 * size)
            mask = within & (row > col)
            mask_t = within & (row < col)
        else:
            q_scale = jnp.exp(spread)
            k_scale = jnp.exp(-spread)
            within = differ < 2 * size
            mask = within & (row >= col)
            mask_t = within & (row <= col)
        q_high, q_low = split2(query * q_scale)
        k_high, k_low = split2(key * k_scale)
        level = nt(
            jnp.concatenate([q_high, q_high, q_low], axis=1),
            jnp.concatenate([k_high, k_low, k_high], axis=1),
        )
        scores = jnp.where(mask, level, scores)
        keep = jnp.where(mask, 1.0, 0.0).astype(bf16)
        keep_t = jnp.where(mask_t, 1.0, 0.0).astype(bf16)
        both = nn(grad_s[0] * keep, jnp.concatenate([k_high, k_low], axis=1))
        grad_query += q_scale * (both[:, :DK] + both[:, DK:] + nn(grad_s[1] * keep, k_high))
        both = nn(grad_st[0] * keep_t, jnp.concatenate([q_high, q_low], axis=1))
        grad_key += k_scale * (both[:, :DK] + both[:, DK:] + nn(grad_st[1] * keep_t, q_high))
    s_high, s_low = split2(scores)
    hid_ref[...] = (nn(s_high, v) + nn(s_low, v)).astype(bf16)
    grad_v = tn(s_high, grad_o) + tn(s_low, grad_o)
    high, mid, low = split3(query * grad_query - key * grad_key)
    grad_decay = nn(upper, high) + (nn(upper, mid) + nn(upper, low))
    grad_ref[0] = (grad_query * (q_gate + query * (1.0 - q_gate))).astype(bf16)
    grad_ref[1] = (key * (grad_decay - grad_key * decay)).astype(bf16)
    grad_ref[2] = grad_v.astype(bf16)


def recurrence(grad_y, w_out, q_pre, f_pre, v_pre):
    per_head = pl.BlockSpec((TOK, DK), lambda h: (0, h))
    return pl.pallas_call(
        recurrence_kernel,
        grid=(HEADS,),
        in_specs=[
            pl.BlockSpec((TOK, D), lambda h: (0, 0)),
            pl.BlockSpec((DK, D), lambda h: (h, 0)),
            per_head,
            per_head,
            per_head,
        ],
        out_specs=[per_head, pl.BlockSpec((3, TOK, DK), lambda h: (0, 0, h))],
        out_shape=[
            jax.ShapeDtypeStruct((TOK, COLS), bf16),
            jax.ShapeDtypeStruct((3, TOK, COLS), bf16),
        ],
        compiler_params=pltpu.CompilerParams(vmem_limit_bytes=VMEM),
        name="recurrence",
    )(grad_y, w_out, q_pre, f_pre, v_pre)


def tiles_of(a):
    return [a[:, 128 * i : 128 * (i + 1)] for i in range(a.shape[1] // 128)]


def left_kernel(half_ref, x_ref, gy_ref, grads_ref, hid_ref, err_in_ref, err_out_ref, basis_in_ref,
                basis_out_ref, left_ref, left_out_ref, token_scr):
    step = pl.program_id(0)

    @pl.when(step == 0)
    def _():
        for p in range(3):
            token_scr[p] = stacked(folded(nt(stacked(basis_in_ref[p]), grads_ref[p])))
        left_out_ref[...] = jnp.zeros_like(left_out_ref)

    for p in range(3):
        part = nn(token_scr[p], x_ref[...]) + nt(stacked(basis_in_ref[p]), err_in_ref[p])
        for i, tile in enumerate(tiles_of(folded(part))):
            left_ref[i, RANK * p : RANK * (p + 1), :] = tile
    basis = stacked(basis_out_ref[...])
    tokens = stacked(folded(nt(basis, gy_ref[...])))
    part = folded(nt(basis, err_out_ref[...]) + nn(tokens, hid_ref[...]))
    for i, tile in enumerate(tiles_of(part)):
        left_out_ref[i] += tile


def left(half, inputs, grad_y, grads, hidden, err_in, err_out, basis_in, basis_out):
    return pl.pallas_call(
        left_kernel,
        grid_spec=pltpu.PrefetchScalarGridSpec(
            num_scalar_prefetch=1,
            grid=(STEPS,),
            in_specs=[
                pl.BlockSpec((TOK, TILE), lambda j, h: (0, h[0] * STEPS + j)),
                pl.BlockSpec((TOK, TILE), lambda j, h: (0, h[0] * STEPS + j)),
                pl.BlockSpec((3, TOK, COLS), lambda j, h: (0, 0, 0)),
                pl.BlockSpec((TOK, COLS), lambda j, h: (0, 0)),
                pl.BlockSpec((3, TILE, COLS), lambda j, h: (0, h[0] * STEPS + j, 0)),
                pl.BlockSpec((COLS, TILE), lambda j, h: (0, h[0] * STEPS + j)),
                pl.BlockSpec((3, RANK, COLS), lambda j, h: (0, 0, 0)),
                pl.BlockSpec((RANK, TILE), lambda j, h: (0, h[0] * STEPS + j)),
            ],
            out_specs=[
                pl.BlockSpec((CT, 3 * RANK, 128), lambda j, h: (j, 0, 0)),
                pl.BlockSpec((HEADS, RANK, 128), lambda j, h: (0, 0, 0)),
            ],
            scratch_shapes=[pltpu.VMEM((3, 2 * RANK, TOK), bf16)],
        ),
        out_shape=[
            jax.ShapeDtypeStruct((12, 3 * RANK, 128), f32),
            jax.ShapeDtypeStruct((HEADS, RANK, 128), f32),
        ],
        compiler_params=pltpu.CompilerParams(vmem_limit_bytes=VMEM),
        name="left",
    )(half, inputs, grad_y, grads, hidden, err_in, err_out, basis_in, basis_out)


def wide(block, rows):
    return jnp.concatenate([block[i * rows : (i + 1) * rows] for i in range(block.shape[0] // rows)], axis=1)


def right_kernel(halves_ref, left_ref, left_out_ref, x_ref, gy_ref, hid_ref, err_in_ref, err_out_ref,
                 right_ref, token_ref, right_out_ref, gram_ref, out_scr):
    step = pl.program_id(0)

    @pl.when(step == 0)
    def _():
        right_ref[...] = jnp.zeros_like(right_ref)
        token_ref[...] = jnp.zeros_like(token_ref)
        left_out = wide(left_out_ref[...], RANK)
        gram_ref[...] = jnp.concatenate([exact_nt(left_out, left_out), jnp.zeros((RANK, RANK), f32)], axis=1)
        factor = stacked(left_out)
        out_scr[:, :COLS] = factor
        out_scr[:, COLS:] = stacked(folded(nt(factor, hid_ref[...])))

    rows = wide(left_ref[...], 3 * RANK)
    for p in range(3):
        factor = stacked(rows[RANK * p : RANK * (p + 1)])
        right_ref[p] += folded(nn(factor, err_in_ref[p]))
        token_ref[p] += folded(nt(factor, x_ref[...]))
    part = folded(nn(out_scr[:, :COLS], err_out_ref[...]) + nn(out_scr[:, COLS:], gy_ref[...]))
    for i, tile in enumerate(tiles_of(part)):
        right_out_ref[i] = tile


def right(halves, gathered, own, inputs, grad_y, hidden, err_in, err_out):
    return pl.pallas_call(
        right_kernel,
        grid_spec=pltpu.PrefetchScalarGridSpec(
            num_scalar_prefetch=1,
            grid=(STEPS,),
            in_specs=[
                pl.BlockSpec((CT * 3 * RANK, 128), lambda j, h: (j, 0)),
                pl.BlockSpec((LO_ROWS, 128), lambda j, h: (L_ROWS // LO_ROWS, 0)),
                pl.BlockSpec((TOK, TILE), lambda j, h: (0, h[0] * STEPS + j)),
                pl.BlockSpec((TOK, TILE), lambda j, h: (0, h[1] * STEPS + j)),
                pl.BlockSpec((TOK, COLS), lambda j, h: (0, 0)),
                pl.BlockSpec((3, TILE, COLS), lambda j, h: (0, h[0] * STEPS + j, 0)),
                pl.BlockSpec((COLS, TILE), lambda j, h: (0, h[1] * STEPS + j)),
            ],
            out_specs=[
                pl.BlockSpec((3, RANK, COLS), lambda j, h: (0, 0, 0)),
                pl.BlockSpec((3, RANK, TOK), lambda j, h: (0, 0, 0)),
                pl.BlockSpec((CT, RANK, 128), lambda j, h: (j, 0, 0)),
                pl.BlockSpec((RANK, 128), lambda j, h: (0, 0)),
            ],
            scratch_shapes=[pltpu.VMEM((2 * RANK, COLS + TOK), bf16)],
        ),
        out_shape=[
            jax.ShapeDtypeStruct((3, RANK, COLS), f32),
            jax.ShapeDtypeStruct((3, RANK, TOK), f32),
            jax.ShapeDtypeStruct((12, RANK, 128), f32),
            jax.ShapeDtypeStruct((RANK, 128), f32),
        ],
        compiler_params=pltpu.CompilerParams(vmem_limit_bytes=VMEM),
        name="right",
    )(halves, gathered, own, inputs, grad_y, hidden, err_in, err_out)


def join_kernel(right_a_ref, right_b_ref, token_a_ref, token_b_ref, grads_ref, keep_ref, arrived_ref, out_ref):
    for p in range(3):
        tokens = stacked(token_a_ref[p] + token_b_ref[p])
        total = right_a_ref[p] + right_b_ref[p] + folded(nn(tokens, grads_ref[p]))
        for i, tile in enumerate(tiles_of(total)):
            out_ref[pl.ds((HEADS * p + i) * RANK, RANK), :] = tile
    out_ref[RI_ROWS : RI_ROWS + RO_ROWS, :] = keep_ref[...] + arrived_ref[...]
    out_ref[RI_ROWS + RO_ROWS :, :] = jnp.zeros((ROWS2 - RI_ROWS - RO_ROWS, 128), f32)


def join(*operands):
    return pl.pallas_call(
        join_kernel,
        out_shape=jax.ShapeDtypeStruct((ROWS2, 128), f32),
        compiler_params=pltpu.CompilerParams(vmem_limit_bytes=VMEM),
        name="join",
    )(*operands)


def ortho_kernel(own_half_ref, own_ref, other_ref, left_out_ref, gram_out_ref, x_ref, turned_ref, ortho_ref,
                 ortho_out_ref, inverse_ref, work_scr):
    step = pl.program_id(0)

    @pl.when(step == 0)
    def _():
        eye = jnp.where(
            lax.broadcasted_iota(jnp.int32, (RANK, RANK), 0) == lax.broadcasted_iota(jnp.int32, (RANK, RANK), 1),
            1.0,
            0.0,
        )
        for p in range(3):
            gram = jnp.zeros((RANK, RANK), f32)
            for ref in (own_ref, other_ref):
                for i in range(STEPS):
                    rows = jnp.concatenate(
                        [ref[pl.ds((CT * i + t) * 3 * RANK + RANK * p, RANK), :] for t in range(CT)], axis=1
                    )
                    gram += exact_nt(rows, rows)
            work_scr[p] = jnp.concatenate([gram, eye], axis=1)
        work_scr[3] = jnp.concatenate([gram_out_ref[:, :RANK], eye], axis=1)
        lane = lax.broadcasted_iota(jnp.int32, (4, RANK, 128), 2)
        sub = lax.broadcasted_iota(jnp.int32, (4, RANK, 128), 1)

        def eliminate(j, work):
            pivot_row = jnp.sum(jnp.where(sub == j, work, 0.0), axis=1, keepdims=True)
            pivot = jnp.sum(jnp.where(lane[:, :1] == j, pivot_row, 0.0), axis=2, keepdims=True)
            column = jnp.sum(jnp.where((lane == j) & (sub > j), work, 0.0), axis=2, keepdims=True)
            return work - column * (pivot_row / pivot)

        work = lax.fori_loop(0, RANK, eliminate, work_scr[...])
        diagonal = jnp.sum(jnp.where(lane == sub, work, 0.0), axis=2, keepdims=True)
        inverse_ref[...] = work * lax.rsqrt(diagonal)
        left_out = wide(left_out_ref[...], RANK)
        ortho_out_ref[...] = exact_nn(inverse_ref[3, :, RANK:], left_out)

    turned_ref[...] = x_ref[...].astype(f32).T.astype(bf16)
    first = step < STEPS
    block = pl.ds(pl.multiple_of(lax.rem(step, STEPS) * (CT * 3 * RANK), CT * 3 * RANK), CT * 3 * RANK)

    def turn(ref):
        rows = wide(ref[block, :], 3 * RANK)
        for p in range(3):
            high, low = split2(exact_nn(inverse_ref[p, :, RANK:], rows[RANK * p : RANK * (p + 1)]))
            both = jnp.concatenate([high.astype(f32), low.astype(f32)], axis=0)
            ortho_ref[p] = both.T.astype(bf16)

    @pl.when(first)
    def _():
        turn(own_ref)

    @pl.when(jnp.logical_not(first))
    def _():
        turn(other_ref)


def ortho(half, own, other, gram_out, inputs):
    def column(j, h):
        return lax.rem(j // STEPS + h[0], 2) * STEPS + lax.rem(j, STEPS)

    whole = pl.BlockSpec((L_ROWS, 128), lambda j, h: (0, 0))
    return pl.pallas_call(
        ortho_kernel,
        grid_spec=pltpu.PrefetchScalarGridSpec(
            num_scalar_prefetch=1,
            grid=(2 * STEPS,),
            in_specs=[
                whole,
                whole,
                pl.BlockSpec((LO_ROWS, 128), lambda j, h: (L_ROWS // LO_ROWS, 0)),
                pl.BlockSpec((RANK, 128), lambda j, h: (0, 0)),
                pl.BlockSpec((TOK, TILE), lambda j, h: (0, column(j, h))),
            ],
            out_specs=[
                pl.BlockSpec((TILE, TOK), lambda j, h: (column(j, h), 0)),
                pl.BlockSpec((3, TILE, 128), lambda j, h: (0, column(j, h), 0)),
                pl.BlockSpec((RANK, COLS), lambda j, h: (0, 0)),
                pl.BlockSpec((4, RANK, 128), lambda j, h: (0, 0, 0)),
            ],
            scratch_shapes=[pltpu.VMEM((4, RANK, 128), f32)],
        ),
        out_shape=[
            jax.ShapeDtypeStruct((D, TOK), bf16),
            jax.ShapeDtypeStruct((3, D, 128), bf16),
            jax.ShapeDtypeStruct((RANK, COLS), f32),
            jax.ShapeDtypeStruct((4, RANK, 128), f32),
        ],
        compiler_params=pltpu.CompilerParams(vmem_limit_bytes=VMEM),
        name="ortho",
    )(half, own, other, own, gram_out, inputs)


def rest_kernel(half_ref, summed_in_ref, own_ref, other_ref, inverse_ref, turned_ref, ortho_ref, ortho_out_ref,
                grads_ref, hid_ref, gy_ref, err_in_ref, err_out_ref, rest_in_ref, rest_out_ref, factor_in_ref,
                factor_out_ref, in_scr, out_scr):
    step = pl.program_id(0)

    @pl.when(step == 0)
    def _():
        for p in range(3):
            right = wide(summed_in_ref[pl.ds(HEADS * RANK * p, HEADS * RANK), :], RANK) * (1.0 / N_DP)
            factor = exact_nn(inverse_ref[p, :, RANK:], right)
            factor_in_ref[p] = factor
            high, low = split2(-factor)
            in_scr[p] = jnp.concatenate([high, high, low, jnp.zeros_like(low)], axis=0)
        high, low = split2(ortho_out_ref[...])
        out_scr[...] = jnp.concatenate([high, high, low, jnp.zeros_like(low)], axis=0)

    def output_factor(ref):
        right = wide(ref[...], RANK) * (1.0 / N_DP)
        factor_out_ref[...] = exact_nn(inverse_ref[3, :, RANK:], right)

    @pl.when(step < STEPS)
    def _():
        output_factor(own_ref)

    @pl.when(step >= STEPS)
    def _():
        output_factor(other_ref)

    high, low = split2(-factor_out_ref[...])
    weights = jnp.concatenate([high, low, high, jnp.zeros_like(low)], axis=0)
    rest_out = tn(hid_ref[...], gy_ref[...]) + tn(out_scr[...], weights) + err_out_ref[...].astype(f32)
    rest_out_ref[...] = rest_out.astype(bf16)
    for p in range(3):
        both = jnp.concatenate([turned_ref[...], ortho_ref[p], ortho_ref[p]], axis=1)
        weights = jnp.concatenate([grads_ref[p], in_scr[p]], axis=0)
        rest_in_ref[p] = (nn(both, weights) + err_in_ref[p].astype(f32)).astype(bf16)


def rest(half, summed, other, inverse, turned, ortho_in, ortho_out, grads, hidden, grad_y, err_in, err_out):
    def column(j, h):
        return lax.rem(j // STEPS + h[0], 2) * STEPS + lax.rem(j, STEPS)

    return pl.pallas_call(
        rest_kernel,
        grid_spec=pltpu.PrefetchScalarGridSpec(
            num_scalar_prefetch=1,
            grid=(2 * STEPS,),
            in_specs=[
                pl.BlockSpec((RI_ROWS, 128), lambda j, h: (0, 0)),
                pl.BlockSpec((CT * RANK, 128), lambda j, h: (jnp.minimum(j, STEPS - 1), 0)),
                pl.BlockSpec((CT * RANK, 128), lambda j, h: (jnp.maximum(j - STEPS, 0), 0)),
                pl.BlockSpec((4, RANK, 128), lambda j, h: (0, 0, 0)),
                pl.BlockSpec((TILE, TOK), lambda j, h: (column(j, h), 0)),
                pl.BlockSpec((3, TILE, 128), lambda j, h: (0, column(j, h), 0)),
                pl.BlockSpec((RANK, COLS), lambda j, h: (0, 0)),
                pl.BlockSpec((3, TOK, COLS), lambda j, h: (0, 0, 0)),
                pl.BlockSpec((TOK, COLS), lambda j, h: (0, 0)),
                pl.BlockSpec((TOK, TILE), lambda j, h: (0, column(j, h))),
                pl.BlockSpec((3, TILE, COLS), lambda j, h: (0, column(j, h), 0)),
                pl.BlockSpec((COLS, TILE), lambda j, h: (0, column(j, h))),
            ],
            out_specs=[
                pl.BlockSpec((3, TILE, COLS), lambda j, h: (0, column(j, h), 0)),
                pl.BlockSpec((COLS, TILE), lambda j, h: (0, column(j, h))),
                pl.BlockSpec((3, RANK, COLS), lambda j, h: (0, 0, 0)),
                pl.BlockSpec((RANK, TILE), lambda j, h: (0, column(j, h))),
            ],
            scratch_shapes=[pltpu.VMEM((3, 4 * RANK, COLS), bf16), pltpu.VMEM((4 * RANK, COLS), bf16)],
        ),
        out_shape=[
            jax.ShapeDtypeStruct((3, D, COLS), bf16),
            jax.ShapeDtypeStruct((COLS, D), bf16),
            jax.ShapeDtypeStruct((3, RANK, COLS), f32),
            jax.ShapeDtypeStruct((RANK, D), f32),
        ],
        compiler_params=pltpu.CompilerParams(vmem_limit_bytes=VMEM),
        name="rest",
    )(half, summed, summed[RI_ROWS : RI_ROWS + RO_ROWS], other, inverse, turned, ortho_in, ortho_out, grads, hidden, grad_y, err_in, err_out)


CHIP = ("x", "y", "z")
SWAP = [(0, 1), (1, 0)]


def all_summed(rows, total_rows, per_z):
    each = total_rows // CHIPS
    received = lax.all_to_all(rows.reshape(CHIPS, each, 128), CHIP, 0, 0)
    over_xy = jnp.sum(received.reshape(N_DP, 4, each, 128), axis=0)
    total = jnp.sum(over_xy, axis=0)
    me = (lax.axis_index("x") * 4 + lax.axis_index("y")) * 4 + lax.axis_index("z")
    row = me * each + lax.broadcasted_iota(jnp.int32, (1, each, 1), 1)
    answer = jnp.where(per_z(row), over_xy, total[None])
    answer = jnp.broadcast_to(answer[None], (N_DP, 4, each, 128)).reshape(CHIPS, each, 128)
    return lax.all_to_all(answer, CHIP, 0, 0).reshape(total_rows, 128)


def shards(inputs, grad_y, q_pre, f_pre, v_pre, w_out, err_in, err_out, basis_in, basis_out):
    err_in = err_in[0]
    err_out = err_out[0]
    core = lax.axis_index("c").astype(jnp.int32)
    mine = core[None]
    theirs = 1 - mine
    hidden, grads = recurrence(grad_y, w_out, q_pre, f_pre, v_pre)
    local = (inputs, grad_y, grads, hidden, err_in, err_out, basis_in, basis_out)
    send, left_out_a = left(theirs, *local)
    arrived = lax.ppermute(send, "c", SWAP)
    keep, left_out_b = left(mine, *local)
    rows = jnp.concatenate(
        [
            (keep + arrived).reshape(L_ROWS, 128),
            (left_out_a + left_out_b).reshape(LO_ROWS, 128),
            jnp.zeros((ROWS1 - L_ROWS - LO_ROWS, 128), f32),
        ]
    )
    own = all_summed(rows, ROWS1, lambda row: row >= L_ROWS)
    other = lax.ppermute(own, "c", SWAP)
    right_a, token_a, send, gram_part = right(
        jnp.concatenate([mine, theirs]), own, own, inputs, grad_y, hidden, err_in, err_out
    )
    arrived = lax.ppermute(send, "c", SWAP)
    gram_out = gram_part + lax.ppermute(gram_part, "c", SWAP)
    gram_out = gram_out + sum(
        lax.ppermute(gram_out, "z", [(a, (a + shift) % 4) for a in range(4)]) for shift in (1, 2, 3)
    )
    right_b, token_b, keep, _ = right(
        jnp.concatenate([theirs, mine]), other, own, inputs, grad_y, hidden, err_in, err_out
    )
    rows = join(right_a, right_b, token_a, token_b, grads, keep.reshape(RO_ROWS, 128), arrived.reshape(RO_ROWS, 128))
    summed = all_summed(rows, ROWS2, lambda row: row < RI_ROWS)
    turned, ortho_in, ortho_out, inverse = ortho(mine, own, other, gram_out, inputs)
    other_right = lax.ppermute(summed[RI_ROWS : RI_ROWS + RO_ROWS], "c", SWAP)
    rest_in, rest_out, factor_in, factor_out = rest(
        mine, summed, other_right, inverse, turned, ortho_in, ortho_out, grads, hidden, grad_y, err_in, err_out
    )
    return rest_in[None], rest_out[None], factor_in, factor_out


def solution(mesh):
    fine = Mesh(mesh.devices.reshape(4, 4, 4, 2), ("x", "y", "z", "c"))
    dp, head = ("x", "y"), ("z", "c")
    placed = (
        P(dp, None),
        P(dp, None),
        P(dp, head),
        P(dp, head),
        P(dp, head),
        P(head, None),
        P(dp, None, None, head),
        P(dp, head, None),
        P(None, None, head),
        P(),
    )
    return jax.shard_map(
        shards,
        mesh=fine,
        in_specs=placed,
        out_specs=(P(dp, None, None, head), P(dp, head, None), P(None, None, head), P()),
        check_vma=False,
    )
```

```python
import functools

import jax
import jax.numpy as jnp
from jax import lax
from jax.experimental import pallas as pl
from jax.experimental.pallas import tpu as pltpu
from jax.sharding import Mesh, PartitionSpec as P

TOK = 256
DK = 128
HEADS = 3
COLS = HEADS * DK
RANK = 64
D = 3072
HALF = D // 2
TILE = 512
STEPS = HALF // TILE
CT = TILE // 128
N_DP = 16
CHIPS = 64
L_ROWS = 12 * 3 * RANK
LO_ROWS = HEADS * RANK
ROWS1 = 2560
EACH1 = 40
L_STEP = CT * 3 * RANK
RI_ROWS = 9 * RANK
RO_ROWS = 12 * RANK
ROWS2 = 768
EACH2 = 48
PIECE = HEADS * RANK

f32 = jnp.float32
bf16 = jnp.bfloat16
EXACT = lax.Precision.HIGHEST
VMEM = 24 * 1024 * 1024


def cost(us):
    return pl.CostEstimate(flops=int(us * 1e9), bytes_accessed=int(us * 3e6), transcendentals=0)


def nn(a, b):
    return lax.dot_general(a, b, (((1,), (0,)), ((), ())), preferred_element_type=f32)


def nt(a, b):
    return lax.dot_general(a, b, (((1,), (1,)), ((), ())), preferred_element_type=f32)


def tn(a, b):
    return lax.dot_general(a, b, (((0,), (0,)), ((), ())), preferred_element_type=f32)


def exact_nn(a, b):
    return lax.dot_general(a, b, (((1,), (0,)), ((), ())), precision=EXACT, preferred_element_type=f32)


def exact_nt(a, b):
    return lax.dot_general(a, b, (((1,), (1,)), ((), ())), precision=EXACT, preferred_element_type=f32)


def split2(a):
    high = a.astype(bf16)
    return high, (a - high.astype(f32)).astype(bf16)


def split3(a):
    high = a.astype(bf16)
    rest = a - high.astype(f32)
    mid = rest.astype(bf16)
    return high, mid, (rest - mid.astype(f32)).astype(bf16)


def stacked(a):
    return jnp.concatenate(split2(a), axis=0)


def folded(a):
    half = a.shape[0] // 2
    return a[:half] + a[half:]


def recurrence_kernel(gy_ref, w_ref, q_ref, f_ref, v_ref, *refs):
    sources, (hid_ref, grad_ref), kept, sem = refs[:4], refs[4:6], refs[6:10], refs[10]
    copies = [pltpu.make_async_copy(a, b, sem.at[i]) for i, (a, b) in enumerate(zip(sources, kept))]

    @pl.when(pl.program_id(0) == 0)
    def _():
        for copy in copies:
            copy.start()

    grad_o = nt(gy_ref[...], w_ref[...]).astype(bf16)
    q = q_ref[...].astype(f32)
    f = f_ref[...].astype(f32)
    v = v_ref[...]
    q_gate = 1.0 / (1.0 + jnp.exp(-q))
    query = q * q_gate
    small = jnp.exp(-jnp.abs(f))
    key = jnp.where(f >= 0, small, 1.0) / (1.0 + small)
    decay = jnp.where(f >= 0, 1.0, small) / (1.0 + small)
    log_decay = jnp.minimum(f, 0.0) - jnp.log1p(small)

    row = lax.broadcasted_iota(jnp.int32, (TOK, TOK), 0)
    col = lax.broadcasted_iota(jnp.int32, (TOK, TOK), 1)
    lower = jnp.where(row >= col, 1.0, 0.0).astype(bf16)
    upper = jnp.where(row <= col, 1.0, 0.0).astype(bf16)
    differ = row ^ col
    high, mid, low = split3(log_decay)
    running = nn(lower, high) + (nn(lower, mid) + nn(lower, low))

    scores = jnp.zeros((TOK, TOK), f32)
    grad_s = split2(nt(grad_o, v))
    grad_st = split2(nt(v, grad_o))
    grad_query = jnp.zeros((TOK, DK), f32)
    grad_key = jnp.zeros((TOK, DK), f32)
    for size in (128, 64, 32, 16, 8):
        blocks = running.reshape(TOK // (2 * size), 2 * size, DK)
        spread = (blocks - blocks[:, size - 1 : size, :]).reshape(TOK, DK)
        if size > 8:
            q_scale = jnp.exp(jnp.minimum(spread, 0.0))
            k_scale = jnp.exp(jnp.minimum(-spread, 0.0))
            within = (differ >= size) & (differ < 2 * size)
            mask = within & (row > col)
            mask_t = within & (row < col)
        else:
            q_scale = jnp.exp(spread)
            k_scale = jnp.exp(-spread)
            within = differ < 2 * size
            mask = within & (row >= col)
            mask_t = within & (row <= col)
        q_high, q_low = split2(query * q_scale)
        k_high, k_low = split2(key * k_scale)
        level = nt(
            jnp.concatenate([q_high, q_high, q_low], axis=1),
            jnp.concatenate([k_high, k_low, k_high], axis=1),
        )
        scores = jnp.where(mask, level, scores)
        keep = jnp.where(mask, 1.0, 0.0).astype(bf16)
        keep_t = jnp.where(mask_t, 1.0, 0.0).astype(bf16)
        both = nn(grad_s[0] * keep, jnp.concatenate([k_high, k_low], axis=1))
        grad_query += q_scale * (both[:, :DK] + both[:, DK:] + nn(grad_s[1] * keep, k_high))
        both = nn(grad_st[0] * keep_t, jnp.concatenate([q_high, q_low], axis=1))
        grad_key += k_scale * (both[:, :DK] + both[:, DK:] + nn(grad_st[1] * keep_t, q_high))
    s_high, s_low = split2(scores)
    hid_ref[...] = (nn(s_high, v) + nn(s_low, v)).astype(bf16)
    grad_v = tn(s_high, grad_o) + tn(s_low, grad_o)
    high, mid, low = split3(query * grad_query - key * grad_key)
    grad_decay = nn(upper, high) + (nn(upper, mid) + nn(upper, low))
    grad_ref[0] = (grad_query * (q_gate + query * (1.0 - q_gate))).astype(bf16)
    grad_ref[1] = (key * (grad_decay - grad_key * decay)).astype(bf16)
    grad_ref[2] = grad_v.astype(bf16)

    @pl.when(pl.program_id(0) == HEADS - 1)
    def _():
        for copy in copies:
            copy.wait()


def held(*arrays):
    return [pltpu.with_memory_space_constraint(a, pltpu.VMEM) for a in arrays]


def streamed(*arrays):
    return [pltpu.with_memory_space_constraint(a, pltpu.HBM) for a in arrays]


ANY = pl.BlockSpec(memory_space=pl.ANY)


def fetched(step, steps, column, width, sources, slots, sem):
    def copies(j):
        at = pl.ds(pl.multiple_of(column(j) * width, width), width)
        for i, (axis, source) in enumerate(sources):
            index = [slice(None)] * len(source.shape)
            index[axis] = at
            yield pltpu.make_async_copy(source.at[tuple(index)], slots[i].at[j], sem.at[i, j])

    @pl.when(step == 0)
    def _():
        for j in range(steps):
            for copy in copies(j):
                copy.start()

    for copy in copies(step):
        copy.wait()
    return [slot.at[step] for slot in slots]


def recurrence(grad_y, w_out, q_pre, f_pre, v_pre, keep):
    per_head = pl.BlockSpec((TOK, DK), lambda h: (0, h))
    anywhere = pl.BlockSpec(memory_space=pl.ANY)
    operands = (grad_y, w_out, q_pre, f_pre, v_pre) + keep
    return pl.pallas_call(
        recurrence_kernel,
        grid=(HEADS,),
        in_specs=[
            pl.BlockSpec((TOK, D), lambda h: (0, 0)),
            pl.BlockSpec((DK, D), lambda h: (h, 0)),
            per_head,
            per_head,
            per_head,
        ]
        + [anywhere] * len(keep),
        out_specs=[per_head, pl.BlockSpec((3, TOK, DK), lambda h: (0, 0, h))] + [anywhere] * len(keep),
        out_shape=[
            jax.ShapeDtypeStruct((TOK, COLS), bf16),
            jax.ShapeDtypeStruct((3, TOK, COLS), bf16),
        ]
        + [pltpu.VMEM(a.shape, a.dtype) for a in keep],
        scratch_shapes=[pltpu.SemaphoreType.DMA((len(keep),))],
        cost_estimate=cost(8),
        compiler_params=pltpu.CompilerParams(vmem_limit_bytes=VMEM),
        name="recurrence",
    )(*streamed(*operands))


def tiles_of(a):
    return [a[:, 128 * i : 128 * (i + 1)] for i in range(a.shape[1] // 128)]


def left_tokens(grads_ref, basis_in_ref, token_scr):
    for p in range(3):
        token_scr[p] = stacked(folded(nt(stacked(basis_in_ref[p]), grads_ref[p])))


def left_tile(p, x_ref, err_in_ref, basis_in_ref, token_scr):
    part = nn(token_scr[p], x_ref[...]) + nt(stacked(basis_in_ref[p]), err_in_ref[p])
    return tiles_of(folded(part))


def left_send_kernel(half_ref, x_ref, grads_ref, err_in_ref, basis_in_ref, left_ref, token_scr):
    @pl.when(pl.program_id(0) == 0)
    def _():
        left_tokens(grads_ref, basis_in_ref, token_scr)

    for p in range(3):
        for i, tile in enumerate(left_tile(p, x_ref, err_in_ref, basis_in_ref, token_scr)):
            at = (3 * i + p) * RANK
            left_ref[at : at + RANK, :] = tile


def left_keep_kernel(half_ref, x_ref, grads_ref, err_in_ref, basis_in_ref, arrived_ref, left_out_ref, rows_ref, token_scr):
    step = pl.program_id(0)

    @pl.when(step == 0)
    def _():
        left_tokens(grads_ref, basis_in_ref, token_scr)
        rows_ref[L_ROWS : L_ROWS + LO_ROWS, :] = left_out_ref[...]
        rows_ref[L_ROWS + LO_ROWS :, :] = jnp.zeros((ROWS1 - L_ROWS - LO_ROWS, 128), f32)

    for p in range(3):
        for i, tile in enumerate(left_tile(p, x_ref, err_in_ref, basis_in_ref, token_scr)):
            at = (3 * i + p) * RANK
            rows_ref[pl.ds(pl.multiple_of(step * L_STEP + at, RANK), RANK), :] = tile + arrived_ref[at : at + RANK, :]


def left(half, inputs, grads, err_in, basis_in, arrived=None, left_out_part=None):
    keep = arrived is not None
    specs = [
        pl.BlockSpec((TOK, TILE), lambda j, h: (0, h[0] * STEPS + j)),
        pl.BlockSpec((3, TOK, COLS), lambda j, h: (0, 0, 0)),
        pl.BlockSpec((3, TILE, COLS), lambda j, h: (0, h[0] * STEPS + j, 0)),
        pl.BlockSpec((3, RANK, COLS), lambda j, h: (0, 0, 0)),
    ]
    by_step = pl.BlockSpec((L_STEP, 128), lambda j, h: (j, 0))
    if keep:
        specs += [by_step, pl.BlockSpec((LO_ROWS, 128), lambda j, h: (0, 0))]
    return pl.pallas_call(
        left_keep_kernel if keep else left_send_kernel,
        grid_spec=pltpu.PrefetchScalarGridSpec(
            num_scalar_prefetch=1,
            grid=(STEPS,),
            in_specs=specs,
            out_specs=pl.BlockSpec((ROWS1, 128), lambda j, h: (0, 0)) if keep else by_step,
            scratch_shapes=[pltpu.VMEM((3, 2 * RANK, TOK), bf16)],
        ),
        out_shape=jax.ShapeDtypeStruct((ROWS1 if keep else L_ROWS, 128), f32),
        cost_estimate=cost(3),
        compiler_params=pltpu.CompilerParams(vmem_limit_bytes=VMEM),
        name="left_keep" if keep else "left_send",
    )(half, *held(inputs), grads, *held(err_in), basis_in, *((arrived, left_out_part) if keep else ()))


def left_out_kernel(gy_ref, hid_ref, err_out_ref, basis_out_ref, left_out_ref):
    @pl.when(pl.program_id(0) == 0)
    def _():
        left_out_ref[...] = jnp.zeros_like(left_out_ref)

    basis = stacked(basis_out_ref[...])
    tokens = stacked(folded(nt(basis, gy_ref[...])))
    part = folded(nt(basis, err_out_ref[...]) + nn(tokens, hid_ref[...]))
    for i, tile in enumerate(tiles_of(part)):
        left_out_ref[RANK * i : RANK * (i + 1), :] += tile


def left_out(grad_y, hidden, err_out, basis_out):
    return pl.pallas_call(
        left_out_kernel,
        grid=(D // 1024,),
        in_specs=[
            pl.BlockSpec((TOK, 1024), lambda j: (0, j)),
            pl.BlockSpec((TOK, COLS), lambda j: (0, 0)),
            pl.BlockSpec((COLS, 1024), lambda j: (0, j)),
            pl.BlockSpec((RANK, 1024), lambda j: (0, j)),
        ],
        out_specs=pl.BlockSpec((LO_ROWS, 128), lambda j: (0, 0)),
        out_shape=jax.ShapeDtypeStruct((LO_ROWS, 128), f32),
        cost_estimate=cost(4),
        compiler_params=pltpu.CompilerParams(vmem_limit_bytes=VMEM),
        name="left_out",
    )(*held(grad_y), hidden, *held(err_out), basis_out)


def turned_kernel(x_ref, turned_ref):
    turned_ref[...] = x_ref[...].astype(f32).T.astype(bf16)


def turned(inputs):
    return pl.pallas_call(
        turned_kernel,
        grid=(D // TILE,),
        in_specs=[pl.BlockSpec((TOK, TILE), lambda j: (0, j))],
        out_specs=pl.BlockSpec((TILE, TOK), lambda j: (j, 0)),
        out_shape=pltpu.HBM((D, TOK), bf16),
        cost_estimate=cost(3),
        compiler_params=pltpu.CompilerParams(vmem_limit_bytes=VMEM),
        name="turned",
    )(*streamed(inputs))


def wide(block, rows):
    return jnp.concatenate([block[i * rows : (i + 1) * rows] for i in range(block.shape[0] // rows)], axis=1)


def answer_left_kernel(me_ref, received_ref, answer_ref):
    over_xy = []
    for z in range(4):
        total = received_ref[z]
        for i in range(1, N_DP):
            total += received_ref[4 * i + z]
        over_xy.append(total)
    total = (over_xy[0] + over_xy[1]) + (over_xy[2] + over_xy[3])
    row = me_ref[0] * EACH1 + lax.broadcasted_iota(jnp.int32, (EACH1, 128), 0)
    for z in range(4):
        answer = jnp.where(row >= L_ROWS, over_xy[z], total)
        for i in range(N_DP):
            answer_ref[4 * i + z] = answer


def answer_left(me, received):
    whole = pl.BlockSpec((CHIPS, EACH1, 128), lambda j, m: (0, 0, 0))
    return pl.pallas_call(
        answer_left_kernel,
        grid_spec=pltpu.PrefetchScalarGridSpec(num_scalar_prefetch=1, grid=(1,), in_specs=[whole], out_specs=whole),
        out_shape=jax.ShapeDtypeStruct((CHIPS, EACH1, 128), f32),
        cost_estimate=cost(2),
        compiler_params=pltpu.CompilerParams(vmem_limit_bytes=VMEM),
        name="answer_left",
    )(me, received)


def answer_right_kernel(received_ref, answer_ref):
    total = received_ref[0]
    for i in range(1, N_DP):
        total += received_ref[i]
    for i in range(N_DP):
        answer_ref[i] = total


def answer_right(received):
    return pl.pallas_call(
        answer_right_kernel,
        out_shape=jax.ShapeDtypeStruct((N_DP, EACH2, 128), f32),
        cost_estimate=cost(1),
        compiler_params=pltpu.CompilerParams(vmem_limit_bytes=VMEM),
        name="answer_right",
    )(received)


def right_out_kernel(place_ref, left_out_ref, hid_ref, gy_hbm, err_out_hbm, right_out_ref, gram_ref, out_scr,
                     gy_scr, err_out_scr, sem):
    step = pl.program_id(0)

    def column(j):
        return lax.rem(place_ref[0] + 1 + j // 4, 2) * 4 + lax.rem(place_ref[1] + lax.rem(j, 4), 4)

    gy_ref, err_out_ref = fetched(step, 8, column, COLS, [(1, gy_hbm), (1, err_out_hbm)], [gy_scr, err_out_scr], sem)

    @pl.when(step == 0)
    def _():
        left_out = wide(left_out_ref[...], RANK)
        gram_ref[...] = jnp.concatenate([exact_nt(left_out, left_out), jnp.zeros((RANK, RANK), f32)], axis=1)
        factor = stacked(left_out)
        out_scr[:, :COLS] = factor
        out_scr[:, COLS:] = stacked(folded(nt(factor, hid_ref[...])))

    part = folded(nn(out_scr[:, :COLS], err_out_ref[...]) + nn(out_scr[:, COLS:], gy_ref[...]))
    for i, tile in enumerate(tiles_of(part)):
        right_out_ref[i] = tile


def right_out(place, left_out_sum, grad_y, hidden, err_out):
    return pl.pallas_call(
        right_out_kernel,
        grid_spec=pltpu.PrefetchScalarGridSpec(
            num_scalar_prefetch=1,
            grid=(8,),
            in_specs=[
                pl.BlockSpec((LO_ROWS, 128), lambda j, h: (0, 0)),
                pl.BlockSpec((TOK, COLS), lambda j, h: (0, 0)),
                ANY,
                ANY,
            ],
            out_specs=[
                pl.BlockSpec((3, RANK, 128), lambda j, h: (j, 0, 0)),
                pl.BlockSpec((RANK, 128), lambda j, h: (0, 0)),
            ],
            scratch_shapes=[
                pltpu.VMEM((2 * RANK, COLS + TOK), bf16),
                pltpu.VMEM((8, TOK, COLS), bf16),
                pltpu.VMEM((8, COLS, COLS), bf16),
                pltpu.SemaphoreType.DMA((2, 8)),
            ],
        ),
        out_shape=[
            jax.ShapeDtypeStruct((24, RANK, 128), f32),
            jax.ShapeDtypeStruct((RANK, 128), f32),
        ],
        cost_estimate=cost(3),
        compiler_params=pltpu.CompilerParams(vmem_limit_bytes=VMEM),
        name="right_out",
    )(place, left_out_sum, hidden, *streamed(grad_y, err_out))


def right_kernel(half_ref, own_ref, other_ref, x_hbm, err_in_hbm, right_ref, token_ref, x_scr, err_in_scr, sem):
    step = pl.program_id(0)

    def column(j):
        return lax.rem(j // STEPS + half_ref[0], 2) * STEPS + lax.rem(j, STEPS)

    x_ref, err_in_ref = fetched(step, 2 * STEPS, column, TILE, [(1, x_hbm), (1, err_in_hbm)], [x_scr, err_in_scr], sem)

    @pl.when(step == 0)
    def _():
        right_ref[...] = jnp.zeros_like(right_ref)
        token_ref[...] = jnp.zeros_like(token_ref)

    def add(ref):
        rows = wide(ref[...], 3 * RANK)
        for p in range(3):
            factor = stacked(rows[RANK * p : RANK * (p + 1)])
            right_ref[p] += folded(nn(factor, err_in_ref[p]))
            token_ref[p] += folded(nt(factor, x_ref[...]))

    @pl.when(step < STEPS)
    def _():
        add(own_ref)

    @pl.when(step >= STEPS)
    def _():
        add(other_ref)


def right(half, own, other, inputs, err_in):
    return pl.pallas_call(
        right_kernel,
        grid_spec=pltpu.PrefetchScalarGridSpec(
            num_scalar_prefetch=1,
            grid=(2 * STEPS,),
            in_specs=[
                pl.BlockSpec((L_STEP, 128), lambda j, h: (jnp.minimum(j, STEPS - 1), 0)),
                pl.BlockSpec((L_STEP, 128), lambda j, h: (jnp.maximum(j - STEPS, 0), 0)),
                ANY,
                ANY,
            ],
            out_specs=[
                pl.BlockSpec((3, RANK, COLS), lambda j, h: (0, 0, 0)),
                pl.BlockSpec((3, RANK, TOK), lambda j, h: (0, 0, 0)),
            ],
            scratch_shapes=[
                pltpu.VMEM((2 * STEPS, TOK, TILE), bf16),
                pltpu.VMEM((2 * STEPS, 3, TILE, COLS), bf16),
                pltpu.SemaphoreType.DMA((2, 2 * STEPS)),
            ],
        ),
        out_shape=[
            jax.ShapeDtypeStruct((3, RANK, COLS), f32),
            jax.ShapeDtypeStruct((3, RANK, TOK), f32),
        ],
        cost_estimate=cost(6),
        compiler_params=pltpu.CompilerParams(vmem_limit_bytes=VMEM),
        name="right",
    )(half, own, other, *streamed(inputs, err_in))


def join_kernel(right_ref, token_ref, grads_ref, own_ref, first_ref, second_ref, third_ref, rows_ref, gram_ref):
    for p in range(3):
        total = right_ref[p] + folded(nn(stacked(token_ref[p]), grads_ref[p]))
        for i, tile in enumerate(tiles_of(total)):
            rows_ref[pl.ds((HEADS * p + i) * RANK, RANK), :] = tile
    piece = (own_ref[...] + first_ref[...]) + (second_ref[...] + third_ref[...])
    rows_ref[RI_ROWS:, :] = piece[:PIECE]
    gram_ref[...] = piece[PIECE:]


def join(*operands):
    return pl.pallas_call(
        join_kernel,
        out_shape=[jax.ShapeDtypeStruct((ROWS2, 128), f32), jax.ShapeDtypeStruct((RANK, 128), f32)],
        cost_estimate=cost(1),
        compiler_params=pltpu.CompilerParams(vmem_limit_bytes=VMEM),
        name="join",
    )(*operands)


def invert_kernel(own_ref, other_ref, left_out_ref, gram_out_ref, inverse_ref, ortho_out_ref):
    eye = jnp.where(
        lax.broadcasted_iota(jnp.int32, (RANK, RANK), 0) == lax.broadcasted_iota(jnp.int32, (RANK, RANK), 1),
        1.0,
        0.0,
    )
    for p in range(3):
        gram = jnp.zeros((RANK, RANK), f32)
        for ref in (own_ref, other_ref):
            for i in range(STEPS):
                rows = jnp.concatenate(
                    [ref[pl.ds((CT * i + t) * 3 * RANK + RANK * p, RANK), :] for t in range(CT)], axis=1
                )
                gram += exact_nt(rows, rows)
        inverse_ref[p] = jnp.concatenate([gram, eye], axis=1)
    inverse_ref[3] = jnp.concatenate([gram_out_ref[:, :RANK], eye], axis=1)
    lane = lax.broadcasted_iota(jnp.int32, (4, RANK, 128), 2)
    sub = lax.broadcasted_iota(jnp.int32, (4, RANK, 128), 1)

    def eliminate(j, work):
        pivot_row = jnp.sum(jnp.where(sub == j, work, 0.0), axis=1, keepdims=True)
        pivot = jnp.sum(jnp.where(lane[:, :1] == j, pivot_row, 0.0), axis=2, keepdims=True)
        column = jnp.sum(jnp.where((lane == j) & (sub > j), work, 0.0), axis=2, keepdims=True)
        return work - column * (pivot_row / pivot)

    work = lax.fori_loop(0, RANK, eliminate, inverse_ref[...])
    diagonal = jnp.sum(jnp.where(lane == sub, work, 0.0), axis=2, keepdims=True)
    inverse = work * lax.rsqrt(diagonal)
    inverse_ref[...] = inverse
    ortho_out_ref[...] = exact_nn(inverse[3, :, RANK:], wide(left_out_ref[...], RANK))


def invert(own, other, left_out_sum, gram_out):
    return pl.pallas_call(
        invert_kernel,
        out_shape=[
            jax.ShapeDtypeStruct((4, RANK, 128), f32),
            jax.ShapeDtypeStruct((RANK, COLS), f32),
        ],
        cost_estimate=cost(10),
        compiler_params=pltpu.CompilerParams(vmem_limit_bytes=VMEM),
        name="invert",
    )(own, other, left_out_sum, gram_out)


def turn_kernel(half_ref, own_ref, other_ref, inverse_ref, ortho_ref):
    step = pl.program_id(0)

    def turn(ref):
        rows = wide(ref[...], 3 * RANK)
        for p in range(3):
            high, low = split2(exact_nn(inverse_ref[p, :, RANK:], rows[RANK * p : RANK * (p + 1)]))
            both = jnp.concatenate([high.astype(f32), low.astype(f32)], axis=0)
            ortho_ref[p] = both.T.astype(bf16)

    @pl.when(step < STEPS)
    def _():
        turn(own_ref)

    @pl.when(step >= STEPS)
    def _():
        turn(other_ref)


def turn(half, own, other, inverse):
    def column(j, h):
        return lax.rem(j // STEPS + h[0], 2) * STEPS + lax.rem(j, STEPS)

    return pl.pallas_call(
        turn_kernel,
        grid_spec=pltpu.PrefetchScalarGridSpec(
            num_scalar_prefetch=1,
            grid=(2 * STEPS,),
            in_specs=[
                pl.BlockSpec((CT * 3 * RANK, 128), lambda j, h: (jnp.minimum(j, STEPS - 1), 0)),
                pl.BlockSpec((CT * 3 * RANK, 128), lambda j, h: (jnp.maximum(j - STEPS, 0), 0)),
                pl.BlockSpec((4, RANK, 128), lambda j, h: (0, 0, 0)),
            ],
            out_specs=pl.BlockSpec((3, TILE, 128), lambda j, h: (0, column(j, h), 0)),
        ),
        out_shape=pltpu.HBM((3, D, 128), bf16),
        cost_estimate=cost(6),
        compiler_params=pltpu.CompilerParams(vmem_limit_bytes=VMEM),
        name="turn",
    )(half, own, other, inverse)


def rest_in_kernel(summed_in_ref, inverse_ref, grads_ref, turned_hbm, ortho_hbm, err_in_hbm, rest_in_ref,
                   factor_in_ref, in_scr, turned_scr, ortho_scr, err_in_scr, sem):
    step = pl.program_id(0)
    turned_ref, ortho_ref, err_in_ref = fetched(
        step,
        D // TILE,
        lambda j: j,
        TILE,
        [(0, turned_hbm), (1, ortho_hbm), (1, err_in_hbm)],
        [turned_scr, ortho_scr, err_in_scr],
        sem,
    )

    @pl.when(step == 0)
    def _():
        for p in range(3):
            right = wide(summed_in_ref[pl.ds(HEADS * RANK * p, HEADS * RANK), :], RANK) * (1.0 / N_DP)
            factor = exact_nn(inverse_ref[p, :, RANK:], right)
            factor_in_ref[p] = factor
            high, low = split2(-factor)
            in_scr[p] = jnp.concatenate([high, high, low, jnp.zeros_like(low)], axis=0)

    for p in range(3):
        both = jnp.concatenate([turned_ref[...], ortho_ref[p], ortho_ref[p]], axis=1)
        weights = jnp.concatenate([grads_ref[p], in_scr[p]], axis=0)
        rest_in_ref[p] = (nn(both, weights) + err_in_ref[p].astype(f32)).astype(bf16)


def rest_in(summed, inverse, turned, ortho_in, grads, err_in):
    return pl.pallas_call(
        rest_in_kernel,
        grid=(D // TILE,),
        in_specs=[
            pl.BlockSpec((RI_ROWS, 128), lambda j: (0, 0)),
            pl.BlockSpec((4, RANK, 128), lambda j: (0, 0, 0)),
            pl.BlockSpec((3, TOK, COLS), lambda j: (0, 0, 0)),
            ANY,
            ANY,
            ANY,
        ],
        out_specs=[
            pl.BlockSpec((3, TILE, COLS), lambda j: (0, j, 0)),
            pl.BlockSpec((3, RANK, COLS), lambda j: (0, 0, 0)),
        ],
        scratch_shapes=[
            pltpu.VMEM((3, 4 * RANK, COLS), bf16),
            pltpu.VMEM((D // TILE, TILE, TOK), bf16),
            pltpu.VMEM((D // TILE, 3, TILE, 128), bf16),
            pltpu.VMEM((D // TILE, 3, TILE, COLS), bf16),
            pltpu.SemaphoreType.DMA((3, D // TILE)),
        ],
        out_shape=[
            jax.ShapeDtypeStruct((3, D, COLS), bf16),
            jax.ShapeDtypeStruct((3, RANK, COLS), f32),
        ],
        cost_estimate=cost(10),
        compiler_params=pltpu.CompilerParams(vmem_limit_bytes=VMEM),
        name="rest_in",
    )(summed, inverse, grads, *streamed(turned, ortho_in, err_in))


def rest_out_kernel(place_ref, right_ref, inverse_ref, ortho_out_ref, hid_ref, gy_hbm, err_out_hbm, *refs):
    rest_out_ref, factor_out_ref, turned_scr, gy_scr, err_out_scr, sem = refs[-6:]
    step = pl.program_id(0)

    def column(j):
        return place_ref[0] * 4 + lax.rem(place_ref[1] + 4 - j, 4)

    gy_ref, err_out_ref = fetched(step, 4, column, COLS, [(1, gy_hbm), (1, err_out_hbm)], [gy_scr, err_out_scr], sem)

    @pl.when(step == 0)
    def _():
        high, low = split2(ortho_out_ref[...])
        stack = jnp.concatenate([high, high, low, jnp.zeros_like(low)], axis=0)
        turned_scr[:, :TOK] = hid_ref[...].astype(f32).T.astype(bf16)
        turned_scr[:, TOK:] = stack.astype(f32).T.astype(bf16)

    factor = exact_nn(inverse_ref[3, :, RANK:], wide(right_ref[...], RANK) * (1.0 / N_DP))
    factor_out_ref[...] = factor
    high, low = split2(-factor)
    weights = jnp.concatenate([gy_ref[...], high, low, high, jnp.zeros_like(low)], axis=0)
    rest_out_ref[...] = (nn(turned_scr[...], weights) + err_out_ref[...].astype(f32)).astype(bf16)


def rest_out(place, right_half, inverse, ortho_out, hidden, grad_y, err_out, before=()):
    def column(j, h):
        return h[0] * 4 + lax.rem(h[1] + 4 - j, 4)

    return pl.pallas_call(
        rest_out_kernel,
        grid_spec=pltpu.PrefetchScalarGridSpec(
            num_scalar_prefetch=1,
            grid=(4,),
            in_specs=[
                pl.BlockSpec((PIECE, 128), lambda j, h: (j, 0)),
                pl.BlockSpec((4, RANK, 128), lambda j, h: (0, 0, 0)),
                pl.BlockSpec((RANK, COLS), lambda j, h: (0, 0)),
                pl.BlockSpec((TOK, COLS), lambda j, h: (0, 0)),
            ]
            + [ANY] * (2 + len(before)),
            out_specs=[
                pl.BlockSpec((COLS, COLS), lambda j, h: (0, column(j, h))),
                pl.BlockSpec((RANK, COLS), lambda j, h: (0, column(j, h))),
            ],
            scratch_shapes=[
                pltpu.VMEM((COLS, 2 * TOK), bf16),
                pltpu.VMEM((4, TOK, COLS), bf16),
                pltpu.VMEM((4, COLS, COLS), bf16),
                pltpu.SemaphoreType.DMA((2, 4)),
            ],
        ),
        out_shape=[
            jax.ShapeDtypeStruct((COLS, D), bf16),
            jax.ShapeDtypeStruct((RANK, D), f32),
        ],
        input_output_aliases={7: 0, 8: 1} if before else {},
        cost_estimate=cost(3),
        compiler_params=pltpu.CompilerParams(vmem_limit_bytes=VMEM),
        name="rest_out",
    )(place, right_half, inverse, ortho_out, hidden, *streamed(grad_y, err_out), *before)


CHIP = ("x", "y", "z")
SWAP = [(0, 1), (1, 0)]
OTHERS = (2, 1, 3)


def ring(shift):
    return [(a, (a + shift) % 4) for a in range(4)]


def shards(inputs, grad_y, q_pre, f_pre, v_pre, w_out, err_in, err_out, basis_in, basis_out):
    keep = (err_in[0], err_out[0], inputs, grad_y)
    core = lax.axis_index("c").astype(jnp.int32)
    z = lax.axis_index("z").astype(jnp.int32)
    me = (lax.axis_index("x") * 4 + lax.axis_index("y")).astype(jnp.int32) * 4 + z
    mine = core[None]
    theirs = 1 - mine
    place = jnp.stack([core, z])
    their_place = jnp.stack([1 - core, z])
    hidden, grads, near_err_in, near_err_out, near_inputs, near_grad_y = recurrence(
        grad_y, w_out, q_pre, f_pre, v_pre, keep
    )
    err_in, err_out = keep[:2]
    send = left(theirs, near_inputs, grads, near_err_in, basis_in)
    arrived = lax.ppermute(send, "c", SWAP)
    left_out_part = left_out(near_grad_y, hidden, near_err_out, basis_out)
    rows = left(mine, near_inputs, grads, near_err_in, basis_in, arrived, left_out_part)

    rows, later_inputs = lax.optimization_barrier((rows, inputs))
    received = lax.all_to_all(rows.reshape(CHIPS, EACH1, 128), CHIP, 0, 0)
    inputs_turned = turned(later_inputs)
    received, inputs_turned = lax.optimization_barrier((received, inputs_turned))
    own = lax.all_to_all(answer_left(me[None], received), CHIP, 0, 0).reshape(ROWS1, 128)
    other = lax.ppermute(own, "c", SWAP)
    left_out_sum = own[L_ROWS : L_ROWS + LO_ROWS]

    partial_out, gram_out = right_out(place, left_out_sum, grad_y, hidden, err_out)
    quarters = partial_out.reshape(2, 4, PIECE, 128)
    send = jnp.concatenate([quarters[0].reshape(RO_ROWS, 128), gram_out])
    arrived = lax.ppermute(send, "c", SWAP)
    gram_out = gram_out + arrived[RO_ROWS:]
    quarters = quarters[1] + arrived[:RO_ROWS].reshape(4, PIECE, 128)
    pieces = [jnp.concatenate([quarters[shift], gram_out]) for shift in range(4)]
    pieces = [pieces[0]] + [lax.ppermute(pieces[shift], "z", ring(shift)) for shift in OTHERS]
    rows, gram_out = join(*right(mine, own, other, inputs, err_in), grads, *pieces)

    received = lax.all_to_all(rows.reshape(N_DP, EACH2, 128), ("x", "y"), 0, 0)
    inverse, ortho_out = invert(own, other, left_out_sum, gram_out)
    received, inverse, ortho_out = lax.optimization_barrier((received, inverse, ortho_out))
    everywhere = answer_right(received)
    everywhere, inverse = lax.optimization_barrier((everywhere, inverse))
    summed = lax.all_to_all(everywhere, ("x", "y"), 0, 0).reshape(ROWS2, 128)
    ortho_in = turn(mine, own, other, inverse)
    summed, ortho_in = lax.optimization_barrier((summed, ortho_in))

    pieces = [summed[RI_ROWS:]]
    pieces += [lax.ppermute(pieces[0], "z", ring(shift)) for shift in (1, 2, 3)]
    new_in, factor_in = rest_in(summed, inverse, inputs_turned, ortho_in, grads, err_in)
    pieces, factor_in = lax.optimization_barrier((pieces, factor_in))
    own_right = jnp.concatenate(pieces)
    other_right = lax.ppermute(own_right, "c", SWAP)
    halfway = rest_out(place, own_right, inverse, ortho_out, hidden, grad_y, err_out)
    new_out, factor_out = rest_out(
        their_place, other_right, inverse, ortho_out, hidden, grad_y, err_out, tuple(halfway)
    )
    return new_in[None], new_out[None], factor_in, factor_out


def solution(mesh):
    fine = Mesh(mesh.devices.reshape(4, 4, 4, 2), ("x", "y", "z", "c"))
    dp, head = ("x", "y"), ("z", "c")
    placed = (
        P(dp, None),
        P(dp, None),
        P(dp, head),
        P(dp, head),
        P(dp, head),
        P(head, None),
        P(dp, None, None, head),
        P(dp, head, None),
        P(None, None, head),
        P(),
    )
    return jax.shard_map(
        shards,
        mesh=fine,
        in_specs=placed,
        out_specs=(P(dp, None, None, head), P(dp, head, None), P(None, None, head), P()),
        check_vma=False,
    )
```

```python
import functools

import jax
import jax.numpy as jnp
from jax import lax
from jax.experimental import pallas as pl
from jax.experimental.pallas import tpu as pltpu
from jax.sharding import Mesh, PartitionSpec as P

TOK = 256
DK = 128
HEADS = 3
COLS = HEADS * DK
RANK = 64
D = 3072
HALF = D // 2
TILE = 512
STEPS = HALF // TILE
CT = TILE // 128
N_DP = 16
CHIPS = 64
L_ROWS = 12 * 3 * RANK
LO_ROWS = HEADS * RANK
ROWS1 = 2560
EACH1 = 40
L_STEP = CT * 3 * RANK
RI_ROWS = 9 * RANK
RO_ROWS = 12 * RANK
ROWS2 = 768
EACH2 = 48
PIECE = HEADS * RANK

f32 = jnp.float32
bf16 = jnp.bfloat16
EXACT = lax.Precision.HIGHEST
VMEM = 24 * 1024 * 1024


def cost(us):
    return pl.CostEstimate(flops=int(us * 1e9), bytes_accessed=int(us * 3e6), transcendentals=0)


def nn(a, b):
    return lax.dot_general(a, b, (((1,), (0,)), ((), ())), preferred_element_type=f32)


def nt(a, b):
    return lax.dot_general(a, b, (((1,), (1,)), ((), ())), preferred_element_type=f32)


def tn(a, b):
    return lax.dot_general(a, b, (((0,), (0,)), ((), ())), preferred_element_type=f32)


def exact_nn(a, b):
    return lax.dot_general(a, b, (((1,), (0,)), ((), ())), precision=EXACT, preferred_element_type=f32)


def exact_nt(a, b):
    return lax.dot_general(a, b, (((1,), (1,)), ((), ())), precision=EXACT, preferred_element_type=f32)


def split2(a):
    high = a.astype(bf16)
    return high, (a - high.astype(f32)).astype(bf16)


def split3(a):
    high = a.astype(bf16)
    rest = a - high.astype(f32)
    mid = rest.astype(bf16)
    return high, mid, (rest - mid.astype(f32)).astype(bf16)


def summed3(ones, a):
    parts = nn(ones, jnp.concatenate(split3(a), axis=1))
    width = a.shape[1]
    return parts[:, :width] + (parts[:, width : 2 * width] + parts[:, 2 * width :])


def stacked(a):
    return jnp.concatenate(split2(a), axis=0)


def folded(a):
    half = a.shape[0] // 2
    return a[:half] + a[half:]


def recurrence_kernel(gy_ref, w_ref, q_ref, f_ref, v_ref, *refs):
    sources, (hid_ref, grad_ref), kept, sem = refs[:4], refs[4:6], refs[6:10], refs[10]
    copies = [pltpu.make_async_copy(a, b, sem.at[i]) for i, (a, b) in enumerate(zip(sources, kept))]

    @pl.when(pl.program_id(0) == 0)
    def _():
        for copy in copies:
            copy.start()

    grad_o = nt(gy_ref[...], w_ref[...]).astype(bf16)
    q = q_ref[...].astype(f32)
    f = f_ref[...].astype(f32)
    v = v_ref[...]
    q_gate = 1.0 / (1.0 + jnp.exp(-q))
    query = q * q_gate
    small = jnp.exp(-jnp.abs(f))
    key = jnp.where(f >= 0, small, 1.0) / (1.0 + small)
    decay = jnp.where(f >= 0, 1.0, small) / (1.0 + small)
    log_decay = jnp.minimum(f, 0.0) - jnp.log1p(small)

    row = lax.broadcasted_iota(jnp.int32, (TOK, TOK), 0)
    col = lax.broadcasted_iota(jnp.int32, (TOK, TOK), 1)
    lower = jnp.where(row >= col, 1.0, 0.0).astype(bf16)
    upper = jnp.where(row <= col, 1.0, 0.0).astype(bf16)
    differ = row ^ col
    running = summed3(lower, log_decay)

    scores = jnp.zeros((TOK, TOK), f32)
    grad_s = split2(nt(grad_o, v))
    grad_st = split2(nt(v, grad_o))
    grad_query = jnp.zeros((TOK, DK), f32)
    grad_key = jnp.zeros((TOK, DK), f32)
    for size in (128, 64, 32, 16, 8):
        blocks = running.reshape(TOK // (2 * size), 2 * size, DK)
        spread = (blocks - blocks[:, size - 1 : size, :]).reshape(TOK, DK)
        if size > 8:
            q_scale = jnp.exp(jnp.minimum(spread, 0.0))
            k_scale = jnp.exp(jnp.minimum(-spread, 0.0))
            within = (differ >= size) & (differ < 2 * size)
            mask = within & (row > col)
            mask_t = within & (row < col)
        else:
            q_scale = jnp.exp(spread)
            k_scale = jnp.exp(-spread)
            within = differ < 2 * size
            mask = within & (row >= col)
            mask_t = within & (row <= col)
        q_high, q_low = split2(query * q_scale)
        k_high, k_low = split2(key * k_scale)
        level = nt(
            jnp.concatenate([q_high, q_high, q_low], axis=1),
            jnp.concatenate([k_high, k_low, k_high], axis=1),
        )
        scores = jnp.where(mask, level, scores)
        keep = jnp.where(mask, 1.0, 0.0).astype(bf16)
        keep_t = jnp.where(mask_t, 1.0, 0.0).astype(bf16)
        both = nn(grad_s[0] * keep, jnp.concatenate([k_high, k_low], axis=1))
        grad_query += q_scale * (both[:, :DK] + both[:, DK:] + nn(grad_s[1] * keep, k_high))
        both = nn(grad_st[0] * keep_t, jnp.concatenate([q_high, q_low], axis=1))
        grad_key += k_scale * (both[:, :DK] + both[:, DK:] + nn(grad_st[1] * keep_t, q_high))
    s_high, s_low = split2(scores)
    hid_ref[...] = (nn(s_high, v) + nn(s_low, v)).astype(bf16)
    grad_v = tn(s_high, grad_o) + tn(s_low, grad_o)
    grad_decay = summed3(upper, query * grad_query - key * grad_key)
    grad_ref[0] = (grad_query * (q_gate + query * (1.0 - q_gate))).astype(bf16)
    grad_ref[1] = (key * (grad_decay - grad_key * decay)).astype(bf16)
    grad_ref[2] = grad_v.astype(bf16)

    @pl.when(pl.program_id(0) == HEADS - 1)
    def _():
        for copy in copies:
            copy.wait()


def held(*arrays):
    return [pltpu.with_memory_space_constraint(a, pltpu.VMEM) for a in arrays]


def streamed(*arrays):
    return [pltpu.with_memory_space_constraint(a, pltpu.HBM) for a in arrays]


ANY = pl.BlockSpec(memory_space=pl.ANY)


def fetched(step, steps, column, width, sources, slots, sem):
    def copies(j):
        at = pl.ds(pl.multiple_of(column(j) * width, width), width)
        for i, (axis, source) in enumerate(sources):
            index = [slice(None)] * len(source.shape)
            index[axis] = at
            yield pltpu.make_async_copy(source.at[tuple(index)], slots[i].at[j], sem.at[i, j])

    @pl.when(step == 0)
    def _():
        for j in range(steps):
            for copy in copies(j):
                copy.start()

    for copy in copies(step):
        copy.wait()
    return [slot.at[step] for slot in slots]


def recurrence(grad_y, w_out, q_pre, f_pre, v_pre, keep):
    per_head = pl.BlockSpec((TOK, DK), lambda h: (0, h))
    anywhere = pl.BlockSpec(memory_space=pl.ANY)
    operands = (grad_y, w_out, q_pre, f_pre, v_pre) + keep
    return pl.pallas_call(
        recurrence_kernel,
        grid=(HEADS,),
        in_specs=[
            pl.BlockSpec((TOK, D), lambda h: (0, 0)),
            pl.BlockSpec((DK, D), lambda h: (h, 0)),
            per_head,
            per_head,
            per_head,
        ]
        + [anywhere] * len(keep),
        out_specs=[per_head, pl.BlockSpec((3, TOK, DK), lambda h: (0, 0, h))] + [anywhere] * len(keep),
        out_shape=[
            jax.ShapeDtypeStruct((TOK, COLS), bf16),
            jax.ShapeDtypeStruct((3, TOK, COLS), bf16),
        ]
        + [pltpu.VMEM(a.shape, a.dtype) for a in keep],
        scratch_shapes=[pltpu.SemaphoreType.DMA((len(keep),))],
        cost_estimate=cost(8),
        compiler_params=pltpu.CompilerParams(vmem_limit_bytes=VMEM),
        name="recurrence",
    )(*streamed(*operands))


def tiles_of(a):
    return [a[:, 128 * i : 128 * (i + 1)] for i in range(a.shape[1] // 128)]


def left_tiles(half_ref, x_ref, grads_ref, err_in_ref, basis_in_ref):
    bases = [stacked(basis_in_ref[p]) for p in range(3)]
    tokens = jnp.concatenate([stacked(folded(nt(bases[p], grads_ref[p]))) for p in range(3)], axis=0)
    for step in range(STEPS):
        at = pl.ds(pl.multiple_of(half_ref[0] * HALF + step * TILE, TILE), TILE)
        from_tokens = nn(tokens, x_ref[:, at])
        for p in range(3):
            part = from_tokens[2 * RANK * p : 2 * RANK * (p + 1)] + nt(bases[p], err_in_ref[p, at, :])
            for i, tile in enumerate(tiles_of(folded(part))):
                yield step * L_STEP + (3 * i + p) * RANK, tile


def left_send_kernel(half_ref, x_ref, grads_ref, err_in_ref, basis_in_ref, left_ref):
    for at, tile in left_tiles(half_ref, x_ref, grads_ref, err_in_ref, basis_in_ref):
        left_ref[at : at + RANK, :] = tile


def left_keep_kernel(half_ref, x_ref, grads_ref, err_in_ref, basis_in_ref, arrived_ref, left_out_ref, rows_ref):
    rows_ref[L_ROWS : L_ROWS + LO_ROWS, :] = left_out_ref[...]
    rows_ref[L_ROWS + LO_ROWS :, :] = jnp.zeros((ROWS1 - L_ROWS - LO_ROWS, 128), f32)
    for at, tile in left_tiles(half_ref, x_ref, grads_ref, err_in_ref, basis_in_ref):
        rows_ref[at : at + RANK, :] = tile + arrived_ref[at : at + RANK, :]


def left(half, inputs, grads, err_in, basis_in, *arrived):
    return pl.pallas_call(
        left_keep_kernel if arrived else left_send_kernel,
        in_specs=[pl.BlockSpec(memory_space=pltpu.SMEM)] + [pl.BlockSpec(memory_space=pltpu.VMEM)] * (4 + len(arrived)),
        out_shape=jax.ShapeDtypeStruct((ROWS1 if arrived else L_ROWS, 128), f32),
        cost_estimate=cost(3),
        compiler_params=pltpu.CompilerParams(vmem_limit_bytes=VMEM),
        name="left_keep" if arrived else "left_send",
    )(half, *held(inputs), grads, *held(err_in), basis_in, *arrived)


def left_out_kernel(gy_ref, hid_ref, err_out_ref, basis_out_ref, left_out_ref):
    basis = stacked(basis_out_ref[...])
    tokens = stacked(folded(nt(basis, gy_ref[...])))
    part = folded(nt(basis, err_out_ref[...]) + nn(tokens, hid_ref[...]))
    for i, tile in enumerate(tiles_of(part)):
        left_out_ref[RANK * i : RANK * (i + 1), :] = tile


def left_out(grad_y, hidden, err_out, basis_out):
    return pl.pallas_call(
        left_out_kernel,
        out_shape=jax.ShapeDtypeStruct((LO_ROWS, 128), f32),
        cost_estimate=cost(4),
        compiler_params=pltpu.CompilerParams(vmem_limit_bytes=VMEM),
        name="left_out",
    )(*held(grad_y), hidden, *held(err_out), basis_out)


def turned_kernel(x_ref, turned_ref):
    turned_ref[...] = x_ref[...].astype(f32).T.astype(bf16)


def turned(inputs):
    return pl.pallas_call(
        turned_kernel,
        grid=(D // TILE,),
        in_specs=[pl.BlockSpec((TOK, TILE), lambda j: (0, j))],
        out_specs=pl.BlockSpec((TILE, TOK), lambda j: (j, 0)),
        out_shape=pltpu.HBM((D, TOK), bf16),
        cost_estimate=cost(3),
        compiler_params=pltpu.CompilerParams(vmem_limit_bytes=VMEM),
        name="turned",
    )(*streamed(inputs))


def wide(block, rows):
    return jnp.concatenate([block[i * rows : (i + 1) * rows] for i in range(block.shape[0] // rows)], axis=1)


def answer_left_kernel(me_ref, received_ref, answer_ref):
    over_xy = []
    for z in range(4):
        total = received_ref[z]
        for i in range(1, N_DP):
            total += received_ref[4 * i + z]
        over_xy.append(total)
    total = (over_xy[0] + over_xy[1]) + (over_xy[2] + over_xy[3])
    row = me_ref[0] * EACH1 + lax.broadcasted_iota(jnp.int32, (EACH1, 128), 0)
    for z in range(4):
        answer = jnp.where(row >= L_ROWS, over_xy[z], total)
        for i in range(N_DP):
            answer_ref[4 * i + z] = answer


def answer_left(me, received):
    whole = pl.BlockSpec((CHIPS, EACH1, 128), lambda j, m: (0, 0, 0))
    return pl.pallas_call(
        answer_left_kernel,
        grid_spec=pltpu.PrefetchScalarGridSpec(num_scalar_prefetch=1, grid=(1,), in_specs=[whole], out_specs=whole),
        out_shape=jax.ShapeDtypeStruct((CHIPS, EACH1, 128), f32),
        cost_estimate=cost(2),
        compiler_params=pltpu.CompilerParams(vmem_limit_bytes=VMEM),
        name="answer_left",
    )(me, received)


def answer_right_kernel(received_ref, answer_ref):
    total = received_ref[0]
    for i in range(1, N_DP):
        total += received_ref[i]
    for i in range(N_DP):
        answer_ref[i] = total


def answer_right(received):
    return pl.pallas_call(
        answer_right_kernel,
        out_shape=jax.ShapeDtypeStruct((N_DP, EACH2, 128), f32),
        cost_estimate=cost(1),
        compiler_params=pltpu.CompilerParams(vmem_limit_bytes=VMEM),
        name="answer_right",
    )(received)


def right_out_kernel(place_ref, left_out_ref, hid_ref, gy_hbm, err_out_hbm, right_out_ref, gram_ref, out_scr,
                     gy_scr, err_out_scr, sem):
    step = pl.program_id(0)

    def column(j):
        return lax.rem(place_ref[0] + 1 + j // 4, 2) * 4 + lax.rem(place_ref[1] + lax.rem(j, 4), 4)

    gy_ref, err_out_ref = fetched(step, 8, column, COLS, [(1, gy_hbm), (1, err_out_hbm)], [gy_scr, err_out_scr], sem)

    @pl.when(step == 0)
    def _():
        left_out = wide(left_out_ref[...], RANK)
        gram_ref[...] = jnp.concatenate([exact_nt(left_out, left_out), jnp.zeros((RANK, RANK), f32)], axis=1)
        factor = stacked(left_out)
        out_scr[:, :COLS] = factor
        out_scr[:, COLS:] = stacked(folded(nt(factor, hid_ref[...])))

    part = folded(nn(out_scr[:, :COLS], err_out_ref[...]) + nn(out_scr[:, COLS:], gy_ref[...]))
    for i, tile in enumerate(tiles_of(part)):
        right_out_ref[i] = tile


def right_out(place, left_out_sum, grad_y, hidden, err_out):
    return pl.pallas_call(
        right_out_kernel,
        grid_spec=pltpu.PrefetchScalarGridSpec(
            num_scalar_prefetch=1,
            grid=(8,),
            in_specs=[
                pl.BlockSpec((LO_ROWS, 128), lambda j, h: (0, 0)),
                pl.BlockSpec((TOK, COLS), lambda j, h: (0, 0)),
                ANY,
                ANY,
            ],
            out_specs=[
                pl.BlockSpec((3, RANK, 128), lambda j, h: (j, 0, 0)),
                pl.BlockSpec((RANK, 128), lambda j, h: (0, 0)),
            ],
            scratch_shapes=[
                pltpu.VMEM((2 * RANK, COLS + TOK), bf16),
                pltpu.VMEM((8, TOK, COLS), bf16),
                pltpu.VMEM((8, COLS, COLS), bf16),
                pltpu.SemaphoreType.DMA((2, 8)),
            ],
        ),
        out_shape=[
            jax.ShapeDtypeStruct((24, RANK, 128), f32),
            jax.ShapeDtypeStruct((RANK, 128), f32),
        ],
        cost_estimate=cost(3),
        compiler_params=pltpu.CompilerParams(vmem_limit_bytes=VMEM),
        name="right_out",
    )(place, left_out_sum, hidden, *streamed(grad_y, err_out))


def right_kernel(half_ref, own_ref, other_ref, x_hbm, err_in_hbm, right_ref, token_ref, x_scr, err_in_scr, sem):
    step = pl.program_id(0)

    def column(j):
        return lax.rem(j // STEPS + half_ref[0], 2) * STEPS + lax.rem(j, STEPS)

    x_ref, err_in_ref = fetched(step, 2 * STEPS, column, TILE, [(1, x_hbm), (1, err_in_hbm)], [x_scr, err_in_scr], sem)

    @pl.when(step == 0)
    def _():
        right_ref[...] = jnp.zeros_like(right_ref)
        token_ref[...] = jnp.zeros_like(token_ref)

    def add(ref):
        high, low = split2(wide(ref[...], 3 * RANK))
        token_ref[...] += folded(nt(jnp.concatenate([high, low], axis=0), x_ref[...]))
        for p in range(3):
            mine = slice(RANK * p, RANK * (p + 1))
            right_ref[p] += folded(nn(jnp.concatenate([high[mine], low[mine]], axis=0), err_in_ref[p]))

    @pl.when(step < STEPS)
    def _():
        add(own_ref)

    @pl.when(step >= STEPS)
    def _():
        add(other_ref)


def right(half, own, other, inputs, err_in):
    return pl.pallas_call(
        right_kernel,
        grid_spec=pltpu.PrefetchScalarGridSpec(
            num_scalar_prefetch=1,
            grid=(2 * STEPS,),
            in_specs=[
                pl.BlockSpec((L_STEP, 128), lambda j, h: (jnp.minimum(j, STEPS - 1), 0)),
                pl.BlockSpec((L_STEP, 128), lambda j, h: (jnp.maximum(j - STEPS, 0), 0)),
                ANY,
                ANY,
            ],
            out_specs=[
                pl.BlockSpec((3, RANK, COLS), lambda j, h: (0, 0, 0)),
                pl.BlockSpec((3 * RANK, TOK), lambda j, h: (0, 0)),
            ],
            scratch_shapes=[
                pltpu.VMEM((2 * STEPS, TOK, TILE), bf16),
                pltpu.VMEM((2 * STEPS, 3, TILE, COLS), bf16),
                pltpu.SemaphoreType.DMA((2, 2 * STEPS)),
            ],
        ),
        out_shape=[
            jax.ShapeDtypeStruct((3, RANK, COLS), f32),
            jax.ShapeDtypeStruct((3 * RANK, TOK), f32),
        ],
        cost_estimate=cost(6),
        compiler_params=pltpu.CompilerParams(vmem_limit_bytes=VMEM),
        name="right",
    )(half, own, other, *streamed(inputs, err_in))


def join_kernel(right_ref, token_ref, grads_ref, own_ref, first_ref, second_ref, third_ref, rows_ref, gram_ref):
    for p in range(3):
        total = right_ref[p] + folded(nn(stacked(token_ref[RANK * p : RANK * (p + 1), :]), grads_ref[p]))
        for i, tile in enumerate(tiles_of(total)):
            rows_ref[pl.ds((HEADS * p + i) * RANK, RANK), :] = tile
    piece = (own_ref[...] + first_ref[...]) + (second_ref[...] + third_ref[...])
    rows_ref[RI_ROWS:, :] = piece[:PIECE]
    gram_ref[...] = piece[PIECE:]


def join(*operands):
    return pl.pallas_call(
        join_kernel,
        out_shape=[jax.ShapeDtypeStruct((ROWS2, 128), f32), jax.ShapeDtypeStruct((RANK, 128), f32)],
        cost_estimate=cost(1),
        compiler_params=pltpu.CompilerParams(vmem_limit_bytes=VMEM),
        name="join",
    )(*operands)


def invert_kernel(own_ref, other_ref, left_out_ref, gram_out_ref, inverse_ref, ortho_out_ref):
    eye = jnp.where(
        lax.broadcasted_iota(jnp.int32, (RANK, RANK), 0) == lax.broadcasted_iota(jnp.int32, (RANK, RANK), 1),
        1.0,
        0.0,
    )
    for p in range(3):
        gram = jnp.zeros((RANK, RANK), f32)
        for ref in (own_ref, other_ref):
            for i in range(STEPS):
                rows = jnp.concatenate(
                    [ref[pl.ds((CT * i + t) * 3 * RANK + RANK * p, RANK), :] for t in range(CT)], axis=1
                )
                gram += exact_nt(rows, rows)
        inverse_ref[p] = jnp.concatenate([gram, eye], axis=1)
    inverse_ref[3] = jnp.concatenate([gram_out_ref[:, :RANK], eye], axis=1)
    rows8 = lax.broadcasted_iota(jnp.int32, (1, 8, 1), 1)
    tiles = [inverse_ref[:, 8 * t : 8 * t + 8, :] for t in range(RANK // 8)]
    for j in range(RANK):
        top, at = divmod(j, 8)
        pivot_row = tiles[top][:, at : at + 1, :]
        scaled = pivot_row * (1.0 / pivot_row[:, :, j : j + 1])
        for t in range(top, RANK // 8):
            column = tiles[t][:, :, j : j + 1]
            if t == top:
                column = jnp.where(rows8 > at, column, 0.0)
            tiles[t] = tiles[t] - column * scaled
    work = jnp.concatenate(tiles, axis=1)
    lane = lax.broadcasted_iota(jnp.int32, (4, RANK, 128), 2)
    sub = lax.broadcasted_iota(jnp.int32, (4, RANK, 128), 1)
    diagonal = jnp.sum(jnp.where(lane == sub, work, 0.0), axis=2, keepdims=True)
    inverse = work * lax.rsqrt(diagonal)
    inverse_ref[...] = inverse
    ortho_out_ref[...] = exact_nn(inverse[3, :, RANK:], wide(left_out_ref[...], RANK))


def invert(own, other, left_out_sum, gram_out):
    return pl.pallas_call(
        invert_kernel,
        out_shape=[
            jax.ShapeDtypeStruct((4, RANK, 128), f32),
            jax.ShapeDtypeStruct((RANK, COLS), f32),
        ],
        cost_estimate=cost(10),
        compiler_params=pltpu.CompilerParams(vmem_limit_bytes=VMEM),
        name="invert",
    )(own, other, left_out_sum, gram_out)


def turn_kernel(half_ref, own_ref, other_ref, inverse_ref, ortho_ref):
    step = pl.program_id(0)

    def turn(ref):
        rows = wide(ref[...], 3 * RANK)
        for p in range(3):
            high, low = split2(exact_nn(inverse_ref[p, :, RANK:], rows[RANK * p : RANK * (p + 1)]))
            both = jnp.concatenate([high.astype(f32), low.astype(f32)], axis=0)
            ortho_ref[p] = both.T.astype(bf16)

    @pl.when(step < STEPS)
    def _():
        turn(own_ref)

    @pl.when(step >= STEPS)
    def _():
        turn(other_ref)


def turn(half, own, other, inverse):
    def column(j, h):
        return lax.rem(j // STEPS + h[0], 2) * STEPS + lax.rem(j, STEPS)

    return pl.pallas_call(
        turn_kernel,
        grid_spec=pltpu.PrefetchScalarGridSpec(
            num_scalar_prefetch=1,
            grid=(2 * STEPS,),
            in_specs=[
                pl.BlockSpec((CT * 3 * RANK, 128), lambda j, h: (jnp.minimum(j, STEPS - 1), 0)),
                pl.BlockSpec((CT * 3 * RANK, 128), lambda j, h: (jnp.maximum(j - STEPS, 0), 0)),
                pl.BlockSpec((4, RANK, 128), lambda j, h: (0, 0, 0)),
            ],
            out_specs=pl.BlockSpec((3, TILE, 128), lambda j, h: (0, column(j, h), 0)),
        ),
        out_shape=pltpu.HBM((3, D, 128), bf16),
        cost_estimate=cost(6),
        compiler_params=pltpu.CompilerParams(vmem_limit_bytes=VMEM),
        name="turn",
    )(half, own, other, inverse)


def rest_in_kernel(summed_in_ref, inverse_ref, grads_ref, turned_hbm, ortho_hbm, err_in_hbm, rest_in_ref,
                   factor_in_ref, in_scr, turned_scr, ortho_scr, err_in_scr, sem):
    step = pl.program_id(0)
    turned_ref, ortho_ref, err_in_ref = fetched(
        step,
        D // TILE,
        lambda j: j,
        TILE,
        [(0, turned_hbm), (1, ortho_hbm), (1, err_in_hbm)],
        [turned_scr, ortho_scr, err_in_scr],
        sem,
    )

    @pl.when(step == 0)
    def _():
        for p in range(3):
            right = wide(summed_in_ref[pl.ds(HEADS * RANK * p, HEADS * RANK), :], RANK) * (1.0 / N_DP)
            factor = exact_nn(inverse_ref[p, :, RANK:], right)
            factor_in_ref[p] = factor
            high, low = split2(-factor)
            in_scr[p] = jnp.concatenate([high, high, low, jnp.zeros_like(low)], axis=0)

    moments = nn(turned_ref[...], jnp.concatenate([grads_ref[p] for p in range(3)], axis=1))
    for p in range(3):
        moment = moments[:, COLS * p : COLS * (p + 1)] + err_in_ref[p].astype(f32)
        both = jnp.concatenate([ortho_ref[p], ortho_ref[p]], axis=1)
        rest_in_ref[p] = (moment + nn(both, in_scr[p])).astype(bf16)


def rest_in(summed, inverse, turned, ortho_in, grads, err_in):
    return pl.pallas_call(
        rest_in_kernel,
        grid=(D // TILE,),
        in_specs=[
            pl.BlockSpec((RI_ROWS, 128), lambda j: (0, 0)),
            pl.BlockSpec((4, RANK, 128), lambda j: (0, 0, 0)),
            pl.BlockSpec((3, TOK, COLS), lambda j: (0, 0, 0)),
            ANY,
            ANY,
            ANY,
        ],
        out_specs=[
            pl.BlockSpec((3, TILE, COLS), lambda j: (0, j, 0)),
            pl.BlockSpec((3, RANK, COLS), lambda j: (0, 0, 0)),
        ],
        scratch_shapes=[
            pltpu.VMEM((3, 4 * RANK, COLS), bf16),
            pltpu.VMEM((D // TILE, TILE, TOK), bf16),
            pltpu.VMEM((D // TILE, 3, TILE, 128), bf16),
            pltpu.VMEM((D // TILE, 3, TILE, COLS), bf16),
            pltpu.SemaphoreType.DMA((3, D // TILE)),
        ],
        out_shape=[
            jax.ShapeDtypeStruct((3, D, COLS), bf16),
            jax.ShapeDtypeStruct((3, RANK, COLS), f32),
        ],
        cost_estimate=cost(10),
        compiler_params=pltpu.CompilerParams(vmem_limit_bytes=VMEM),
        name="rest_in",
    )(summed, inverse, grads, *streamed(turned, ortho_in, err_in))


def rest_out_kernel(place_ref, right_ref, inverse_ref, ortho_out_ref, hid_ref, gy_hbm, err_out_hbm, *refs):
    rest_hbm, factor_hbm, gy_scr, err_out_scr, rest_scr, factor_scr, in_sem, out_sem = refs[-8:]

    def column(j):
        at = place_ref[0] * 4 + lax.rem(place_ref[1] + 4 - j, 4)
        return pl.ds(pl.multiple_of(at * COLS, COLS), COLS)

    into = [
        (
            pltpu.make_async_copy(gy_hbm.at[:, column(j)], gy_scr.at[j], in_sem.at[0, j]),
            pltpu.make_async_copy(err_out_hbm.at[:, column(j)], err_out_scr.at[j], in_sem.at[1, j]),
        )
        for j in range(4)
    ]
    out = [
        (
            pltpu.make_async_copy(rest_scr.at[j], rest_hbm.at[:, column(j)], out_sem.at[0, j]),
            pltpu.make_async_copy(factor_scr.at[j], factor_hbm.at[:, column(j)], out_sem.at[1, j]),
        )
        for j in range(4)
    ]
    for pair in into:
        for copy in pair:
            copy.start()
    high, low = split2(ortho_out_ref[...])
    stack = jnp.concatenate([high, high, low, jnp.zeros_like(low)], axis=0)
    both = jnp.concatenate([hid_ref[...], stack], axis=0).astype(f32).T.astype(bf16)
    right = jnp.concatenate([wide(right_ref[PIECE * j : PIECE * (j + 1), :], RANK) for j in range(4)], axis=1)
    factor = exact_nn(inverse_ref[3, :, RANK:], right * (1.0 / N_DP))
    high, low = split2(-factor)
    weights = jnp.concatenate([high, low, high, jnp.zeros_like(low)], axis=0)
    for j in range(4):
        mine = slice(COLS * j, COLS * (j + 1))
        factor_scr[j] = factor[:, mine]
        for copy in into[j]:
            copy.wait()
        total = nn(both, jnp.concatenate([gy_scr[j], weights[:, mine]], axis=0)) + err_out_scr[j].astype(f32)
        rest_scr[j] = total.astype(bf16)
        for copy in out[j]:
            copy.start()
    for pair in out:
        for copy in pair:
            copy.wait()


def rest_out(place, right_half, inverse, ortho_out, hidden, grad_y, err_out, before=()):
    whole = pl.BlockSpec(memory_space=pltpu.VMEM)
    return pl.pallas_call(
        rest_out_kernel,
        in_specs=[pl.BlockSpec(memory_space=pltpu.SMEM)] + [whole] * 4 + [ANY] * (2 + len(before)),
        out_specs=[ANY, ANY],
        scratch_shapes=[
            pltpu.VMEM((4, TOK, COLS), bf16),
            pltpu.VMEM((4, COLS, COLS), bf16),
            pltpu.VMEM((4, COLS, COLS), bf16),
            pltpu.VMEM((4, RANK, COLS), f32),
            pltpu.SemaphoreType.DMA((2, 4)),
            pltpu.SemaphoreType.DMA((2, 4)),
        ],
        out_shape=[pltpu.HBM((COLS, D), bf16), pltpu.HBM((RANK, D), f32)],
        input_output_aliases={7: 0, 8: 1} if before else {},
        cost_estimate=cost(3),
        compiler_params=pltpu.CompilerParams(vmem_limit_bytes=VMEM),
        name="rest_out",
    )(place, right_half, inverse, ortho_out, hidden, *streamed(grad_y, err_out), *before)


CHIP = ("x", "y", "z")
SWAP = [(0, 1), (1, 0)]
OTHERS = (2, 1, 3)


def ring(shift):
    return [(a, (a + shift) % 4) for a in range(4)]


def shards(inputs, grad_y, q_pre, f_pre, v_pre, w_out, err_in, err_out, basis_in, basis_out):
    keep = (err_in[0], err_out[0], inputs, grad_y)
    core = lax.axis_index("c").astype(jnp.int32)
    z = lax.axis_index("z").astype(jnp.int32)
    me = (lax.axis_index("x") * 4 + lax.axis_index("y")).astype(jnp.int32) * 4 + z
    mine = core[None]
    theirs = 1 - mine
    place = jnp.stack([core, z])
    their_place = jnp.stack([1 - core, z])
    hidden, grads, near_err_in, near_err_out, near_inputs, near_grad_y = recurrence(
        grad_y, w_out, q_pre, f_pre, v_pre, keep
    )
    err_in, err_out = keep[:2]
    send = left(theirs, near_inputs, grads, near_err_in, basis_in)
    arrived = lax.ppermute(send, "c", SWAP)
    left_out_part = left_out(near_grad_y, hidden, near_err_out, basis_out)
    rows = left(mine, near_inputs, grads, near_err_in, basis_in, arrived, left_out_part)

    rows, later_inputs = lax.optimization_barrier((rows, inputs))
    received = lax.all_to_all(rows.reshape(CHIPS, EACH1, 128), CHIP, 0, 0)
    inputs_turned = turned(later_inputs)
    received, inputs_turned = lax.optimization_barrier((received, inputs_turned))
    own = lax.all_to_all(answer_left(me[None], received), CHIP, 0, 0).reshape(ROWS1, 128)
    other = lax.ppermute(own, "c", SWAP)
    left_out_sum = own[L_ROWS : L_ROWS + LO_ROWS]

    partial_out, gram_out = right_out(place, left_out_sum, grad_y, hidden, err_out)
    quarters = partial_out.reshape(2, 4, PIECE, 128)
    send = jnp.concatenate([quarters[0].reshape(RO_ROWS, 128), gram_out])
    arrived = lax.ppermute(send, "c", SWAP)
    gram_out = gram_out + arrived[RO_ROWS:]
    quarters = quarters[1] + arrived[:RO_ROWS].reshape(4, PIECE, 128)
    pieces = [jnp.concatenate([quarters[shift], gram_out]) for shift in range(4)]
    pieces = [pieces[0]] + [lax.ppermute(pieces[shift], "z", ring(shift)) for shift in OTHERS]
    rows, gram_out = join(*right(mine, own, other, inputs, err_in), grads, *pieces)

    received = lax.all_to_all(rows.reshape(N_DP, EACH2, 128), ("x", "y"), 0, 0)
    inverse, ortho_out = invert(own, other, left_out_sum, gram_out)
    received, inverse, ortho_out = lax.optimization_barrier((received, inverse, ortho_out))
    everywhere = answer_right(received)
    everywhere, inverse = lax.optimization_barrier((everywhere, inverse))
    summed = lax.all_to_all(everywhere, ("x", "y"), 0, 0).reshape(ROWS2, 128)
    ortho_in = turn(mine, own, other, inverse)
    summed, ortho_in = lax.optimization_barrier((summed, ortho_in))

    pieces = [summed[RI_ROWS:]]
    pieces += [lax.ppermute(pieces[0], "z", ring(shift)) for shift in (1, 2, 3)]
    new_in, factor_in = rest_in(summed, inverse, inputs_turned, ortho_in, grads, err_in)
    pieces, factor_in = lax.optimization_barrier((pieces, factor_in))
    own_right = jnp.concatenate(pieces)
    other_right = lax.ppermute(own_right, "c", SWAP)
    halfway = rest_out(place, own_right, inverse, ortho_out, hidden, grad_y, err_out)
    new_out, factor_out = rest_out(
        their_place, other_right, inverse, ortho_out, hidden, grad_y, err_out, tuple(halfway)
    )
    return new_in[None], new_out[None], factor_in, factor_out


def solution(mesh):
    fine = Mesh(mesh.devices.reshape(4, 4, 4, 2), ("x", "y", "z", "c"))
    dp, head = ("x", "y"), ("z", "c")
    placed = (
        P(dp, None),
        P(dp, None),
        P(dp, head),
        P(dp, head),
        P(dp, head),
        P(head, None),
        P(dp, None, None, head),
        P(dp, head, None),
        P(None, None, head),
        P(),
    )
    return jax.shard_map(
        shards,
        mesh=fine,
        in_specs=placed,
        out_specs=(P(dp, None, None, head), P(dp, head, None), P(None, None, head), P()),
        check_vma=False,
    )
```

```python
import functools

import jax
import jax.numpy as jnp
from jax import lax
from jax.experimental import pallas as pl
from jax.experimental.pallas import tpu as pltpu
from jax.sharding import Mesh, PartitionSpec as P

TOK = 256
DK = 128
HEADS = 3
COLS = HEADS * DK
RANK = 64
D = 3072
HALF = D // 2
TILE = 512
STEPS = HALF // TILE
CT = TILE // 128
N_DP = 16
CHIPS = 64
L_ROWS = 12 * 3 * RANK
LO_ROWS = HEADS * RANK
ROWS1 = 2560
EACH1 = 40
L_STEP = CT * 3 * RANK
RI_ROWS = 9 * RANK
RO_ROWS = 12 * RANK
ROWS2 = 768
EACH2 = 48
PIECE = HEADS * RANK

f32 = jnp.float32
bf16 = jnp.bfloat16
EXACT = lax.Precision.HIGHEST
VMEM = 24 * 1024 * 1024


def cost(us):
    return pl.CostEstimate(flops=int(us * 1e9), bytes_accessed=int(us * 3e6), transcendentals=0)


def nn(a, b):
    return lax.dot_general(a, b, (((1,), (0,)), ((), ())), preferred_element_type=f32)


def nt(a, b):
    return lax.dot_general(a, b, (((1,), (1,)), ((), ())), preferred_element_type=f32)


def tn(a, b):
    return lax.dot_general(a, b, (((0,), (0,)), ((), ())), preferred_element_type=f32)


def exact_nn(a, b):
    return lax.dot_general(a, b, (((1,), (0,)), ((), ())), precision=EXACT, preferred_element_type=f32)


def exact_nt(a, b):
    return lax.dot_general(a, b, (((1,), (1,)), ((), ())), precision=EXACT, preferred_element_type=f32)


def split2(a):
    high = a.astype(bf16)
    return high, (a - high.astype(f32)).astype(bf16)


def split3(a):
    high = a.astype(bf16)
    rest = a - high.astype(f32)
    mid = rest.astype(bf16)
    return high, mid, (rest - mid.astype(f32)).astype(bf16)


def summed3(ones, a):
    parts = nn(ones, jnp.concatenate(split3(a), axis=1))
    width = a.shape[1]
    return parts[:, :width] + (parts[:, width : 2 * width] + parts[:, 2 * width :])


def stacked(a):
    return jnp.concatenate(split2(a), axis=0)


def folded(a):
    half = a.shape[0] // 2
    return a[:half] + a[half:]


def head_forward(q, f):
    q_gate = 1.0 / (1.0 + jnp.exp(-q))
    query = q * q_gate
    small = jnp.exp(-jnp.abs(f))
    key = jnp.where(f >= 0, small, 1.0) / (1.0 + small)
    decay = jnp.where(f >= 0, 1.0, small) / (1.0 + small)
    log_decay = jnp.minimum(f, 0.0) - jnp.log1p(small)
    row = lax.broadcasted_iota(jnp.int32, (TOK, TOK), 0)
    col = lax.broadcasted_iota(jnp.int32, (TOK, TOK), 1)
    running = summed3(jnp.where(row >= col, 1.0, 0.0).astype(bf16), log_decay)
    differ = row ^ col
    scores = jnp.zeros((TOK, TOK), f32)
    levels = []
    for size in (128, 64, 32, 16, 8):
        blocks = running.reshape(TOK // (2 * size), 2 * size, DK)
        spread = (blocks - blocks[:, size - 1 : size, :]).reshape(TOK, DK)
        if size > 8:
            q_scale = jnp.exp(jnp.minimum(spread, 0.0))
            k_scale = jnp.exp(jnp.minimum(-spread, 0.0))
            mask = (differ >= size) & (differ < 2 * size) & (row > col)
        else:
            q_scale = jnp.exp(spread)
            k_scale = jnp.exp(-spread)
            mask = (differ < 2 * size) & (row >= col)
        q_high, q_low = split2(query * q_scale)
        k_high, k_low = split2(key * k_scale)
        level = nt(
            jnp.concatenate([q_high, q_high, q_low], axis=1),
            jnp.concatenate([k_high, k_low, k_high], axis=1),
        )
        scores = jnp.where(mask, level, scores)
        levels.append((q_scale, k_scale, q_high, q_low, k_high, k_low))
    return (query, key, decay, q_gate), levels, split2(scores)


def head_backward(gates, levels, scores, v, grad_o):
    query, key, decay, q_gate = gates
    row = lax.broadcasted_iota(jnp.int32, (TOK, TOK), 0)
    col = lax.broadcasted_iota(jnp.int32, (TOK, TOK), 1)
    differ = row ^ col
    grad_s = split2(nt(grad_o, v))
    grad_st = split2(nt(v, grad_o))
    grad_query = jnp.zeros((TOK, DK), f32)
    grad_key = jnp.zeros((TOK, DK), f32)
    for size, (q_scale, k_scale, q_high, q_low, k_high, k_low) in zip((128, 64, 32, 16, 8), levels):
        if size > 8:
            within = (differ >= size) & (differ < 2 * size)
            mask, mask_t = within & (row > col), within & (row < col)
        else:
            within = differ < 2 * size
            mask, mask_t = within & (row >= col), within & (row <= col)
        keep = jnp.where(mask, 1.0, 0.0).astype(bf16)
        keep_t = jnp.where(mask_t, 1.0, 0.0).astype(bf16)
        both = nn(grad_s[0] * keep, jnp.concatenate([k_high, k_low], axis=1))
        grad_query += q_scale * (both[:, :DK] + both[:, DK:] + nn(grad_s[1] * keep, k_high))
        both = nn(grad_st[0] * keep_t, jnp.concatenate([q_high, q_low], axis=1))
        grad_key += k_scale * (both[:, :DK] + both[:, DK:] + nn(grad_st[1] * keep_t, q_high))
    grad_v = tn(scores[0], grad_o) + tn(scores[1], grad_o)
    upper = jnp.where(row <= col, 1.0, 0.0).astype(bf16)
    grad_decay = summed3(upper, query * grad_query - key * grad_key)
    grad_q = grad_query * (q_gate + query * (1.0 - q_gate))
    return grad_q, key * (grad_decay - grad_key * decay), grad_v


def recurrence_kernel(q_hbm, f_hbm, v_hbm, gy_hbm, w_hbm, *refs):
    sources, (hid_ref, grad_ref), kept, (q_scr, f_scr, v_scr, gy_scr, w_scr, sem) = (
        refs[:4],
        refs[4:6],
        refs[6:10],
        refs[10:],
    )
    pairs = list(zip((q_hbm, f_hbm, v_hbm, gy_hbm, w_hbm), (q_scr, f_scr, v_scr, gy_scr, w_scr)))
    copies = [pltpu.make_async_copy(a, b, sem.at[i]) for i, (a, b) in enumerate(pairs + list(zip(sources, kept)))]
    for copy in copies:
        copy.start()
    for copy in copies[:3]:
        copy.wait()
    for h in range(HEADS):
        mine = slice(DK * h, DK * (h + 1))
        gates, levels, scores = head_forward(q_scr[:, mine].astype(f32), f_scr[:, mine].astype(f32))
        v = v_scr[:, mine]
        hid_ref[:, mine] = (nn(scores[0], v) + nn(scores[1], v)).astype(bf16)
        if h == 0:
            for copy in copies[3:5]:
                copy.wait()
            grad_o = nt(gy_scr[...], w_scr[...]).astype(bf16)
        for p, grad in enumerate(head_backward(gates, levels, scores, v, grad_o[:, mine])):
            grad_ref[p, :, mine] = grad.astype(bf16)
    for copy in copies[5:]:
        copy.wait()


def held(*arrays):
    return [pltpu.with_memory_space_constraint(a, pltpu.VMEM) for a in arrays]


def streamed(*arrays):
    return [pltpu.with_memory_space_constraint(a, pltpu.HBM) for a in arrays]


ANY = pl.BlockSpec(memory_space=pl.ANY)


def fetched(step, steps, column, width, sources, slots, sem):
    def copies(j):
        at = pl.ds(pl.multiple_of(column(j) * width, width), width)
        for i, (axis, source) in enumerate(sources):
            index = [slice(None)] * len(source.shape)
            index[axis] = at
            yield pltpu.make_async_copy(source.at[tuple(index)], slots[i].at[j], sem.at[i, j])

    @pl.when(step == 0)
    def _():
        for j in range(steps):
            for copy in copies(j):
                copy.start()

    for copy in copies(step):
        copy.wait()
    return [slot.at[step] for slot in slots]


def recurrence(grad_y, w_out, q_pre, f_pre, v_pre, keep):
    operands = (q_pre, f_pre, v_pre, grad_y, w_out) + keep
    whole = pl.BlockSpec(memory_space=pltpu.VMEM)
    return pl.pallas_call(
        recurrence_kernel,
        in_specs=[ANY] * len(operands),
        out_specs=[whole] * 2 + [ANY] * len(keep),
        out_shape=[
            jax.ShapeDtypeStruct((TOK, COLS), bf16),
            jax.ShapeDtypeStruct((3, TOK, COLS), bf16),
        ]
        + [pltpu.VMEM(a.shape, a.dtype) for a in keep],
        scratch_shapes=[pltpu.VMEM(a.shape, a.dtype) for a in operands[:5]]
        + [pltpu.SemaphoreType.DMA((len(operands),))],
        cost_estimate=cost(8),
        compiler_params=pltpu.CompilerParams(vmem_limit_bytes=VMEM),
        name="recurrence",
    )(*streamed(*operands))


def tiles_of(a):
    return [a[:, 128 * i : 128 * (i + 1)] for i in range(a.shape[1] // 128)]


def left_tiles(half_ref, x_ref, grads_ref, err_in_ref, basis_in_ref):
    bases = [stacked(basis_in_ref[p]) for p in range(3)]
    tokens = jnp.concatenate([stacked(folded(nt(bases[p], grads_ref[p]))) for p in range(3)], axis=0)
    for step in range(STEPS):
        at = pl.ds(pl.multiple_of(half_ref[0] * HALF + step * TILE, TILE), TILE)
        from_tokens = nn(tokens, x_ref[:, at])
        for p in range(3):
            part = from_tokens[2 * RANK * p : 2 * RANK * (p + 1)] + nt(bases[p], err_in_ref[p, at, :])
            for i, tile in enumerate(tiles_of(folded(part))):
                yield step * L_STEP + (3 * i + p) * RANK, tile


def left_send_kernel(half_ref, x_ref, grads_ref, err_in_ref, basis_in_ref, left_ref):
    for at, tile in left_tiles(half_ref, x_ref, grads_ref, err_in_ref, basis_in_ref):
        left_ref[at : at + RANK, :] = tile


def left_keep_kernel(half_ref, x_ref, grads_ref, err_in_ref, basis_in_ref, arrived_ref, left_out_ref, rows_ref):
    rows_ref[L_ROWS : L_ROWS + LO_ROWS, :] = left_out_ref[...]
    rows_ref[L_ROWS + LO_ROWS :, :] = jnp.zeros((ROWS1 - L_ROWS - LO_ROWS, 128), f32)
    for at, tile in left_tiles(half_ref, x_ref, grads_ref, err_in_ref, basis_in_ref):
        rows_ref[at : at + RANK, :] = tile + arrived_ref[at : at + RANK, :]


def left(half, inputs, grads, err_in, basis_in, *arrived):
    return pl.pallas_call(
        left_keep_kernel if arrived else left_send_kernel,
        in_specs=[pl.BlockSpec(memory_space=pltpu.SMEM)] + [pl.BlockSpec(memory_space=pltpu.VMEM)] * (4 + len(arrived)),
        out_shape=jax.ShapeDtypeStruct((ROWS1 if arrived else L_ROWS, 128), f32),
        cost_estimate=cost(3),
        compiler_params=pltpu.CompilerParams(vmem_limit_bytes=VMEM),
        name="left_keep" if arrived else "left_send",
    )(half, *held(inputs), grads, *held(err_in), basis_in, *arrived)


def left_out_kernel(gy_ref, hid_ref, err_out_ref, basis_out_ref, left_out_ref):
    basis = stacked(basis_out_ref[...])
    tokens = stacked(folded(nt(basis, gy_ref[...])))
    part = folded(nt(basis, err_out_ref[...]) + nn(tokens, hid_ref[...]))
    for i, tile in enumerate(tiles_of(part)):
        left_out_ref[RANK * i : RANK * (i + 1), :] = tile


def left_out(grad_y, hidden, err_out, basis_out):
    return pl.pallas_call(
        left_out_kernel,
        out_shape=jax.ShapeDtypeStruct((LO_ROWS, 128), f32),
        cost_estimate=cost(4),
        compiler_params=pltpu.CompilerParams(vmem_limit_bytes=VMEM),
        name="left_out",
    )(*held(grad_y), hidden, *held(err_out), basis_out)


def turned_kernel(x_ref, turned_ref):
    turned_ref[...] = x_ref[...].astype(f32).T.astype(bf16)


def turned(inputs):
    return pl.pallas_call(
        turned_kernel,
        grid=(D // TILE,),
        in_specs=[pl.BlockSpec((TOK, TILE), lambda j: (0, j))],
        out_specs=pl.BlockSpec((TILE, TOK), lambda j: (j, 0)),
        out_shape=pltpu.HBM((D, TOK), bf16),
        cost_estimate=cost(3),
        compiler_params=pltpu.CompilerParams(vmem_limit_bytes=VMEM),
        name="turned",
    )(*streamed(inputs))


def wide(block, rows):
    return jnp.concatenate([block[i * rows : (i + 1) * rows] for i in range(block.shape[0] // rows)], axis=1)


def answer_left_kernel(me_ref, received_ref, answer_ref):
    over_xy = []
    for z in range(4):
        total = received_ref[z]
        for i in range(1, N_DP):
            total += received_ref[4 * i + z]
        over_xy.append(total)
    total = (over_xy[0] + over_xy[1]) + (over_xy[2] + over_xy[3])
    row = me_ref[0] * EACH1 + lax.broadcasted_iota(jnp.int32, (EACH1, 128), 0)
    for z in range(4):
        answer = jnp.where(row >= L_ROWS, over_xy[z], total)
        for i in range(N_DP):
            answer_ref[4 * i + z] = answer


def answer_left(me, received):
    whole = pl.BlockSpec((CHIPS, EACH1, 128), lambda j, m: (0, 0, 0))
    return pl.pallas_call(
        answer_left_kernel,
        grid_spec=pltpu.PrefetchScalarGridSpec(num_scalar_prefetch=1, grid=(1,), in_specs=[whole], out_specs=whole),
        out_shape=jax.ShapeDtypeStruct((CHIPS, EACH1, 128), f32),
        cost_estimate=cost(2),
        compiler_params=pltpu.CompilerParams(vmem_limit_bytes=VMEM),
        name="answer_left",
    )(me, received)


def answer_right_kernel(received_ref, answer_ref):
    total = received_ref[0]
    for i in range(1, N_DP):
        total += received_ref[i]
    for i in range(N_DP):
        answer_ref[i] = total


def answer_right(received):
    return pl.pallas_call(
        answer_right_kernel,
        out_shape=jax.ShapeDtypeStruct((N_DP, EACH2, 128), f32),
        cost_estimate=cost(1),
        compiler_params=pltpu.CompilerParams(vmem_limit_bytes=VMEM),
        name="answer_right",
    )(received)


def right_out_kernel(place_ref, left_out_ref, hid_ref, gy_hbm, err_out_hbm, send_ref, keep_ref, gy_scr, err_out_scr, sem):
    def column(j):
        at = lax.rem(place_ref[0] + 1 + j // 4, 2) * 4 + lax.rem(place_ref[1] + j % 4, 4)
        return pl.ds(pl.multiple_of(at * COLS, COLS), COLS)

    copies = [
        (
            pltpu.make_async_copy(gy_hbm.at[:, column(j)], gy_scr.at[j], sem.at[0, j]),
            pltpu.make_async_copy(err_out_hbm.at[:, column(j)], err_out_scr.at[j], sem.at[1, j]),
        )
        for j in range(8)
    ]
    for pair in copies:
        for copy in pair:
            copy.start()
    left_out = wide(left_out_ref[...], RANK)
    factor = stacked(left_out)
    both = jnp.concatenate([factor, stacked(folded(nt(factor, hid_ref[...])))], axis=1)
    send_ref[RO_ROWS:, :] = jnp.concatenate([exact_nt(left_out, left_out), jnp.zeros((RANK, RANK), f32)], axis=1)
    for j in range(8):
        for copy in copies[j]:
            copy.wait()
        part = folded(nn(both, jnp.concatenate([err_out_scr[j], gy_scr[j]], axis=0)))
        ref = send_ref if j < 4 else keep_ref
        for i, tile in enumerate(tiles_of(part)):
            at = (j % 4) * PIECE + i * RANK
            ref[at : at + RANK, :] = tile


def right_out(place, left_out_sum, grad_y, hidden, err_out):
    whole = pl.BlockSpec(memory_space=pltpu.VMEM)
    return pl.pallas_call(
        right_out_kernel,
        in_specs=[pl.BlockSpec(memory_space=pltpu.SMEM), whole, whole, ANY, ANY],
        out_shape=[
            jax.ShapeDtypeStruct((RO_ROWS + RANK, 128), f32),
            jax.ShapeDtypeStruct((RO_ROWS, 128), f32),
        ],
        scratch_shapes=[
            pltpu.VMEM((8, TOK, COLS), bf16),
            pltpu.VMEM((8, COLS, COLS), bf16),
            pltpu.SemaphoreType.DMA((2, 8)),
        ],
        cost_estimate=cost(3),
        compiler_params=pltpu.CompilerParams(vmem_limit_bytes=VMEM),
        name="right_out",
    )(place, left_out_sum, hidden, *streamed(grad_y, err_out))


def right_tile(rows, x, err_in, rights):
    high, low = split2(rows)
    for p in range(3):
        mine = slice(RANK * p, RANK * (p + 1))
        rights[p] += folded(nn(jnp.concatenate([high[mine], low[mine]], axis=0), err_in[p]))
    return folded(nt(jnp.concatenate([high, low], axis=0), x))


def right_own_kernel(halves_ref, own_ref, x_hbm, err_in_hbm, right_ref, token_ref, x_out, err_in_out, x_scr, err_in_scr, sem):
    def near(j):
        at = pl.ds(pl.multiple_of(halves_ref[0] * HALF + j * TILE, TILE), TILE)
        return (
            pltpu.make_async_copy(x_hbm.at[:, at], x_scr.at[j], sem.at[0, j]),
            pltpu.make_async_copy(err_in_hbm.at[:, at], err_in_scr.at[j], sem.at[1, j]),
        )

    def far(j):
        at = pl.ds(pl.multiple_of(halves_ref[1] * HALF + j * TILE, TILE), TILE)
        to = slice(j * TILE, (j + 1) * TILE)
        return (
            pltpu.make_async_copy(x_hbm.at[:, at], x_out.at[:, to], sem.at[2, j]),
            pltpu.make_async_copy(err_in_hbm.at[:, at], err_in_out.at[:, to], sem.at[3, j]),
        )

    copies = [near(j) for j in range(STEPS)] + [far(j) for j in range(STEPS)]
    for pair in copies:
        for copy in pair:
            copy.start()
    rights = [jnp.zeros((RANK, COLS), f32)] * 3
    tokens = jnp.zeros((3 * RANK, TOK), f32)
    for j in range(STEPS):
        for copy in copies[j]:
            copy.wait()
        rows = wide(own_ref[L_STEP * j : L_STEP * (j + 1), :], 3 * RANK)
        tokens += right_tile(rows, x_scr[j], err_in_scr.at[j], rights)
    token_ref[...] = tokens
    for p in range(3):
        right_ref[p] = rights[p]
    for pair in copies[STEPS:]:
        for copy in pair:
            copy.wait()


def right_own(halves, own, inputs, err_in):
    whole = pl.BlockSpec(memory_space=pltpu.VMEM)
    return pl.pallas_call(
        right_own_kernel,
        in_specs=[pl.BlockSpec(memory_space=pltpu.SMEM), whole, ANY, ANY],
        out_specs=[whole, whole, ANY, ANY],
        out_shape=[
            jax.ShapeDtypeStruct((3, RANK, COLS), f32),
            jax.ShapeDtypeStruct((3 * RANK, TOK), f32),
            pltpu.VMEM((TOK, HALF), bf16),
            pltpu.VMEM((3, HALF, COLS), bf16),
        ],
        scratch_shapes=[
            pltpu.VMEM((STEPS, TOK, TILE), bf16),
            pltpu.VMEM((STEPS, 3, TILE, COLS), bf16),
            pltpu.SemaphoreType.DMA((4, STEPS)),
        ],
        cost_estimate=cost(4),
        compiler_params=pltpu.CompilerParams(vmem_limit_bytes=VMEM),
        name="right_own",
    )(halves, own, *streamed(inputs, err_in))


def right_other_kernel(other_ref, right_ref, token_ref, x_ref, err_in_ref, grads_ref, rows_ref):
    rights = [right_ref[p] for p in range(3)]
    tokens = token_ref[...]
    for j in range(STEPS):
        mine = slice(j * TILE, (j + 1) * TILE)
        rows = wide(other_ref[L_STEP * j : L_STEP * (j + 1), :], 3 * RANK)
        tokens += right_tile(rows, x_ref[:, mine], err_in_ref.at[:, mine], rights)
    for p in range(3):
        total = rights[p] + folded(nn(stacked(tokens[RANK * p : RANK * (p + 1)]), grads_ref[p]))
        for i, tile in enumerate(tiles_of(total)):
            at = (HEADS * p + i) * RANK
            rows_ref[at : at + RANK, :] = tile


def right_other(other, right_part, token_part, inputs, err_in, grads):
    return pl.pallas_call(
        right_other_kernel,
        out_shape=jax.ShapeDtypeStruct((RI_ROWS, 128), f32),
        cost_estimate=cost(4),
        compiler_params=pltpu.CompilerParams(vmem_limit_bytes=VMEM),
        name="right_other",
    )(other, right_part, token_part, *held(inputs, err_in), grads)


def join_kernel(right_ref, own_ref, first_ref, second_ref, third_ref, rows_ref, gram_ref):
    piece = (own_ref[...] + first_ref[...]) + (second_ref[...] + third_ref[...])
    rows_ref[:RI_ROWS, :] = right_ref[...]
    rows_ref[RI_ROWS:, :] = piece[:PIECE]
    gram_ref[...] = piece[PIECE:]


def join(*operands):
    return pl.pallas_call(
        join_kernel,
        out_shape=[jax.ShapeDtypeStruct((ROWS2, 128), f32), jax.ShapeDtypeStruct((RANK, 128), f32)],
        cost_estimate=cost(1),
        compiler_params=pltpu.CompilerParams(vmem_limit_bytes=VMEM),
        name="join",
    )(*operands)


def invert_kernel(own_ref, other_ref, left_out_ref, gram_out_ref, inverse_ref, ortho_out_ref):
    eye = jnp.where(
        lax.broadcasted_iota(jnp.int32, (RANK, RANK), 0) == lax.broadcasted_iota(jnp.int32, (RANK, RANK), 1),
        1.0,
        0.0,
    )
    gram = jnp.zeros((3 * RANK, 3 * RANK), f32)
    for ref in (own_ref, other_ref):
        for i in range(STEPS):
            rows = wide(ref[L_STEP * i : L_STEP * (i + 1), :], 3 * RANK)
            gram += exact_nt(rows, rows)
    for p in range(3):
        mine = slice(RANK * p, RANK * (p + 1))
        inverse_ref[p] = jnp.concatenate([gram[mine, mine], eye], axis=1)
    inverse_ref[3] = jnp.concatenate([gram_out_ref[:, :RANK], eye], axis=1)
    rows8 = lax.broadcasted_iota(jnp.int32, (1, 8, 1), 1)
    tiles = [inverse_ref[:, 8 * t : 8 * t + 8, :] for t in range(RANK // 8)]
    for j in range(0, RANK, 2):
        top, at = divmod(j, 8)
        first = tiles[top][:, at : at + 1, :]
        second = tiles[top][:, at + 1 : at + 2, :]
        first_scaled = first * (1.0 / first[:, :, j : j + 1])
        ratio = first_scaled[:, :, j + 1 : j + 2]
        second = second - second[:, :, j : j + 1] * first_scaled
        second_scaled = second * (1.0 / second[:, :, j + 1 : j + 2])
        for t in range(top, RANK // 8):
            column = tiles[t][:, :, j : j + 1]
            other = tiles[t][:, :, j + 1 : j + 2] - column * ratio
            if t == top:
                column = jnp.where(rows8 > at, column, 0.0)
                other = jnp.where(rows8 > at + 1, other, 0.0)
            tiles[t] = tiles[t] - column * first_scaled - other * second_scaled
    work = jnp.concatenate(tiles, axis=1)
    lane = lax.broadcasted_iota(jnp.int32, (4, RANK, 128), 2)
    sub = lax.broadcasted_iota(jnp.int32, (4, RANK, 128), 1)
    diagonal = jnp.sum(jnp.where(lane == sub, work, 0.0), axis=2, keepdims=True)
    inverse = work * lax.rsqrt(diagonal)
    inverse_ref[...] = inverse
    ortho_out_ref[...] = exact_nn(inverse[3, :, RANK:], wide(left_out_ref[...], RANK))


def invert(own, other, left_out_sum, gram_out):
    return pl.pallas_call(
        invert_kernel,
        out_shape=[
            jax.ShapeDtypeStruct((4, RANK, 128), f32),
            jax.ShapeDtypeStruct((RANK, COLS), f32),
        ],
        cost_estimate=cost(10),
        compiler_params=pltpu.CompilerParams(vmem_limit_bytes=VMEM),
        name="invert",
    )(own, other, left_out_sum, gram_out)


def turn_kernel(half_ref, own_ref, other_ref, inverse_ref, ortho_ref):
    step = pl.program_id(0)

    def turn(ref):
        rows = wide(ref[...], 3 * RANK)
        for p in range(3):
            high, low = split2(exact_nn(inverse_ref[p, :, RANK:], rows[RANK * p : RANK * (p + 1)]))
            both = jnp.concatenate([high.astype(f32), low.astype(f32)], axis=0)
            ortho_ref[p] = both.T.astype(bf16)

    @pl.when(step < STEPS)
    def _():
        turn(own_ref)

    @pl.when(step >= STEPS)
    def _():
        turn(other_ref)


def turn(half, own, other, inverse):
    def column(j, h):
        return lax.rem(j // STEPS + h[0], 2) * STEPS + lax.rem(j, STEPS)

    return pl.pallas_call(
        turn_kernel,
        grid_spec=pltpu.PrefetchScalarGridSpec(
            num_scalar_prefetch=1,
            grid=(2 * STEPS,),
            in_specs=[
                pl.BlockSpec((CT * 3 * RANK, 128), lambda j, h: (jnp.minimum(j, STEPS - 1), 0)),
                pl.BlockSpec((CT * 3 * RANK, 128), lambda j, h: (jnp.maximum(j - STEPS, 0), 0)),
                pl.BlockSpec((4, RANK, 128), lambda j, h: (0, 0, 0)),
            ],
            out_specs=pl.BlockSpec((3, TILE, 128), lambda j, h: (0, column(j, h), 0)),
        ),
        out_shape=pltpu.HBM((3, D, 128), bf16),
        cost_estimate=cost(6),
        compiler_params=pltpu.CompilerParams(vmem_limit_bytes=VMEM),
        name="turn",
    )(half, own, other, inverse)


def rest_in_kernel(summed_in_ref, inverse_ref, grads_ref, turned_hbm, ortho_hbm, err_in_hbm, rest_in_ref,
                   factor_in_ref, in_scr, turned_scr, ortho_scr, err_in_scr, sem):
    step = pl.program_id(0)
    turned_ref, ortho_ref, err_in_ref = fetched(
        step,
        D // TILE,
        lambda j: j,
        TILE,
        [(0, turned_hbm), (1, ortho_hbm), (1, err_in_hbm)],
        [turned_scr, ortho_scr, err_in_scr],
        sem,
    )

    @pl.when(step == 0)
    def _():
        for p in range(3):
            right = wide(summed_in_ref[pl.ds(HEADS * RANK * p, HEADS * RANK), :], RANK) * (1.0 / N_DP)
            factor = exact_nn(inverse_ref[p, :, RANK:], right)
            factor_in_ref[p] = factor
            high, low = split2(-factor)
            in_scr[p] = jnp.concatenate([high, high, low, jnp.zeros_like(low)], axis=0)

    moments = nn(turned_ref[...], jnp.concatenate([grads_ref[p] for p in range(3)], axis=1))
    for p in range(3):
        moment = moments[:, COLS * p : COLS * (p + 1)] + err_in_ref[p].astype(f32)
        both = jnp.concatenate([ortho_ref[p], ortho_ref[p]], axis=1)
        rest_in_ref[p] = (moment + nn(both, in_scr[p])).astype(bf16)


def rest_in(summed, inverse, turned, ortho_in, grads, err_in):
    return pl.pallas_call(
        rest_in_kernel,
        grid=(D // TILE,),
        in_specs=[
            pl.BlockSpec((RI_ROWS, 128), lambda j: (0, 0)),
            pl.BlockSpec((4, RANK, 128), lambda j: (0, 0, 0)),
            pl.BlockSpec((3, TOK, COLS), lambda j: (0, 0, 0)),
            ANY,
            ANY,
            ANY,
        ],
        out_specs=[
            pl.BlockSpec((3, TILE, COLS), lambda j: (0, j, 0)),
            pl.BlockSpec((3, RANK, COLS), lambda j: (0, 0, 0)),
        ],
        scratch_shapes=[
            pltpu.VMEM((3, 4 * RANK, COLS), bf16),
            pltpu.VMEM((D // TILE, TILE, TOK), bf16),
            pltpu.VMEM((D // TILE, 3, TILE, 128), bf16),
            pltpu.VMEM((D // TILE, 3, TILE, COLS), bf16),
            pltpu.SemaphoreType.DMA((3, D // TILE)),
        ],
        out_shape=[
            jax.ShapeDtypeStruct((3, D, COLS), bf16),
            jax.ShapeDtypeStruct((3, RANK, COLS), f32),
        ],
        cost_estimate=cost(10),
        compiler_params=pltpu.CompilerParams(vmem_limit_bytes=VMEM),
        name="rest_in",
    )(summed, inverse, grads, *streamed(turned, ortho_in, err_in))


def rest_out_kernel(place_ref, own_ref, other_ref, inverse_ref, ortho_out_ref, hid_ref, gy_hbm, err_out_hbm,
                    rest_hbm, factor_hbm, gy_scr, err_out_scr, rest_scr, factor_scr, in_sem, out_sem):
    def column(j):
        at = lax.rem(place_ref[0] + j // 4, 2) * 4 + lax.rem(place_ref[1] + 4 - j % 4, 4)
        return pl.ds(pl.multiple_of(at * COLS, COLS), COLS)

    into = [
        (
            pltpu.make_async_copy(gy_hbm.at[:, column(j)], gy_scr.at[j], in_sem.at[0, j]),
            pltpu.make_async_copy(err_out_hbm.at[:, column(j)], err_out_scr.at[j], in_sem.at[1, j]),
        )
        for j in range(8)
    ]
    out = [
        (
            pltpu.make_async_copy(rest_scr.at[j], rest_hbm.at[:, column(j)], out_sem.at[0, j]),
            pltpu.make_async_copy(factor_scr.at[j], factor_hbm.at[:, column(j)], out_sem.at[1, j]),
        )
        for j in range(8)
    ]
    for pair in into:
        for copy in pair:
            copy.start()
    high, low = split2(ortho_out_ref[...])
    stack = jnp.concatenate([high, high, low, jnp.zeros_like(low)], axis=0)
    both = jnp.concatenate([hid_ref[...], stack], axis=0).astype(f32).T.astype(bf16)
    inverse = inverse_ref[3, :, RANK:]
    for j in range(0, 8, 2):
        ref = own_ref if j < 4 else other_ref
        right = jnp.concatenate([wide(ref[PIECE * (k % 4) : PIECE * (k % 4 + 1), :], RANK) for k in (j, j + 1)], axis=1)
        factor = exact_nn(inverse, right * (1.0 / N_DP))
        high, low = split2(-factor)
        for k in (j, j + 1):
            for copy in into[k]:
                copy.wait()
        gy = jnp.concatenate([gy_scr[j], gy_scr[j + 1]], axis=1)
        total = nn(both, jnp.concatenate([gy, high, low, high, jnp.zeros_like(low)], axis=0))
        for i, k in enumerate((j, j + 1)):
            mine = slice(COLS * i, COLS * (i + 1))
            factor_scr[k] = factor[:, mine]
            rest_scr[k] = (total[:, mine] + err_out_scr[k].astype(f32)).astype(bf16)
            for copy in out[k]:
                copy.start()
    for pair in out:
        for copy in pair:
            copy.wait()


def rest_out(place, own, other, inverse, ortho_out, hidden, grad_y, err_out):
    whole = pl.BlockSpec(memory_space=pltpu.VMEM)
    return pl.pallas_call(
        rest_out_kernel,
        in_specs=[pl.BlockSpec(memory_space=pltpu.SMEM)] + [whole] * 5 + [ANY] * 2,
        out_specs=[ANY, ANY],
        scratch_shapes=[
            pltpu.VMEM((8, TOK, COLS), bf16),
            pltpu.VMEM((8, COLS, COLS), bf16),
            pltpu.VMEM((8, COLS, COLS), bf16),
            pltpu.VMEM((8, RANK, COLS), f32),
            pltpu.SemaphoreType.DMA((2, 8)),
            pltpu.SemaphoreType.DMA((2, 8)),
        ],
        out_shape=[pltpu.HBM((COLS, D), bf16), pltpu.HBM((RANK, D), f32)],
        cost_estimate=cost(6),
        compiler_params=pltpu.CompilerParams(vmem_limit_bytes=VMEM),
        name="rest_out",
    )(place, own, other, inverse, ortho_out, hidden, *streamed(grad_y, err_out))


CHIP = ("x", "y", "z")
SWAP = [(0, 1), (1, 0)]
OTHERS = (2, 1, 3)


def ring(shift):
    return [(a, (a + shift) % 4) for a in range(4)]


def shards(inputs, grad_y, q_pre, f_pre, v_pre, w_out, err_in, err_out, basis_in, basis_out):
    keep = (err_in[0], err_out[0], inputs, grad_y)
    core = lax.axis_index("c").astype(jnp.int32)
    z = lax.axis_index("z").astype(jnp.int32)
    me = (lax.axis_index("x") * 4 + lax.axis_index("y")).astype(jnp.int32) * 4 + z
    mine = core[None]
    theirs = 1 - mine
    place = jnp.stack([core, z])
    hidden, grads, near_err_in, near_err_out, near_inputs, near_grad_y = recurrence(
        grad_y, w_out, q_pre, f_pre, v_pre, keep
    )
    err_in, err_out = keep[:2]
    send = left(theirs, near_inputs, grads, near_err_in, basis_in)
    arrived = lax.ppermute(send, "c", SWAP)
    left_out_part = left_out(near_grad_y, hidden, near_err_out, basis_out)
    rows = left(mine, near_inputs, grads, near_err_in, basis_in, arrived, left_out_part)

    rows, later_inputs = lax.optimization_barrier((rows, inputs))
    received = lax.all_to_all(rows.reshape(CHIPS, EACH1, 128), CHIP, 0, 0)
    inputs_turned = turned(later_inputs)
    received, inputs_turned = lax.optimization_barrier((received, inputs_turned))
    own = lax.all_to_all(answer_left(me[None], received), CHIP, 0, 0).reshape(ROWS1, 128)
    other = lax.ppermute(own, "c", SWAP)
    left_out_sum = own[L_ROWS : L_ROWS + LO_ROWS]

    send, keep_out = right_out(place, left_out_sum, grad_y, hidden, err_out)
    arrived = lax.ppermute(send, "c", SWAP)
    right_part = right_own(jnp.concatenate([mine, theirs]), own, inputs, err_in)
    arrived, right_part = lax.optimization_barrier((arrived, right_part))
    gram_out = send[RO_ROWS:] + arrived[RO_ROWS:]
    quarters = (keep_out + arrived[:RO_ROWS]).reshape(4, PIECE, 128)
    pieces = [jnp.concatenate([quarters[shift], gram_out]) for shift in range(4)]
    pieces = [pieces[0]] + [lax.ppermute(pieces[shift], "z", ring(shift)) for shift in OTHERS]
    rows, gram_out = join(right_other(other, *right_part, grads), *pieces)

    received = lax.all_to_all(rows.reshape(N_DP, EACH2, 128), ("x", "y"), 0, 0)
    inverse, ortho_out = invert(own, other, left_out_sum, gram_out)
    received, inverse, ortho_out = lax.optimization_barrier((received, inverse, ortho_out))
    everywhere = answer_right(received)
    everywhere, inverse = lax.optimization_barrier((everywhere, inverse))
    summed = lax.all_to_all(everywhere, ("x", "y"), 0, 0).reshape(ROWS2, 128)
    ortho_in = turn(mine, own, other, inverse)
    summed, ortho_in = lax.optimization_barrier((summed, ortho_in))

    pieces = [summed[RI_ROWS:]]
    pieces += [lax.ppermute(pieces[0], "z", ring(shift)) for shift in (1, 2, 3)]
    new_in, factor_in = rest_in(summed, inverse, inputs_turned, ortho_in, grads, err_in)
    pieces, factor_in = lax.optimization_barrier((pieces, factor_in))
    own_right = jnp.concatenate(pieces)
    other_right = lax.ppermute(own_right, "c", SWAP)
    new_out, factor_out = rest_out(place, own_right, other_right, inverse, ortho_out, hidden, grad_y, err_out)
    return new_in[None], new_out[None], factor_in, factor_out


def solution(mesh):
    fine = Mesh(mesh.devices.reshape(4, 4, 4, 2), ("x", "y", "z", "c"))
    dp, head = ("x", "y"), ("z", "c")
    placed = (
        P(dp, None),
        P(dp, None),
        P(dp, head),
        P(dp, head),
        P(dp, head),
        P(head, None),
        P(dp, None, None, head),
        P(dp, head, None),
        P(None, None, head),
        P(),
    )
    return jax.shard_map(
        shards,
        mesh=fine,
        in_specs=placed,
        out_specs=(P(dp, None, None, head), P(dp, head, None), P(None, None, head), P()),
        check_vma=False,
    )
```

```python
import functools

import jax
import jax.numpy as jnp
from jax import lax
from jax.experimental import pallas as pl
from jax.experimental.pallas import tpu as pltpu
from jax.sharding import Mesh, PartitionSpec as P

TOK = 256
DK = 128
HEADS = 3
COLS = HEADS * DK
RANK = 64
D = 3072
HALF = D // 2
TILE = 512
STEPS = HALF // TILE
CT = TILE // 128
N_DP = 16
CHIPS = 64
L_ROWS = 12 * 3 * RANK
LO_ROWS = HEADS * RANK
ROWS1 = 2560
EACH1 = 40
L_STEP = CT * 3 * RANK
RI_ROWS = 9 * RANK
RO_ROWS = 12 * RANK
ROWS2 = 768
EACH2 = 48
PIECE = HEADS * RANK

f32 = jnp.float32
bf16 = jnp.bfloat16
EXACT = lax.Precision.HIGHEST
VMEM = 24 * 1024 * 1024


def cost(us):
    return pl.CostEstimate(flops=int(us * 1e9), bytes_accessed=int(us * 3e6), transcendentals=0)


def nn(a, b):
    return lax.dot_general(a, b, (((1,), (0,)), ((), ())), preferred_element_type=f32)


def nt(a, b):
    return lax.dot_general(a, b, (((1,), (1,)), ((), ())), preferred_element_type=f32)


def tn(a, b):
    return lax.dot_general(a, b, (((0,), (0,)), ((), ())), preferred_element_type=f32)


def exact_nn(a, b):
    return lax.dot_general(a, b, (((1,), (0,)), ((), ())), precision=EXACT, preferred_element_type=f32)


def exact_nt(a, b):
    return lax.dot_general(a, b, (((1,), (1,)), ((), ())), precision=EXACT, preferred_element_type=f32)


def split2(a):
    high = a.astype(bf16)
    return high, (a - high.astype(f32)).astype(bf16)


def split3(a):
    high = a.astype(bf16)
    rest = a - high.astype(f32)
    mid = rest.astype(bf16)
    return high, mid, (rest - mid.astype(f32)).astype(bf16)


def summed3(ones, a):
    parts = nn(ones, jnp.concatenate(split3(a), axis=1))
    width = a.shape[1]
    return parts[:, :width] + (parts[:, width : 2 * width] + parts[:, 2 * width :])


def stacked(a):
    return jnp.concatenate(split2(a), axis=0)


def folded(a):
    half = a.shape[0] // 2
    return a[:half] + a[half:]


def head_forward(q, f):
    q_gate = 1.0 / (1.0 + jnp.exp(-q))
    query = q * q_gate
    small = jnp.exp(-jnp.abs(f))
    key = jnp.where(f >= 0, small, 1.0) / (1.0 + small)
    decay = jnp.where(f >= 0, 1.0, small) / (1.0 + small)
    log_decay = jnp.minimum(f, 0.0) - jnp.log1p(small)
    row = lax.broadcasted_iota(jnp.int32, (TOK, TOK), 0)
    col = lax.broadcasted_iota(jnp.int32, (TOK, TOK), 1)
    running = summed3(jnp.where(row >= col, 1.0, 0.0).astype(bf16), log_decay)
    differ = row ^ col
    scores = jnp.zeros((TOK, TOK), f32)
    levels = []
    for size in (128, 64, 32, 16, 8):
        blocks = running.reshape(TOK // (2 * size), 2 * size, DK)
        spread = (blocks - blocks[:, size - 1 : size, :]).reshape(TOK, DK)
        if size > 8:
            q_scale = jnp.exp(jnp.minimum(spread, 0.0))
            k_scale = jnp.exp(jnp.minimum(-spread, 0.0))
            mask = (differ >= size) & (differ < 2 * size) & (row > col)
        else:
            q_scale = jnp.exp(spread)
            k_scale = jnp.exp(-spread)
            mask = (differ < 2 * size) & (row >= col)
        q_high, q_low = split2(query * q_scale)
        k_high, k_low = split2(key * k_scale)
        level = nt(
            jnp.concatenate([q_high, q_high, q_low], axis=1),
            jnp.concatenate([k_high, k_low, k_high], axis=1),
        )
        scores = jnp.where(mask, level, scores)
        levels.append((q_scale, k_scale, q_high, q_low, k_high, k_low))
    return (query, key, decay, q_gate), levels, split2(scores)


def head_backward(gates, levels, scores, v, grad_o):
    query, key, decay, q_gate = gates
    row = lax.broadcasted_iota(jnp.int32, (TOK, TOK), 0)
    col = lax.broadcasted_iota(jnp.int32, (TOK, TOK), 1)
    differ = row ^ col
    grad_s = split2(nt(grad_o, v))
    grad_st = split2(nt(v, grad_o))
    grad_query = jnp.zeros((TOK, DK), f32)
    grad_key = jnp.zeros((TOK, DK), f32)
    for size, (q_scale, k_scale, q_high, q_low, k_high, k_low) in zip((128, 64, 32, 16, 8), levels):
        if size > 8:
            within = (differ >= size) & (differ < 2 * size)
            mask, mask_t = within & (row > col), within & (row < col)
        else:
            within = differ < 2 * size
            mask, mask_t = within & (row >= col), within & (row <= col)
        keep = jnp.where(mask, 1.0, 0.0).astype(bf16)
        keep_t = jnp.where(mask_t, 1.0, 0.0).astype(bf16)
        both = nn(grad_s[0] * keep, jnp.concatenate([k_high, k_low], axis=1))
        grad_query += q_scale * (both[:, :DK] + both[:, DK:] + nn(grad_s[1] * keep, k_high))
        both = nn(grad_st[0] * keep_t, jnp.concatenate([q_high, q_low], axis=1))
        grad_key += k_scale * (both[:, :DK] + both[:, DK:] + nn(grad_st[1] * keep_t, q_high))
    grad_v = tn(scores[0], grad_o) + tn(scores[1], grad_o)
    upper = jnp.where(row <= col, 1.0, 0.0).astype(bf16)
    grad_decay = summed3(upper, query * grad_query - key * grad_key)
    grad_q = grad_query * (q_gate + query * (1.0 - q_gate))
    return grad_q, key * (grad_decay - grad_key * decay), grad_v


def recurrence_kernel(q_hbm, f_hbm, v_hbm, gy_hbm, w_hbm, *refs):
    sources, (hid_ref, grad_ref), kept, (q_scr, f_scr, v_scr, gy_scr, w_scr, sem) = (
        refs[:4],
        refs[4:6],
        refs[6:10],
        refs[10:],
    )
    pairs = list(zip((q_hbm, f_hbm, v_hbm, gy_hbm, w_hbm), (q_scr, f_scr, v_scr, gy_scr, w_scr)))
    copies = [pltpu.make_async_copy(a, b, sem.at[i]) for i, (a, b) in enumerate(pairs + list(zip(sources, kept)))]
    for copy in copies:
        copy.start()
    for copy in copies[:3]:
        copy.wait()
    for h in range(HEADS):
        mine = slice(DK * h, DK * (h + 1))
        gates, levels, scores = head_forward(q_scr[:, mine].astype(f32), f_scr[:, mine].astype(f32))
        v = v_scr[:, mine]
        hid_ref[:, mine] = (nn(scores[0], v) + nn(scores[1], v)).astype(bf16)
        if h == 0:
            for copy in copies[3:5]:
                copy.wait()
            grad_o = nt(gy_scr[...], w_scr[...]).astype(bf16)
        for p, grad in enumerate(head_backward(gates, levels, scores, v, grad_o[:, mine])):
            grad_ref[p, :, mine] = grad.astype(bf16)
    for copy in copies[5:]:
        copy.wait()


def held(*arrays):
    return [pltpu.with_memory_space_constraint(a, pltpu.VMEM) for a in arrays]


def streamed(*arrays):
    return [pltpu.with_memory_space_constraint(a, pltpu.HBM) for a in arrays]


ANY = pl.BlockSpec(memory_space=pl.ANY)


def fetched(step, steps, column, width, sources, slots, sem):
    def copies(j):
        at = pl.ds(pl.multiple_of(column(j) * width, width), width)
        for i, (axis, source) in enumerate(sources):
            index = [slice(None)] * len(source.shape)
            index[axis] = at
            yield pltpu.make_async_copy(source.at[tuple(index)], slots[i].at[j], sem.at[i, j])

    @pl.when(step == 0)
    def _():
        for j in range(steps):
            for copy in copies(j):
                copy.start()

    for copy in copies(step):
        copy.wait()
    return [slot.at[step] for slot in slots]


def recurrence(grad_y, w_out, q_pre, f_pre, v_pre, keep):
    operands = (q_pre, f_pre, v_pre, grad_y, w_out) + keep
    whole = pl.BlockSpec(memory_space=pltpu.VMEM)
    return pl.pallas_call(
        recurrence_kernel,
        in_specs=[ANY] * len(operands),
        out_specs=[whole] * 2 + [ANY] * len(keep),
        out_shape=[
            jax.ShapeDtypeStruct((TOK, COLS), bf16),
            jax.ShapeDtypeStruct((3, TOK, COLS), bf16),
        ]
        + [pltpu.VMEM(a.shape, a.dtype) for a in keep],
        scratch_shapes=[pltpu.VMEM(a.shape, a.dtype) for a in operands[:5]]
        + [pltpu.SemaphoreType.DMA((len(operands),))],
        cost_estimate=cost(8),
        compiler_params=pltpu.CompilerParams(vmem_limit_bytes=VMEM),
        name="recurrence",
    )(*streamed(*operands))


def tiles_of(a):
    return [a[:, 128 * i : 128 * (i + 1)] for i in range(a.shape[1] // 128)]


def left_tiles(half_ref, x_ref, grads_ref, err_in_ref, basis_in_ref):
    bases = [stacked(basis_in_ref[p]) for p in range(3)]
    tokens = jnp.concatenate([stacked(folded(nt(bases[p], grads_ref[p]))) for p in range(3)], axis=0)
    for step in range(STEPS):
        at = pl.ds(pl.multiple_of(half_ref[0] * HALF + step * TILE, TILE), TILE)
        from_tokens = nn(tokens, x_ref[:, at])
        for p in range(3):
            part = from_tokens[2 * RANK * p : 2 * RANK * (p + 1)] + nt(bases[p], err_in_ref[p, at, :])
            for i, tile in enumerate(tiles_of(folded(part))):
                yield step * L_STEP + (3 * i + p) * RANK, tile


def left_send_kernel(half_ref, x_ref, grads_ref, err_in_ref, basis_in_ref, left_ref):
    for at, tile in left_tiles(half_ref, x_ref, grads_ref, err_in_ref, basis_in_ref):
        left_ref[at : at + RANK, :] = tile


def left_keep_kernel(half_ref, x_ref, grads_ref, err_in_ref, basis_in_ref, arrived_ref, left_out_ref, rows_ref):
    rows_ref[L_ROWS : L_ROWS + LO_ROWS, :] = left_out_ref[...]
    rows_ref[L_ROWS + LO_ROWS :, :] = jnp.zeros((ROWS1 - L_ROWS - LO_ROWS, 128), f32)
    for at, tile in left_tiles(half_ref, x_ref, grads_ref, err_in_ref, basis_in_ref):
        rows_ref[at : at + RANK, :] = tile + arrived_ref[at : at + RANK, :]


def left(half, inputs, grads, err_in, basis_in, *arrived):
    return pl.pallas_call(
        left_keep_kernel if arrived else left_send_kernel,
        in_specs=[pl.BlockSpec(memory_space=pltpu.SMEM)] + [pl.BlockSpec(memory_space=pltpu.VMEM)] * (4 + len(arrived)),
        out_shape=jax.ShapeDtypeStruct((ROWS1 if arrived else L_ROWS, 128), f32),
        cost_estimate=cost(3),
        compiler_params=pltpu.CompilerParams(vmem_limit_bytes=VMEM),
        name="left_keep" if arrived else "left_send",
    )(half, *held(inputs), grads, *held(err_in), basis_in, *arrived)


def left_out_kernel(gy_ref, hid_ref, err_out_ref, basis_out_ref, left_out_ref):
    basis = stacked(basis_out_ref[...])
    tokens = stacked(folded(nt(basis, gy_ref[...])))
    part = folded(nt(basis, err_out_ref[...]) + nn(tokens, hid_ref[...]))
    for i, tile in enumerate(tiles_of(part)):
        left_out_ref[RANK * i : RANK * (i + 1), :] = tile


def left_out(grad_y, hidden, err_out, basis_out):
    return pl.pallas_call(
        left_out_kernel,
        out_shape=jax.ShapeDtypeStruct((LO_ROWS, 128), f32),
        cost_estimate=cost(4),
        compiler_params=pltpu.CompilerParams(vmem_limit_bytes=VMEM),
        name="left_out",
    )(*held(grad_y), hidden, *held(err_out), basis_out)


def turned_kernel(x_ref, turned_ref):
    turned_ref[...] = x_ref[...].astype(f32).T.astype(bf16)


def turned(inputs):
    return pl.pallas_call(
        turned_kernel,
        grid=(D // TILE,),
        in_specs=[pl.BlockSpec((TOK, TILE), lambda j: (0, j))],
        out_specs=pl.BlockSpec((TILE, TOK), lambda j: (j, 0)),
        out_shape=pltpu.HBM((D, TOK), bf16),
        cost_estimate=cost(3),
        compiler_params=pltpu.CompilerParams(vmem_limit_bytes=VMEM),
        name="turned",
    )(*streamed(inputs))


def wide(block, rows):
    return jnp.concatenate([block[i * rows : (i + 1) * rows] for i in range(block.shape[0] // rows)], axis=1)


def answer_left_kernel(me_ref, received_ref, answer_ref):
    over_xy = []
    for z in range(4):
        total = received_ref[z]
        for i in range(1, N_DP):
            total += received_ref[4 * i + z]
        over_xy.append(total)
    total = (over_xy[0] + over_xy[1]) + (over_xy[2] + over_xy[3])
    row = me_ref[0] * EACH1 + lax.broadcasted_iota(jnp.int32, (EACH1, 128), 0)
    for z in range(4):
        answer = jnp.where(row >= L_ROWS, over_xy[z], total)
        for i in range(N_DP):
            answer_ref[4 * i + z] = answer


def answer_left(me, received):
    whole = pl.BlockSpec((CHIPS, EACH1, 128), lambda j, m: (0, 0, 0))
    return pl.pallas_call(
        answer_left_kernel,
        grid_spec=pltpu.PrefetchScalarGridSpec(num_scalar_prefetch=1, grid=(1,), in_specs=[whole], out_specs=whole),
        out_shape=jax.ShapeDtypeStruct((CHIPS, EACH1, 128), f32),
        cost_estimate=cost(2),
        compiler_params=pltpu.CompilerParams(vmem_limit_bytes=VMEM),
        name="answer_left",
    )(me, received)


def answer_right_kernel(received_ref, answer_ref):
    total = received_ref[0]
    for i in range(1, N_DP):
        total += received_ref[i]
    for i in range(N_DP):
        answer_ref[i] = total


def answer_right(received):
    return pl.pallas_call(
        answer_right_kernel,
        out_shape=jax.ShapeDtypeStruct((N_DP, EACH2, 128), f32),
        cost_estimate=cost(1),
        compiler_params=pltpu.CompilerParams(vmem_limit_bytes=VMEM),
        name="answer_right",
    )(received)


def right_out_kernel(place_ref, left_out_ref, hid_ref, gy_hbm, err_out_hbm, send_ref, keep_ref, gy_scr, err_out_scr, sem):
    def column(j):
        at = lax.rem(place_ref[0] + 1 + j // 4, 2) * 4 + lax.rem(place_ref[1] + j % 4, 4)
        return pl.ds(pl.multiple_of(at * COLS, COLS), COLS)

    copies = [
        (
            pltpu.make_async_copy(gy_hbm.at[:, column(j)], gy_scr.at[j], sem.at[0, j]),
            pltpu.make_async_copy(err_out_hbm.at[:, column(j)], err_out_scr.at[j], sem.at[1, j]),
        )
        for j in range(8)
    ]
    for pair in copies:
        for copy in pair:
            copy.start()
    left_out = wide(left_out_ref[...], RANK)
    factor = stacked(left_out)
    both = jnp.concatenate([factor, stacked(folded(nt(factor, hid_ref[...])))], axis=1)
    send_ref[RO_ROWS:, :] = jnp.concatenate([exact_nt(left_out, left_out), jnp.zeros((RANK, RANK), f32)], axis=1)
    for j in range(8):
        for copy in copies[j]:
            copy.wait()
        part = folded(nn(both, jnp.concatenate([err_out_scr[j], gy_scr[j]], axis=0)))
        ref = send_ref if j < 4 else keep_ref
        for i, tile in enumerate(tiles_of(part)):
            at = (j % 4) * PIECE + i * RANK
            ref[at : at + RANK, :] = tile


def right_out(place, left_out_sum, grad_y, hidden, err_out):
    whole = pl.BlockSpec(memory_space=pltpu.VMEM)
    return pl.pallas_call(
        right_out_kernel,
        in_specs=[pl.BlockSpec(memory_space=pltpu.SMEM), whole, whole, ANY, ANY],
        out_shape=[
            jax.ShapeDtypeStruct((RO_ROWS + RANK, 128), f32),
            jax.ShapeDtypeStruct((RO_ROWS, 128), f32),
        ],
        scratch_shapes=[
            pltpu.VMEM((8, TOK, COLS), bf16),
            pltpu.VMEM((8, COLS, COLS), bf16),
            pltpu.SemaphoreType.DMA((2, 8)),
        ],
        cost_estimate=cost(3),
        compiler_params=pltpu.CompilerParams(vmem_limit_bytes=VMEM),
        name="right_out",
    )(place, left_out_sum, hidden, *streamed(grad_y, err_out))


def right_tile(rows, x, err_in, rights):
    high, low = split2(rows)
    for p in range(3):
        mine = slice(RANK * p, RANK * (p + 1))
        rights[p] += folded(nn(jnp.concatenate([high[mine], low[mine]], axis=0), err_in[p]))
    return folded(nt(jnp.concatenate([high, low], axis=0), x))


def near_copies(half, x_hbm, err_in_hbm, x_out, err_in_out, sem):
    copies = []
    for j in range(STEPS):
        at = pl.ds(pl.multiple_of(half * HALF + j * TILE, TILE), TILE)
        to = slice(j * TILE, (j + 1) * TILE)
        copies.append(pltpu.make_async_copy(x_hbm.at[:, at], x_out.at[:, to], sem.at[0, j]))
        copies.append(pltpu.make_async_copy(err_in_hbm.at[:, at], err_in_out.at[:, to], sem.at[1, j]))
    return copies


def right_sums(left_ref, x_ref, err_in_ref, tokens, rights):
    for j in range(STEPS):
        mine = slice(j * TILE, (j + 1) * TILE)
        rows = wide(left_ref[L_STEP * j : L_STEP * (j + 1), :], 3 * RANK)
        tokens += right_tile(rows, x_ref[:, mine], err_in_ref.at[:, mine], rights)
    return tokens


def right_own_kernel(half_ref, own_ref, x_ref, err_in_ref, x_hbm, err_in_hbm, right_ref, token_ref, x_out, err_in_out, sem):
    copies = near_copies(half_ref[0], x_hbm, err_in_hbm, x_out, err_in_out, sem)
    for copy in copies:
        copy.start()
    rights = [jnp.zeros((RANK, COLS), f32)] * 3
    token_ref[...] = right_sums(own_ref, x_ref, err_in_ref, jnp.zeros((3 * RANK, TOK), f32), rights)
    for p in range(3):
        right_ref[p] = rights[p]
    for copy in copies:
        copy.wait()


def right_own(other_half, own, near_inputs, near_err_in, inputs, err_in):
    whole = pl.BlockSpec(memory_space=pltpu.VMEM)
    return pl.pallas_call(
        right_own_kernel,
        in_specs=[pl.BlockSpec(memory_space=pltpu.SMEM), whole, whole, whole, ANY, ANY],
        out_specs=[whole, whole, ANY, ANY],
        out_shape=[
            jax.ShapeDtypeStruct((3, RANK, COLS), f32),
            jax.ShapeDtypeStruct((3 * RANK, TOK), f32),
            pltpu.VMEM((TOK, HALF), bf16),
            pltpu.VMEM((3, HALF, COLS), bf16),
        ],
        scratch_shapes=[pltpu.SemaphoreType.DMA((2, STEPS))],
        cost_estimate=cost(3),
        compiler_params=pltpu.CompilerParams(vmem_limit_bytes=VMEM),
        name="right_own",
    )(other_half, own, *held(near_inputs, near_err_in), *streamed(inputs, err_in))


def right_other_kernel(other_ref, right_ref, token_ref, x_ref, err_in_ref, grads_ref, rows_ref):
    rights = [right_ref[p] for p in range(3)]
    tokens = right_sums(other_ref, x_ref, err_in_ref, token_ref[...], rights)
    for p in range(3):
        total = rights[p] + folded(nn(stacked(tokens[RANK * p : RANK * (p + 1)]), grads_ref[p]))
        for i, tile in enumerate(tiles_of(total)):
            at = (HEADS * p + i) * RANK
            rows_ref[at : at + RANK, :] = tile


def right_other(other, right_part, token_part, inputs, err_in, grads):
    return pl.pallas_call(
        right_other_kernel,
        out_shape=jax.ShapeDtypeStruct((RI_ROWS, 128), f32),
        cost_estimate=cost(4),
        compiler_params=pltpu.CompilerParams(vmem_limit_bytes=VMEM),
        name="right_other",
    )(other, right_part, token_part, *held(inputs, err_in), grads)


def join_kernel(right_ref, own_ref, first_ref, second_ref, third_ref, rows_ref, gram_ref):
    piece = (own_ref[...] + first_ref[...]) + (second_ref[...] + third_ref[...])
    rows_ref[:RI_ROWS, :] = right_ref[...]
    rows_ref[RI_ROWS:, :] = piece[:PIECE]
    gram_ref[...] = piece[PIECE:]


def join(*operands):
    return pl.pallas_call(
        join_kernel,
        out_shape=[jax.ShapeDtypeStruct((ROWS2, 128), f32), jax.ShapeDtypeStruct((RANK, 128), f32)],
        cost_estimate=cost(1),
        compiler_params=pltpu.CompilerParams(vmem_limit_bytes=VMEM),
        name="join",
    )(*operands)


def gram_kernel(half_ref, own_ref, other_ref, x_hbm, err_in_hbm, gram_ref, x_out, err_in_out, sem):
    copies = near_copies(half_ref[0], x_hbm, err_in_hbm, x_out, err_in_out, sem)
    for copy in copies:
        copy.start()
    gram = jnp.zeros((3 * RANK, 3 * RANK), f32)
    for ref in (own_ref, other_ref):
        for i in range(STEPS):
            rows = wide(ref[L_STEP * i : L_STEP * (i + 1), :], 3 * RANK)
            gram += exact_nt(rows, rows)
    gram_ref[...] = gram
    for copy in copies:
        copy.wait()


def gram(half, own, other, inputs, err_in):
    whole = pl.BlockSpec(memory_space=pltpu.VMEM)
    return pl.pallas_call(
        gram_kernel,
        in_specs=[pl.BlockSpec(memory_space=pltpu.SMEM), whole, whole, ANY, ANY],
        out_specs=[whole, ANY, ANY],
        out_shape=[
            jax.ShapeDtypeStruct((3 * RANK, 3 * RANK), f32),
            pltpu.VMEM((TOK, HALF), bf16),
            pltpu.VMEM((3, HALF, COLS), bf16),
        ],
        scratch_shapes=[pltpu.SemaphoreType.DMA((2, STEPS))],
        cost_estimate=cost(3),
        compiler_params=pltpu.CompilerParams(vmem_limit_bytes=VMEM),
        name="gram",
    )(half, own, other, *streamed(inputs, err_in))


def invert_kernel(gram_in_ref, left_out_ref, gram_out_ref, inverse_ref, ortho_out_ref):
    eye = jnp.where(
        lax.broadcasted_iota(jnp.int32, (RANK, RANK), 0) == lax.broadcasted_iota(jnp.int32, (RANK, RANK), 1),
        1.0,
        0.0,
    )
    gram = gram_in_ref[...]
    for p in range(3):
        mine = slice(RANK * p, RANK * (p + 1))
        inverse_ref[p] = jnp.concatenate([gram[mine, mine], eye], axis=1)
    inverse_ref[3] = jnp.concatenate([gram_out_ref[:, :RANK], eye], axis=1)
    rows8 = lax.broadcasted_iota(jnp.int32, (1, 8, 1), 1)
    tiles = [inverse_ref[:, 8 * t : 8 * t + 8, :] for t in range(RANK // 8)]
    for j in range(RANK):
        top, at = divmod(j, 8)
        pivot_row = tiles[top][:, at : at + 1, :]
        scaled = pivot_row * (1.0 / pivot_row[:, :, j : j + 1])
        for t in range(top, RANK // 8):
            column = tiles[t][:, :, j : j + 1]
            if t == top:
                column = jnp.where(rows8 > at, column, 0.0)
            tiles[t] = tiles[t] - column * scaled
    work = jnp.concatenate(tiles, axis=1)
    lane = lax.broadcasted_iota(jnp.int32, (4, RANK, 128), 2)
    sub = lax.broadcasted_iota(jnp.int32, (4, RANK, 128), 1)
    diagonal = jnp.sum(jnp.where(lane == sub, work, 0.0), axis=2, keepdims=True)
    inverse = work * lax.rsqrt(diagonal)
    inverse_ref[...] = inverse
    ortho_out_ref[...] = exact_nn(inverse[3, :, RANK:], wide(left_out_ref[...], RANK))


def invert(gram_in, left_out_sum, gram_out):
    return pl.pallas_call(
        invert_kernel,
        out_shape=[
            jax.ShapeDtypeStruct((4, RANK, 128), f32),
            jax.ShapeDtypeStruct((RANK, COLS), f32),
        ],
        cost_estimate=cost(10),
        compiler_params=pltpu.CompilerParams(vmem_limit_bytes=VMEM),
        name="invert",
    )(gram_in, left_out_sum, gram_out)


def turn_kernel(half_ref, own_ref, other_ref, inverse_ref, ortho_ref):
    step = pl.program_id(0)

    def turn(ref):
        rows = wide(ref[...], 3 * RANK)
        for p in range(3):
            high, low = split2(exact_nn(inverse_ref[p, :, RANK:], rows[RANK * p : RANK * (p + 1)]))
            both = jnp.concatenate([high.astype(f32), low.astype(f32)], axis=0)
            ortho_ref[p] = both.T.astype(bf16)

    @pl.when(step < STEPS)
    def _():
        turn(own_ref)

    @pl.when(step >= STEPS)
    def _():
        turn(other_ref)


def turn(half, own, other, inverse):
    def column(j, h):
        return lax.rem(j // STEPS + h[0], 2) * STEPS + lax.rem(j, STEPS)

    return pl.pallas_call(
        turn_kernel,
        grid_spec=pltpu.PrefetchScalarGridSpec(
            num_scalar_prefetch=1,
            grid=(2 * STEPS,),
            in_specs=[
                pl.BlockSpec((CT * 3 * RANK, 128), lambda j, h: (jnp.minimum(j, STEPS - 1), 0)),
                pl.BlockSpec((CT * 3 * RANK, 128), lambda j, h: (jnp.maximum(j - STEPS, 0), 0)),
                pl.BlockSpec((4, RANK, 128), lambda j, h: (0, 0, 0)),
            ],
            out_specs=pl.BlockSpec((3, TILE, 128), lambda j, h: (0, column(j, h), 0)),
        ),
        out_shape=pltpu.HBM((3, D, 128), bf16),
        cost_estimate=cost(6),
        compiler_params=pltpu.CompilerParams(vmem_limit_bytes=VMEM),
        name="turn",
    )(half, own, other, inverse)


def rest_in_kernel(summed_in_ref, inverse_ref, grads_ref, turned_hbm, ortho_hbm, err_in_hbm, rest_in_ref,
                   factor_in_ref, in_scr, turned_scr, ortho_scr, err_in_scr, sem):
    step = pl.program_id(0)
    turned_ref, ortho_ref, err_in_ref = fetched(
        step,
        D // TILE,
        lambda j: j,
        TILE,
        [(0, turned_hbm), (1, ortho_hbm), (1, err_in_hbm)],
        [turned_scr, ortho_scr, err_in_scr],
        sem,
    )

    @pl.when(step == 0)
    def _():
        for p in range(3):
            right = wide(summed_in_ref[pl.ds(HEADS * RANK * p, HEADS * RANK), :], RANK) * (1.0 / N_DP)
            factor = exact_nn(inverse_ref[p, :, RANK:], right)
            factor_in_ref[p] = factor
            high, low = split2(-factor)
            in_scr[p] = jnp.concatenate([high, high, low, jnp.zeros_like(low)], axis=0)

    moments = nn(turned_ref[...], jnp.concatenate([grads_ref[p] for p in range(3)], axis=1))
    for p in range(3):
        moment = moments[:, COLS * p : COLS * (p + 1)] + err_in_ref[p].astype(f32)
        both = jnp.concatenate([ortho_ref[p], ortho_ref[p]], axis=1)
        rest_in_ref[p] = (moment + nn(both, in_scr[p])).astype(bf16)


def rest_in(summed, inverse, turned, ortho_in, grads, err_in):
    return pl.pallas_call(
        rest_in_kernel,
        grid=(D // TILE,),
        in_specs=[
            pl.BlockSpec((RI_ROWS, 128), lambda j: (0, 0)),
            pl.BlockSpec((4, RANK, 128), lambda j: (0, 0, 0)),
            pl.BlockSpec((3, TOK, COLS), lambda j: (0, 0, 0)),
            ANY,
            ANY,
            ANY,
        ],
        out_specs=[
            pl.BlockSpec((3, TILE, COLS), lambda j: (0, j, 0)),
            pl.BlockSpec((3, RANK, COLS), lambda j: (0, 0, 0)),
        ],
        scratch_shapes=[
            pltpu.VMEM((3, 4 * RANK, COLS), bf16),
            pltpu.VMEM((D // TILE, TILE, TOK), bf16),
            pltpu.VMEM((D // TILE, 3, TILE, 128), bf16),
            pltpu.VMEM((D // TILE, 3, TILE, COLS), bf16),
            pltpu.SemaphoreType.DMA((3, D // TILE)),
        ],
        out_shape=[
            jax.ShapeDtypeStruct((3, D, COLS), bf16),
            jax.ShapeDtypeStruct((3, RANK, COLS), f32),
        ],
        cost_estimate=cost(10),
        compiler_params=pltpu.CompilerParams(vmem_limit_bytes=VMEM),
        name="rest_in",
    )(summed, inverse, grads, *streamed(turned, ortho_in, err_in))


def rest_out_kernel(place_ref, *refs):
    piece_refs, (inverse_ref, ortho_out_ref, hid_ref, gy_hbm, err_out_hbm) = refs[:4], refs[4:9]
    rest_hbm, factor_hbm, gy_scr, err_out_scr, rest_scr, factor_scr, in_sem, out_sem = refs[9:]

    def column(j):
        at = lax.rem(place_ref[0] + j // 4, 2) * 4 + lax.rem(place_ref[1] + 4 - j % 4, 4)
        return pl.ds(pl.multiple_of(at * COLS, COLS), COLS)

    into = [
        (
            pltpu.make_async_copy(gy_hbm.at[:, column(j)], gy_scr.at[j], in_sem.at[0, j]),
            pltpu.make_async_copy(err_out_hbm.at[:, column(j)], err_out_scr.at[j], in_sem.at[1, j]),
        )
        for j in range(8)
    ]
    out = [
        (
            pltpu.make_async_copy(rest_scr.at[j], rest_hbm.at[:, column(j)], out_sem.at[0, j]),
            pltpu.make_async_copy(factor_scr.at[j], factor_hbm.at[:, column(j)], out_sem.at[1, j]),
        )
        for j in range(8)
    ]
    for pair in into:
        for copy in pair:
            copy.start()
    high, low = split2(ortho_out_ref[...])
    stack = jnp.concatenate([high, high, low, jnp.zeros_like(low)], axis=0)
    both = jnp.concatenate([hid_ref[...], stack], axis=0).astype(f32).T.astype(bf16)
    inverse = inverse_ref[3, :, RANK:]
    for j in range(0, 8, 2):
        mine = slice(PIECE * (j // 4), PIECE * (j // 4 + 1))
        right = jnp.concatenate([wide(piece_refs[k % 4][mine, :], RANK) for k in (j, j + 1)], axis=1)
        factor = exact_nn(inverse, right * (1.0 / N_DP))
        high, low = split2(-factor)
        for k in (j, j + 1):
            for copy in into[k]:
                copy.wait()
        gy = jnp.concatenate([gy_scr[j], gy_scr[j + 1]], axis=1)
        total = nn(both, jnp.concatenate([gy, high, low, high, jnp.zeros_like(low)], axis=0))
        for i, k in enumerate((j, j + 1)):
            mine = slice(COLS * i, COLS * (i + 1))
            factor_scr[k] = factor[:, mine]
            rest_scr[k] = (total[:, mine] + err_out_scr[k].astype(f32)).astype(bf16)
            for copy in out[k]:
                copy.start()
    for pair in out:
        for copy in pair:
            copy.wait()


def rest_out(place, pieces, inverse, ortho_out, hidden, grad_y, err_out):
    whole = pl.BlockSpec(memory_space=pltpu.VMEM)
    return pl.pallas_call(
        rest_out_kernel,
        in_specs=[pl.BlockSpec(memory_space=pltpu.SMEM)] + [whole] * 7 + [ANY] * 2,
        out_specs=[ANY, ANY],
        scratch_shapes=[
            pltpu.VMEM((8, TOK, COLS), bf16),
            pltpu.VMEM((8, COLS, COLS), bf16),
            pltpu.VMEM((8, COLS, COLS), bf16),
            pltpu.VMEM((8, RANK, COLS), f32),
            pltpu.SemaphoreType.DMA((2, 8)),
            pltpu.SemaphoreType.DMA((2, 8)),
        ],
        out_shape=[pltpu.HBM((COLS, D), bf16), pltpu.HBM((RANK, D), f32)],
        cost_estimate=cost(6),
        compiler_params=pltpu.CompilerParams(vmem_limit_bytes=VMEM),
        name="rest_out",
    )(place, *pieces, inverse, ortho_out, hidden, *streamed(grad_y, err_out))


CHIP = ("x", "y", "z")
SWAP = [(0, 1), (1, 0)]
OTHERS = (2, 1, 3)


def ring(shift):
    return [(a, (a + shift) % 4) for a in range(4)]


def shards(inputs, grad_y, q_pre, f_pre, v_pre, w_out, err_in, err_out, basis_in, basis_out):
    keep = (err_in[0], err_out[0], inputs, grad_y)
    core = lax.axis_index("c").astype(jnp.int32)
    z = lax.axis_index("z").astype(jnp.int32)
    me = (lax.axis_index("x") * 4 + lax.axis_index("y")).astype(jnp.int32) * 4 + z
    mine = core[None]
    theirs = 1 - mine
    place = jnp.stack([core, z])
    hidden, grads, near_err_in, near_err_out, near_inputs, near_grad_y = recurrence(
        grad_y, w_out, q_pre, f_pre, v_pre, keep
    )
    err_in, err_out = keep[:2]
    send = left(theirs, near_inputs, grads, near_err_in, basis_in)
    arrived = lax.ppermute(send, "c", SWAP)
    left_out_part = left_out(near_grad_y, hidden, near_err_out, basis_out)
    rows = left(mine, near_inputs, grads, near_err_in, basis_in, arrived, left_out_part)

    rows, later_inputs = lax.optimization_barrier((rows, inputs))
    received = lax.all_to_all(rows.reshape(CHIPS, EACH1, 128), CHIP, 0, 0)
    inputs_turned = turned(later_inputs)
    received, inputs_turned = lax.optimization_barrier((received, inputs_turned))
    own = lax.all_to_all(answer_left(me[None], received), CHIP, 0, 0).reshape(ROWS1, 128)
    other = lax.ppermute(own, "c", SWAP)
    left_out_sum = own[L_ROWS : L_ROWS + LO_ROWS]

    send, keep_out = right_out(place, left_out_sum, grad_y, hidden, err_out)
    arrived = lax.ppermute(send, "c", SWAP)
    gram_in, near_inputs, near_err_in = gram(mine, own, other, inputs, err_in)
    arrived, gram_in = lax.optimization_barrier((arrived, gram_in))
    gram_out = send[RO_ROWS:] + arrived[RO_ROWS:]
    quarters = (keep_out + arrived[:RO_ROWS]).reshape(4, PIECE, 128)
    pieces = [jnp.concatenate([quarters[shift], gram_out]) for shift in range(4)]
    pieces = [pieces[0]] + [lax.ppermute(pieces[shift], "z", ring(shift)) for shift in OTHERS]
    right_part = right_own(theirs, own, near_inputs, near_err_in, inputs, err_in)
    rows, gram_out = join(right_other(other, *right_part, grads), *pieces)

    received = lax.all_to_all(rows.reshape(N_DP, EACH2, 128), ("x", "y"), 0, 0)
    inverse, ortho_out = invert(gram_in, left_out_sum, gram_out)
    received, inverse, ortho_out = lax.optimization_barrier((received, inverse, ortho_out))
    everywhere = answer_right(received)
    everywhere, inverse = lax.optimization_barrier((everywhere, inverse))
    summed = lax.all_to_all(everywhere, ("x", "y"), 0, 0).reshape(ROWS2, 128)
    ortho_in = turn(mine, own, other, inverse)
    summed, ortho_in = lax.optimization_barrier((summed, ortho_in))

    piece = summed[RI_ROWS:]
    pieces = [jnp.concatenate([piece, lax.ppermute(piece, "c", SWAP)])]
    pieces += [lax.ppermute(pieces[0], "z", ring(shift)) for shift in (1, 2, 3)]
    new_in, factor_in = rest_in(summed, inverse, inputs_turned, ortho_in, grads, err_in)
    new_out, factor_out = rest_out(place, pieces, inverse, ortho_out, hidden, grad_y, err_out)
    return new_in[None], new_out[None], factor_in, factor_out


def solution(mesh):
    fine = Mesh(mesh.devices.reshape(4, 4, 4, 2), ("x", "y", "z", "c"))
    dp, head = ("x", "y"), ("z", "c")
    placed = (
        P(dp, None),
        P(dp, None),
        P(dp, head),
        P(dp, head),
        P(dp, head),
        P(head, None),
        P(dp, None, None, head),
        P(dp, head, None),
        P(None, None, head),
        P(),
    )
    return jax.shard_map(
        shards,
        mesh=fine,
        in_specs=placed,
        out_specs=(P(dp, None, None, head), P(dp, head, None), P(None, None, head), P()),
        check_vma=False,
    )
```

```python
import functools

import jax
import jax.numpy as jnp
from jax import lax
from jax.experimental import pallas as pl
from jax.experimental.pallas import tpu as pltpu
from jax.sharding import Mesh, PartitionSpec as P

TOK = 256
DK = 128
HEADS = 3
COLS = HEADS * DK
RANK = 64
D = 3072
HALF = D // 2
TILE = 512
STEPS = HALF // TILE
CT = TILE // 128
N_DP = 16
CHIPS = 64
L_ROWS = 12 * 3 * RANK
LO_ROWS = HEADS * RANK
ROWS1 = 2560
EACH1 = 40
L_STEP = CT * 3 * RANK
RI_ROWS = 9 * RANK
RO_ROWS = 12 * RANK
ROWS2 = 768
EACH2 = 48
PIECE = HEADS * RANK

f32 = jnp.float32
bf16 = jnp.bfloat16
EXACT = lax.Precision.HIGHEST
VMEM = 24 * 1024 * 1024
VMEM_LAST = 40 * 1024 * 1024


def cost(us):
    return pl.CostEstimate(flops=int(us * 1e9), bytes_accessed=int(us * 3e6), transcendentals=0)


def nn(a, b):
    return lax.dot_general(a, b, (((1,), (0,)), ((), ())), preferred_element_type=f32)


def nt(a, b):
    return lax.dot_general(a, b, (((1,), (1,)), ((), ())), preferred_element_type=f32)


def tn(a, b):
    return lax.dot_general(a, b, (((0,), (0,)), ((), ())), preferred_element_type=f32)


def exact_nt(a, b):
    return lax.dot_general(a, b, (((1,), (1,)), ((), ())), precision=EXACT, preferred_element_type=f32)


def split2(a):
    high = a.astype(bf16)
    return high, (a - high.astype(f32)).astype(bf16)


def thrice(a, b):
    a_high, a_low = split2(a)
    b_high, b_low = split2(b)
    return nn(jnp.concatenate([a_high, a_high, a_low], axis=1), jnp.concatenate([b_high, b_low, b_high], axis=0))


def split3(a):
    high = a.astype(bf16)
    rest = a - high.astype(f32)
    mid = rest.astype(bf16)
    return high, mid, (rest - mid.astype(f32)).astype(bf16)


def summed3(ones, a):
    parts = nn(ones, jnp.concatenate(split3(a), axis=1))
    width = a.shape[1]
    return parts[:, :width] + (parts[:, width : 2 * width] + parts[:, 2 * width :])


def stacked(a):
    return jnp.concatenate(split2(a), axis=0)


def folded(a):
    half = a.shape[0] // 2
    return a[:half] + a[half:]


def head_forward(q, f):
    q_gate = 1.0 / (1.0 + jnp.exp(-q))
    query = q * q_gate
    small = jnp.exp(-jnp.abs(f))
    key = jnp.where(f >= 0, small, 1.0) / (1.0 + small)
    decay = jnp.where(f >= 0, 1.0, small) / (1.0 + small)
    log_decay = jnp.minimum(f, 0.0) - jnp.log1p(small)
    row = lax.broadcasted_iota(jnp.int32, (TOK, TOK), 0)
    col = lax.broadcasted_iota(jnp.int32, (TOK, TOK), 1)
    running = summed3(jnp.where(row >= col, 1.0, 0.0).astype(bf16), log_decay)
    differ = row ^ col
    scores = jnp.zeros((TOK, TOK), f32)
    levels = []
    for size in (128, 64, 32, 16, 8):
        blocks = running.reshape(TOK // (2 * size), 2 * size, DK)
        spread = (blocks - blocks[:, size - 1 : size, :]).reshape(TOK, DK)
        if size > 8:
            q_scale = jnp.exp(jnp.minimum(spread, 0.0))
            k_scale = jnp.exp(jnp.minimum(-spread, 0.0))
            mask = (differ >= size) & (differ < 2 * size) & (row > col)
        else:
            q_scale = jnp.exp(spread)
            k_scale = jnp.exp(-spread)
            mask = (differ < 2 * size) & (row >= col)
        q_high, q_low = split2(query * q_scale)
        k_high, k_low = split2(key * k_scale)
        level = nt(
            jnp.concatenate([q_high, q_high, q_low], axis=1),
            jnp.concatenate([k_high, k_low, k_high], axis=1),
        )
        scores = jnp.where(mask, level, scores)
        levels.append((q_scale, k_scale, q_high, q_low, k_high, k_low))
    return (query, key, decay, q_gate), levels, split2(scores)


def head_backward(gates, levels, scores, v, grad_o):
    query, key, decay, q_gate = gates
    row = lax.broadcasted_iota(jnp.int32, (TOK, TOK), 0)
    col = lax.broadcasted_iota(jnp.int32, (TOK, TOK), 1)
    differ = row ^ col
    grad_s = split2(nt(grad_o, v))
    grad_st = split2(nt(v, grad_o))
    grad_query = jnp.zeros((TOK, DK), f32)
    grad_key = jnp.zeros((TOK, DK), f32)
    for size, (q_scale, k_scale, q_high, q_low, k_high, k_low) in zip((128, 64, 32, 16, 8), levels):
        if size > 8:
            within = (differ >= size) & (differ < 2 * size)
            mask, mask_t = within & (row > col), within & (row < col)
        else:
            within = differ < 2 * size
            mask, mask_t = within & (row >= col), within & (row <= col)
        keep = jnp.where(mask, 1.0, 0.0).astype(bf16)
        keep_t = jnp.where(mask_t, 1.0, 0.0).astype(bf16)
        both = nn(grad_s[0] * keep, jnp.concatenate([k_high, k_low], axis=1))
        grad_query += q_scale * (both[:, :DK] + both[:, DK:] + nn(grad_s[1] * keep, k_high))
        both = nn(grad_st[0] * keep_t, jnp.concatenate([q_high, q_low], axis=1))
        grad_key += k_scale * (both[:, :DK] + both[:, DK:] + nn(grad_st[1] * keep_t, q_high))
    grad_v = tn(scores[0], grad_o) + tn(scores[1], grad_o)
    upper = jnp.where(row <= col, 1.0, 0.0).astype(bf16)
    grad_decay = summed3(upper, query * grad_query - key * grad_key)
    grad_q = grad_query * (q_gate + query * (1.0 - q_gate))
    return grad_q, key * (grad_decay - grad_key * decay), grad_v


def recurrence_kernel(q_hbm, f_hbm, v_hbm, gy_hbm, w_hbm, *refs):
    sources, (hid_ref, grad_ref), kept, (q_scr, f_scr, v_scr, gy_scr, w_scr, sem) = (
        refs[:4],
        refs[4:6],
        refs[6:10],
        refs[10:],
    )
    pairs = list(zip((q_hbm, f_hbm, v_hbm, gy_hbm, w_hbm), (q_scr, f_scr, v_scr, gy_scr, w_scr)))
    copies = [pltpu.make_async_copy(a, b, sem.at[i]) for i, (a, b) in enumerate(pairs + list(zip(sources, kept)))]
    for copy in copies:
        copy.start()
    for copy in copies[:3]:
        copy.wait()
    for h in range(HEADS):
        mine = slice(DK * h, DK * (h + 1))
        gates, levels, scores = head_forward(q_scr[:, mine].astype(f32), f_scr[:, mine].astype(f32))
        v = v_scr[:, mine]
        hid_ref[:, mine] = (nn(scores[0], v) + nn(scores[1], v)).astype(bf16)
        if h == 0:
            for copy in copies[3:5]:
                copy.wait()
            grad_o = nt(gy_scr[...], w_scr[...]).astype(bf16)
        for p, grad in enumerate(head_backward(gates, levels, scores, v, grad_o[:, mine])):
            grad_ref[p, :, mine] = grad.astype(bf16)
    for copy in copies[5:]:
        copy.wait()


def held(*arrays):
    return [pltpu.with_memory_space_constraint(a, pltpu.VMEM) for a in arrays]


def streamed(*arrays):
    return [pltpu.with_memory_space_constraint(a, pltpu.HBM) for a in arrays]


ANY = pl.BlockSpec(memory_space=pl.ANY)


def fetched(step, steps, column, width, sources, slots, sem):
    def copies(j):
        at = pl.ds(pl.multiple_of(column(j) * width, width), width)
        for i, (axis, source) in enumerate(sources):
            index = [slice(None)] * len(source.shape)
            index[axis] = at
            yield pltpu.make_async_copy(source.at[tuple(index)], slots[i].at[j], sem.at[i, j])

    @pl.when(step == 0)
    def _():
        for j in range(steps):
            for copy in copies(j):
                copy.start()

    for copy in copies(step):
        copy.wait()
    return [slot.at[step] for slot in slots]


def recurrence(grad_y, w_out, q_pre, f_pre, v_pre, keep):
    operands = (q_pre, f_pre, v_pre, grad_y, w_out) + keep
    whole = pl.BlockSpec(memory_space=pltpu.VMEM)
    return pl.pallas_call(
        recurrence_kernel,
        in_specs=[ANY] * len(operands),
        out_specs=[whole] * 2 + [ANY] * len(keep),
        out_shape=[
            jax.ShapeDtypeStruct((TOK, COLS), bf16),
            jax.ShapeDtypeStruct((3, TOK, COLS), bf16),
        ]
        + [pltpu.VMEM(a.shape, a.dtype) for a in keep],
        scratch_shapes=[pltpu.VMEM(a.shape, a.dtype) for a in operands[:5]]
        + [pltpu.SemaphoreType.DMA((len(operands),))],
        cost_estimate=cost(8),
        compiler_params=pltpu.CompilerParams(vmem_limit_bytes=VMEM),
        name="recurrence",
    )(*streamed(*operands))


def tiles_of(a):
    return [a[:, 128 * i : 128 * (i + 1)] for i in range(a.shape[1] // 128)]


def left_tiles(half_ref, x_ref, grads_ref, err_in_ref, basis_in_ref):
    bases = [stacked(basis_in_ref[p]) for p in range(3)]
    tokens = jnp.concatenate([stacked(folded(nt(bases[p], grads_ref[p]))) for p in range(3)], axis=0)
    for step in range(STEPS):
        at = pl.ds(pl.multiple_of(half_ref[0] * HALF + step * TILE, TILE), TILE)
        from_tokens = nn(tokens, x_ref[:, at])
        for p in range(3):
            part = from_tokens[2 * RANK * p : 2 * RANK * (p + 1)] + nt(bases[p], err_in_ref[p, at, :])
            for i, tile in enumerate(tiles_of(folded(part))):
                yield step * L_STEP + (3 * i + p) * RANK, tile


def left_send_kernel(half_ref, x_ref, grads_ref, err_in_ref, basis_in_ref, left_ref):
    for at, tile in left_tiles(half_ref, x_ref, grads_ref, err_in_ref, basis_in_ref):
        left_ref[at : at + RANK, :] = tile


def left_keep_kernel(half_ref, x_ref, grads_ref, err_in_ref, basis_in_ref, arrived_ref, left_out_ref, rows_hbm, rows_scr, sem):
    parts = [slice(L_STEP * step, L_STEP * (step + 1)) for step in range(STEPS)] + [slice(L_ROWS, ROWS1)]
    copies = [pltpu.make_async_copy(rows_scr.at[part], rows_hbm.at[part], sem.at[i]) for i, part in enumerate(parts)]
    rows_scr[L_ROWS : L_ROWS + LO_ROWS, :] = left_out_ref[...]
    rows_scr[L_ROWS + LO_ROWS :, :] = jnp.zeros((ROWS1 - L_ROWS - LO_ROWS, 128), f32)
    copies[STEPS].start()
    for i, (at, tile) in enumerate(left_tiles(half_ref, x_ref, grads_ref, err_in_ref, basis_in_ref)):
        rows_scr[at : at + RANK, :] = tile + arrived_ref[at : at + RANK, :]
        if (i + 1) % (3 * CT) == 0:
            copies[i // (3 * CT)].start()
    for copy in copies:
        copy.wait()


def left(half, inputs, grads, err_in, basis_in, *arrived):
    keep = {}
    if arrived:
        keep = dict(
            out_specs=ANY, scratch_shapes=[pltpu.VMEM((ROWS1, 128), f32), pltpu.SemaphoreType.DMA((STEPS + 1,))]
        )
    return pl.pallas_call(
        left_keep_kernel if arrived else left_send_kernel,
        in_specs=[pl.BlockSpec(memory_space=pltpu.SMEM)] + [pl.BlockSpec(memory_space=pltpu.VMEM)] * (4 + len(arrived)),
        out_shape=pltpu.HBM((ROWS1, 128), f32) if arrived else jax.ShapeDtypeStruct((L_ROWS, 128), f32),
        cost_estimate=cost(3),
        compiler_params=pltpu.CompilerParams(vmem_limit_bytes=VMEM),
        name="left_keep" if arrived else "left_send",
        **keep,
    )(half, *held(inputs), grads, *held(err_in), basis_in, *arrived)


def left_out_kernel(gy_ref, hid_ref, err_out_ref, basis_out_ref, left_out_ref):
    basis = stacked(basis_out_ref[...])
    tokens = stacked(folded(nt(basis, gy_ref[...])))
    part = folded(nt(basis, err_out_ref[...]) + nn(tokens, hid_ref[...]))
    for i, tile in enumerate(tiles_of(part)):
        left_out_ref[RANK * i : RANK * (i + 1), :] = tile


def left_out(grad_y, hidden, err_out, basis_out):
    return pl.pallas_call(
        left_out_kernel,
        out_shape=jax.ShapeDtypeStruct((LO_ROWS, 128), f32),
        cost_estimate=cost(4),
        compiler_params=pltpu.CompilerParams(vmem_limit_bytes=VMEM),
        name="left_out",
    )(*held(grad_y), hidden, *held(err_out), basis_out)


def ahead_kernel(x_ref, grads_ref, err_in_ref, hid_ref, gy_ref, err_out_ref, x_later_ref, turned_ref, moment_in_ref,
                 moment_out_ref):
    turned_ref[...] = x_ref[...].astype(f32).T.astype(bf16)
    later = x_later_ref[...].astype(f32).T.astype(bf16)
    moments = nn(later, jnp.concatenate([grads_ref[p] for p in range(3)], axis=1))
    for p in range(3):
        moment_in_ref[p] = moments[:, COLS * p : COLS * (p + 1)] + err_in_ref[p].astype(f32)
    moment_out_ref[...] = tn(hid_ref[...], gy_ref[...]) + err_out_ref[...].astype(f32)


def ahead(inputs, grads, err_in, hidden, grad_y, err_out):
    wide_tile = D // STEPS
    return pl.pallas_call(
        ahead_kernel,
        grid=(STEPS,),
        in_specs=[
            pl.BlockSpec((TOK, TILE), lambda j: (0, j)),
            pl.BlockSpec((3, TOK, COLS), lambda j: (0, 0, 0)),
            pl.BlockSpec((3, TILE, COLS), lambda j: (0, j + STEPS, 0)),
            pl.BlockSpec((TOK, COLS), lambda j: (0, 0)),
            pl.BlockSpec((TOK, wide_tile), lambda j: (0, j)),
            pl.BlockSpec((COLS, wide_tile), lambda j: (0, j)),
            pl.BlockSpec((TOK, TILE), lambda j: (0, j + STEPS)),
        ],
        out_specs=[
            pl.BlockSpec((TILE, TOK), lambda j: (j, 0)),
            pl.BlockSpec((3, TILE, COLS), lambda j: (0, j, 0)),
            pl.BlockSpec((COLS, wide_tile), lambda j: (0, j)),
        ],
        out_shape=[
            pltpu.HBM((HALF, TOK), bf16),
            pltpu.HBM((3, HALF, COLS), f32),
            pltpu.HBM((COLS, D), f32),
        ],
        cost_estimate=cost(9),
        compiler_params=pltpu.CompilerParams(vmem_limit_bytes=VMEM),
        name="ahead",
    )(*streamed(inputs, grads, err_in, hidden, grad_y, err_out, inputs))


def wide(block, rows):
    return jnp.concatenate([block[i * rows : (i + 1) * rows] for i in range(block.shape[0] // rows)], axis=1)


def answer_left_kernel(me_ref, received_ref, answer_ref):
    over_xy = []
    for z in range(4):
        total = received_ref[z]
        for i in range(1, N_DP):
            total += received_ref[4 * i + z]
        over_xy.append(total)
    total = (over_xy[0] + over_xy[1]) + (over_xy[2] + over_xy[3])
    row = me_ref[0] * EACH1 + lax.broadcasted_iota(jnp.int32, (EACH1, 128), 0)
    for z in range(4):
        answer = jnp.where(row >= L_ROWS, over_xy[z], total)
        for i in range(N_DP):
            answer_ref[4 * i + z] = answer


def answer_left(me, received):
    whole = pl.BlockSpec((CHIPS, EACH1, 128), lambda j, m: (0, 0, 0))
    return pl.pallas_call(
        answer_left_kernel,
        grid_spec=pltpu.PrefetchScalarGridSpec(num_scalar_prefetch=1, grid=(1,), in_specs=[whole], out_specs=whole),
        out_shape=jax.ShapeDtypeStruct((CHIPS, EACH1, 128), f32),
        cost_estimate=cost(2),
        compiler_params=pltpu.CompilerParams(vmem_limit_bytes=VMEM),
        name="answer_left",
    )(me, received)


def answer_right_kernel(received_ref, answer_ref):
    total = received_ref[0]
    for i in range(1, N_DP):
        total += received_ref[i]
    for i in range(N_DP):
        answer_ref[i] = total


def answer_right(received):
    return pl.pallas_call(
        answer_right_kernel,
        out_shape=jax.ShapeDtypeStruct((N_DP, EACH2, 128), f32),
        cost_estimate=cost(1),
        compiler_params=pltpu.CompilerParams(vmem_limit_bytes=VMEM),
        name="answer_right",
    )(received)


def right_out_kernel(place_ref, left_out_ref, hid_ref, gy_hbm, err_out_hbm, send_ref, keep_ref, gy_scr, err_out_scr, sem):
    def column(j):
        at = lax.rem(place_ref[0] + 1 + j // 4, 2) * 4 + lax.rem(place_ref[1] + j % 4, 4)
        return pl.ds(pl.multiple_of(at * COLS, COLS), COLS)

    copies = [
        (
            pltpu.make_async_copy(gy_hbm.at[:, column(j)], gy_scr.at[j], sem.at[0, j]),
            pltpu.make_async_copy(err_out_hbm.at[:, column(j)], err_out_scr.at[j], sem.at[1, j]),
        )
        for j in range(8)
    ]
    for pair in copies:
        for copy in pair:
            copy.start()
    left_out = wide(left_out_ref[...], RANK)
    factor = stacked(left_out)
    both = jnp.concatenate([factor, stacked(folded(nt(factor, hid_ref[...])))], axis=1)
    send_ref[RO_ROWS:, :] = jnp.concatenate([exact_nt(left_out, left_out), jnp.zeros((RANK, RANK), f32)], axis=1)
    for j in range(0, 8, 2):
        for pair in copies[j : j + 2]:
            for copy in pair:
                copy.wait()
        err_out = jnp.concatenate([err_out_scr[j], err_out_scr[j + 1]], axis=1)
        gy = jnp.concatenate([gy_scr[j], gy_scr[j + 1]], axis=1)
        part = folded(nn(both, jnp.concatenate([err_out, gy], axis=0)))
        ref = send_ref if j < 4 else keep_ref
        for i, tile in enumerate(tiles_of(part)):
            at = (j % 4) * PIECE + i * RANK
            ref[at : at + RANK, :] = tile


def right_out(place, left_out_sum, grad_y, hidden, err_out):
    whole = pl.BlockSpec(memory_space=pltpu.VMEM)
    return pl.pallas_call(
        right_out_kernel,
        in_specs=[pl.BlockSpec(memory_space=pltpu.SMEM), whole, whole, ANY, ANY],
        out_shape=[
            jax.ShapeDtypeStruct((RO_ROWS + RANK, 128), f32),
            jax.ShapeDtypeStruct((RO_ROWS, 128), f32),
        ],
        scratch_shapes=[
            pltpu.VMEM((8, TOK, COLS), bf16),
            pltpu.VMEM((8, COLS, COLS), bf16),
            pltpu.SemaphoreType.DMA((2, 8)),
        ],
        cost_estimate=cost(3),
        compiler_params=pltpu.CompilerParams(vmem_limit_bytes=VMEM),
        name="right_out",
    )(place, left_out_sum, hidden, *streamed(grad_y, err_out))


def right_tile(rows, x, err_in, rights):
    high, low = split2(rows)
    for p in range(3):
        mine = slice(RANK * p, RANK * (p + 1))
        rights[p] += folded(nn(jnp.concatenate([high[mine], low[mine]], axis=0), err_in[p]))
    return folded(nt(jnp.concatenate([high, low], axis=0), x))


def near_copies(half, x_hbm, err_in_hbm, x_out, err_in_out, sem):
    copies = []
    for j in range(STEPS):
        at = pl.ds(pl.multiple_of(half * HALF + j * TILE, TILE), TILE)
        to = slice(j * TILE, (j + 1) * TILE)
        copies.append(pltpu.make_async_copy(x_hbm.at[:, at], x_out.at[:, to], sem.at[0, j]))
        copies.append(pltpu.make_async_copy(err_in_hbm.at[:, at], err_in_out.at[:, to], sem.at[1, j]))
    return copies


def right_sums(left_ref, x_ref, err_in_ref, tokens, rights):
    for j in range(STEPS):
        mine = slice(j * TILE, (j + 1) * TILE)
        rows = wide(left_ref[L_STEP * j : L_STEP * (j + 1), :], 3 * RANK)
        tokens += right_tile(rows, x_ref[:, mine], err_in_ref.at[:, mine], rights)
    return tokens


def right_own_kernel(half_ref, own_ref, x_ref, err_in_ref, x_hbm, err_in_hbm, right_ref, token_ref, x_out, err_in_out, sem):
    copies = near_copies(half_ref[0], x_hbm, err_in_hbm, x_out, err_in_out, sem)
    for copy in copies:
        copy.start()
    rights = [jnp.zeros((RANK, COLS), f32)] * 3
    token_ref[...] = right_sums(own_ref, x_ref, err_in_ref, jnp.zeros((3 * RANK, TOK), f32), rights)
    for p in range(3):
        right_ref[p] = rights[p]
    for copy in copies:
        copy.wait()


def right_own(other_half, own, near_inputs, near_err_in, inputs, err_in):
    whole = pl.BlockSpec(memory_space=pltpu.VMEM)
    return pl.pallas_call(
        right_own_kernel,
        in_specs=[pl.BlockSpec(memory_space=pltpu.SMEM), whole, whole, whole, ANY, ANY],
        out_specs=[whole, whole, ANY, ANY],
        out_shape=[
            jax.ShapeDtypeStruct((3, RANK, COLS), f32),
            jax.ShapeDtypeStruct((3 * RANK, TOK), f32),
            pltpu.VMEM((TOK, HALF), bf16),
            pltpu.VMEM((3, HALF, COLS), bf16),
        ],
        scratch_shapes=[pltpu.SemaphoreType.DMA((2, STEPS))],
        cost_estimate=cost(3),
        compiler_params=pltpu.CompilerParams(vmem_limit_bytes=VMEM),
        name="right_own",
    )(other_half, own, *held(near_inputs, near_err_in), *streamed(inputs, err_in))


def right_other_kernel(other_ref, right_ref, token_ref, x_ref, err_in_ref, grads_ref, rows_ref):
    rights = [right_ref[p] for p in range(3)]
    tokens = right_sums(other_ref, x_ref, err_in_ref, token_ref[...], rights)
    for p in range(3):
        total = rights[p] + folded(nn(stacked(tokens[RANK * p : RANK * (p + 1)]), grads_ref[p]))
        for i, tile in enumerate(tiles_of(total)):
            at = (HEADS * p + i) * RANK
            rows_ref[at : at + RANK, :] = tile


def right_other(other, right_part, token_part, inputs, err_in, grads):
    return pl.pallas_call(
        right_other_kernel,
        out_shape=jax.ShapeDtypeStruct((RI_ROWS, 128), f32),
        cost_estimate=cost(4),
        compiler_params=pltpu.CompilerParams(vmem_limit_bytes=VMEM),
        name="right_other",
    )(other, right_part, token_part, *held(inputs, err_in), grads)


def join_kernel(right_ref, own_ref, first_ref, second_ref, third_ref, rows_ref, gram_ref):
    piece = (own_ref[...] + first_ref[...]) + (second_ref[...] + third_ref[...])
    rows_ref[:RI_ROWS, :] = right_ref[...]
    rows_ref[RI_ROWS:, :] = piece[:PIECE]
    gram_ref[...] = piece[PIECE:]


def join(*operands):
    return pl.pallas_call(
        join_kernel,
        out_shape=[jax.ShapeDtypeStruct((ROWS2, 128), f32), jax.ShapeDtypeStruct((RANK, 128), f32)],
        cost_estimate=cost(1),
        compiler_params=pltpu.CompilerParams(vmem_limit_bytes=VMEM),
        name="join",
    )(*operands)


def gram_kernel(half_ref, own_ref, other_ref, x_hbm, err_in_hbm, gram_ref, x_out, err_in_out, sem):
    copies = near_copies(half_ref[0], x_hbm, err_in_hbm, x_out, err_in_out, sem)
    for copy in copies:
        copy.start()
    gram = jnp.zeros((3 * RANK, 3 * RANK), f32)
    for ref in (own_ref, other_ref):
        for i in range(STEPS):
            rows = wide(ref[L_STEP * i : L_STEP * (i + 1), :], 3 * RANK)
            gram += exact_nt(rows, rows)
    gram_ref[...] = gram
    for copy in copies:
        copy.wait()


def gram(half, own, other, inputs, err_in):
    whole = pl.BlockSpec(memory_space=pltpu.VMEM)
    return pl.pallas_call(
        gram_kernel,
        in_specs=[pl.BlockSpec(memory_space=pltpu.SMEM), whole, whole, ANY, ANY],
        out_specs=[whole, ANY, ANY],
        out_shape=[
            jax.ShapeDtypeStruct((3 * RANK, 3 * RANK), f32),
            pltpu.VMEM((TOK, HALF), bf16),
            pltpu.VMEM((3, HALF, COLS), bf16),
        ],
        scratch_shapes=[pltpu.SemaphoreType.DMA((2, STEPS))],
        cost_estimate=cost(3),
        compiler_params=pltpu.CompilerParams(vmem_limit_bytes=VMEM),
        name="gram",
    )(half, own, other, *streamed(inputs, err_in))


def invert_kernel(gram_in_ref, left_out_ref, gram_out_ref, inverse_ref, ortho_out_ref):
    eye = jnp.where(
        lax.broadcasted_iota(jnp.int32, (RANK, RANK), 0) == lax.broadcasted_iota(jnp.int32, (RANK, RANK), 1),
        1.0,
        0.0,
    )
    gram = gram_in_ref[...]
    for p in range(3):
        mine = slice(RANK * p, RANK * (p + 1))
        inverse_ref[p] = jnp.concatenate([gram[mine, mine], eye], axis=1)
    inverse_ref[3] = jnp.concatenate([gram_out_ref[:, :RANK], eye], axis=1)
    rows8 = lax.broadcasted_iota(jnp.int32, (1, 8, 1), 1)
    tiles = [inverse_ref[:, 8 * t : 8 * t + 8, :] for t in range(RANK // 8)]
    for j in range(RANK):
        top, at = divmod(j, 8)
        pivot_row = tiles[top][:, at : at + 1, :]
        scaled = pivot_row * (1.0 / pivot_row[:, :, j : j + 1])
        for t in range(top, RANK // 8):
            column = tiles[t][:, :, j : j + 1]
            if t == top:
                column = jnp.where(rows8 > at, column, 0.0)
            tiles[t] = tiles[t] - column * scaled
    work = jnp.concatenate(tiles, axis=1)
    lane = lax.broadcasted_iota(jnp.int32, (4, RANK, 128), 2)
    sub = lax.broadcasted_iota(jnp.int32, (4, RANK, 128), 1)
    diagonal = jnp.sum(jnp.where(lane == sub, work, 0.0), axis=2, keepdims=True)
    inverse = work * lax.rsqrt(diagonal)
    inverse_ref[...] = inverse
    ortho_out_ref[...] = thrice(inverse[3, :, RANK:], wide(left_out_ref[...], RANK))


def invert(gram_in, left_out_sum, gram_out):
    return pl.pallas_call(
        invert_kernel,
        out_shape=[
            jax.ShapeDtypeStruct((4, RANK, 128), f32),
            jax.ShapeDtypeStruct((RANK, COLS), f32),
        ],
        cost_estimate=cost(10),
        compiler_params=pltpu.CompilerParams(vmem_limit_bytes=VMEM),
        name="invert",
    )(gram_in, left_out_sum, gram_out)


def turn_kernel(half_ref, own_ref, other_ref, inverse_ref, ortho_ref):
    step = pl.program_id(0)

    def turn(ref):
        rows = wide(ref[...], 3 * RANK)
        for p in range(3):
            high, low = split2(thrice(inverse_ref[p, :, RANK:], rows[RANK * p : RANK * (p + 1)]))
            both = jnp.concatenate([high.astype(f32), low.astype(f32)], axis=0)
            ortho_ref[p] = both.T.astype(bf16)

    @pl.when(step < STEPS)
    def _():
        turn(own_ref)

    @pl.when(step >= STEPS)
    def _():
        turn(other_ref)


def turn(half, own, other, inverse):
    def column(j, h):
        return lax.rem(j // STEPS + h[0], 2) * STEPS + lax.rem(j, STEPS)

    return pl.pallas_call(
        turn_kernel,
        grid_spec=pltpu.PrefetchScalarGridSpec(
            num_scalar_prefetch=1,
            grid=(2 * STEPS,),
            in_specs=[
                pl.BlockSpec((CT * 3 * RANK, 128), lambda j, h: (jnp.minimum(j, STEPS - 1), 0)),
                pl.BlockSpec((CT * 3 * RANK, 128), lambda j, h: (jnp.maximum(j - STEPS, 0), 0)),
                pl.BlockSpec((4, RANK, 128), lambda j, h: (0, 0, 0)),
            ],
            out_specs=pl.BlockSpec((3, TILE, 128), lambda j, h: (0, column(j, h), 0)),
        ),
        out_shape=pltpu.HBM((3, D, 128), bf16),
        cost_estimate=cost(6),
        compiler_params=pltpu.CompilerParams(vmem_limit_bytes=VMEM),
        name="turn",
    )(half, own, other, inverse)


def rest_in_kernel(summed_in_ref, inverse_hbm, grads_hbm, turned_hbm, err_in_hbm, ortho_hbm, moment_hbm, rest_hbm,
                   factor_in_ref, inverse_scr, grads_scr, turned_scr, err_in_scr, ortho_scr, moment_scr, rest_scr, in_sem,
                   out_sem):
    def rows(j):
        return slice(TILE * j, TILE * (j + 1))

    tiles = range(2 * STEPS)
    first = [
        pltpu.make_async_copy(inverse_hbm, inverse_scr, in_sem.at[0, len(tiles)]),
        pltpu.make_async_copy(grads_hbm, grads_scr, in_sem.at[1, len(tiles)]),
    ]
    into = [[pltpu.make_async_copy(ortho_hbm.at[:, rows(j)], ortho_scr.at[j], in_sem.at[0, j])] for j in tiles]
    for j in range(STEPS):
        into[j].append(pltpu.make_async_copy(turned_hbm.at[rows(j)], turned_scr.at[j], in_sem.at[1, j]))
        into[j].append(pltpu.make_async_copy(err_in_hbm.at[:, rows(j)], err_in_scr.at[j], in_sem.at[2, j]))
        into[j + STEPS].append(
            pltpu.make_async_copy(moment_hbm.at[:, rows(j)], moment_scr.at[j], in_sem.at[1, j + STEPS])
        )
    out = [pltpu.make_async_copy(rest_scr.at[j], rest_hbm.at[:, rows(j)], out_sem.at[j]) for j in tiles]
    for copy in first:
        copy.start()
    for group in into:
        for copy in group:
            copy.start()
    for copy in first:
        copy.wait()
    grads = jnp.concatenate([grads_scr[p] for p in range(3)], axis=1)
    weights = []
    for p in range(3):
        right = wide(summed_in_ref[HEADS * RANK * p : HEADS * RANK * (p + 1), :], RANK) * (1.0 / N_DP)
        factor = thrice(inverse_scr[p, :, RANK:], right)
        factor_in_ref[p] = factor
        high, low = split2(-factor)
        weights.append(jnp.concatenate([high, high, low, jnp.zeros_like(low)], axis=0))
    for j in tiles:
        for copy in into[j]:
            copy.wait()
        moments = nn(turned_scr[j], grads) if j < STEPS else None
        for p in range(3):
            if j < STEPS:
                moment = moments[:, COLS * p : COLS * (p + 1)] + err_in_scr[j, p].astype(f32)
            else:
                moment = moment_scr[j - STEPS, p]
            both = jnp.concatenate([ortho_scr[j, p], ortho_scr[j, p]], axis=1)
            rest_scr[j, p] = (moment + nn(both, weights[p])).astype(bf16)
        out[j].start()
    for copy in out:
        copy.wait()


def rest_in(summed, inverse, grads, turned, err_in, ortho_in, moment_in):
    whole = pl.BlockSpec(memory_space=pltpu.VMEM)
    tiles = 2 * STEPS
    return pl.pallas_call(
        rest_in_kernel,
        in_specs=[whole] + [ANY] * 6,
        out_specs=[ANY, whole],
        scratch_shapes=[
            pltpu.VMEM((4, RANK, 128), f32),
            pltpu.VMEM((3, TOK, COLS), bf16),
            pltpu.VMEM((STEPS, TILE, TOK), bf16),
            pltpu.VMEM((STEPS, 3, TILE, COLS), bf16),
            pltpu.VMEM((tiles, 3, TILE, 128), bf16),
            pltpu.VMEM((STEPS, 3, TILE, COLS), f32),
            pltpu.VMEM((tiles, 3, TILE, COLS), bf16),
            pltpu.SemaphoreType.DMA((3, tiles + 1)),
            pltpu.SemaphoreType.DMA((tiles,)),
        ],
        out_shape=[
            pltpu.HBM((3, D, COLS), bf16),
            jax.ShapeDtypeStruct((3, RANK, COLS), f32),
        ],
        cost_estimate=cost(9),
        compiler_params=pltpu.CompilerParams(vmem_limit_bytes=VMEM_LAST),
        name="rest_in",
    )(summed, *streamed(inverse, grads, turned, err_in, ortho_in, moment_in))


def rest_out_kernel(place_ref, *refs):
    piece_refs, (inverse_hbm, ortho_out_hbm, moment_hbm) = refs[:4], refs[4:7]
    rest_hbm, factor_hbm, inverse_scr, ortho_out_scr, moment_scr, rest_scr, factor_scr, first_sem, in_sem, out_sem = refs[7:]
    small = zip((inverse_hbm.at[3], ortho_out_hbm), (inverse_scr, ortho_out_scr))
    first = [pltpu.make_async_copy(a, b, first_sem.at[i]) for i, (a, b) in enumerate(small)]

    def column(j):
        at = lax.rem(place_ref[0] + j // 4, 2) * 4 + lax.rem(place_ref[1] + 4 - j % 4, 4)
        return pl.ds(pl.multiple_of(at * COLS, COLS), COLS)

    into = [pltpu.make_async_copy(moment_hbm.at[:, column(j)], moment_scr.at[j], in_sem.at[j]) for j in range(8)]
    out = [
        (
            pltpu.make_async_copy(rest_scr.at[j], rest_hbm.at[:, column(j)], out_sem.at[0, j]),
            pltpu.make_async_copy(factor_scr.at[j], factor_hbm.at[:, column(j)], out_sem.at[1, j]),
        )
        for j in range(8)
    ]
    for copy in first:
        copy.start()
    for copy in into:
        copy.start()
    for copy in first:
        copy.wait()
    high, low = split2(ortho_out_scr[...])
    stack = jnp.concatenate([high, high, low, jnp.zeros_like(low)], axis=0)
    both = stack.astype(f32).T.astype(bf16)
    inverse = inverse_scr[:, RANK:]
    for j in range(0, 8, 2):
        mine = slice(PIECE * (j // 4), PIECE * (j // 4 + 1))
        right = jnp.concatenate([wide(piece_refs[k % 4][mine, :], RANK) for k in (j, j + 1)], axis=1)
        factor = thrice(inverse, right * (1.0 / N_DP))
        high, low = split2(-factor)
        for k in (j, j + 1):
            into[k].wait()
        total = nn(both, jnp.concatenate([high, low, high, jnp.zeros_like(low)], axis=0))
        for i, k in enumerate((j, j + 1)):
            mine = slice(COLS * i, COLS * (i + 1))
            factor_scr[k] = factor[:, mine]
            rest_scr[k] = (total[:, mine] + moment_scr[k]).astype(bf16)
            for copy in out[k]:
                copy.start()
    for pair in out:
        for copy in pair:
            copy.wait()


def rest_out(place, pieces, inverse, ortho_out, moment_out):
    whole = pl.BlockSpec(memory_space=pltpu.VMEM)
    return pl.pallas_call(
        rest_out_kernel,
        in_specs=[pl.BlockSpec(memory_space=pltpu.SMEM)] + [whole] * 4 + [ANY] * 3,
        out_specs=[ANY, ANY],
        scratch_shapes=[
            pltpu.VMEM((RANK, 128), f32),
            pltpu.VMEM((RANK, COLS), f32),
            pltpu.VMEM((8, COLS, COLS), f32),
            pltpu.VMEM((8, COLS, COLS), bf16),
            pltpu.VMEM((8, RANK, COLS), f32),
            pltpu.SemaphoreType.DMA((2,)),
            pltpu.SemaphoreType.DMA((8,)),
            pltpu.SemaphoreType.DMA((2, 8)),
        ],
        out_shape=[pltpu.HBM((COLS, D), bf16), pltpu.HBM((RANK, D), f32)],
        cost_estimate=cost(6),
        compiler_params=pltpu.CompilerParams(vmem_limit_bytes=VMEM),
        name="rest_out",
    )(place, *pieces, *streamed(inverse, ortho_out, moment_out))


CHIP = ("x", "y", "z")
SWAP = [(0, 1), (1, 0)]
OTHERS = (2, 1, 3)


def ring(shift):
    return [(a, (a + shift) % 4) for a in range(4)]


def shards(inputs, grad_y, q_pre, f_pre, v_pre, w_out, err_in, err_out, basis_in, basis_out):
    keep = (err_in[0], err_out[0], inputs, grad_y)
    core = lax.axis_index("c").astype(jnp.int32)
    z = lax.axis_index("z").astype(jnp.int32)
    me = (lax.axis_index("x") * 4 + lax.axis_index("y")).astype(jnp.int32) * 4 + z
    mine = core[None]
    theirs = 1 - mine
    place = jnp.stack([core, z])
    hidden, grads, near_err_in, near_err_out, near_inputs, near_grad_y = recurrence(
        grad_y, w_out, q_pre, f_pre, v_pre, keep
    )
    err_in, err_out = keep[:2]
    send = left(theirs, near_inputs, grads, near_err_in, basis_in)
    arrived = lax.ppermute(send, "c", SWAP)
    left_out_part = left_out(near_grad_y, hidden, near_err_out, basis_out)
    rows = left(mine, near_inputs, grads, near_err_in, basis_in, arrived, left_out_part)

    rows, hidden_now = lax.optimization_barrier((rows, hidden))
    received = lax.all_to_all(rows.reshape(CHIPS, EACH1, 128), CHIP, 0, 0)
    inputs_turned, moment_in, moment_out = ahead(inputs, grads, err_in, hidden_now, grad_y, err_out)
    received, inputs_turned = lax.optimization_barrier((received, inputs_turned))
    own = lax.all_to_all(answer_left(me[None], received), CHIP, 0, 0).reshape(ROWS1, 128)
    other = lax.ppermute(own, "c", SWAP)
    left_out_sum = own[L_ROWS : L_ROWS + LO_ROWS]

    send, keep_out = right_out(place, left_out_sum, grad_y, hidden, err_out)
    arrived = lax.ppermute(send, "c", SWAP)
    gram_in, near_inputs, near_err_in = gram(mine, own, other, inputs, err_in)
    arrived, gram_in = lax.optimization_barrier((arrived, gram_in))
    gram_out = send[RO_ROWS:] + arrived[RO_ROWS:]
    quarters = (keep_out + arrived[:RO_ROWS]).reshape(4, PIECE, 128)
    pieces = [jnp.concatenate([quarters[shift], gram_out]) for shift in range(4)]
    pieces = [pieces[0]] + [lax.ppermute(pieces[shift], "z", ring(shift)) for shift in OTHERS]
    right_part = right_own(theirs, own, near_inputs, near_err_in, inputs, err_in)
    rows, gram_out = join(right_other(other, *right_part, grads), *pieces)

    received = lax.all_to_all(rows.reshape(N_DP, EACH2, 128), ("x", "y"), 0, 0)
    inverse, ortho_out = invert(gram_in, left_out_sum, gram_out)
    received, inverse, ortho_out = lax.optimization_barrier((received, inverse, ortho_out))
    everywhere = answer_right(received)
    everywhere, inverse = lax.optimization_barrier((everywhere, inverse))
    summed = lax.all_to_all(everywhere, ("x", "y"), 0, 0).reshape(ROWS2, 128)
    ortho_in = turn(mine, own, other, inverse)
    summed, ortho_in = lax.optimization_barrier((summed, ortho_in))

    piece = summed[RI_ROWS:]
    pieces = [jnp.concatenate([piece, lax.ppermute(piece, "c", SWAP)])]
    pieces += [lax.ppermute(pieces[0], "z", ring(shift)) for shift in (1, 2, 3)]
    new_in, factor_in = rest_in(summed, inverse, grads, inputs_turned, err_in, ortho_in, moment_in)
    new_out, factor_out = rest_out(place, pieces, inverse, ortho_out, moment_out)
    return new_in[None], new_out[None], factor_in, factor_out


def solution(mesh):
    fine = Mesh(mesh.devices.reshape(4, 4, 4, 2), ("x", "y", "z", "c"))
    dp, head = ("x", "y"), ("z", "c")
    placed = (
        P(dp, None),
        P(dp, None),
        P(dp, head),
        P(dp, head),
        P(dp, head),
        P(head, None),
        P(dp, None, None, head),
        P(dp, head, None),
        P(None, None, head),
        P(),
    )
    return jax.shard_map(
        shards,
        mesh=fine,
        in_specs=placed,
        out_specs=(P(dp, None, None, head), P(dp, head, None), P(None, None, head), P()),
        check_vma=False,
    )
```

```python
import functools

import jax
import jax.numpy as jnp
from jax import lax
from jax.experimental import pallas as pl
from jax.experimental.pallas import tpu as pltpu
from jax.sharding import Mesh, PartitionSpec as P

TOK = 256
DK = 128
HEADS = 3
COLS = HEADS * DK
RANK = 64
D = 3072
HALF = D // 2
TILE = 512
STEPS = HALF // TILE
CT = TILE // 128
N_DP = 16
CHIPS = 64
L_ROWS = 12 * 3 * RANK
LO_ROWS = HEADS * RANK
ROWS1 = 2560
EACH1 = 40
L_STEP = CT * 3 * RANK
RI_ROWS = 9 * RANK
RO_ROWS = 12 * RANK
ROWS2 = 768
EACH2 = 48
PIECE = HEADS * RANK

f32 = jnp.float32
bf16 = jnp.bfloat16
EXACT = lax.Precision.HIGHEST
VMEM = 24 * 1024 * 1024
VMEM_LAST = 40 * 1024 * 1024


def cost(us):
    return pl.CostEstimate(flops=int(us * 1e9), bytes_accessed=int(us * 3e6), transcendentals=0)


def nn(a, b):
    return lax.dot_general(a, b, (((1,), (0,)), ((), ())), preferred_element_type=f32)


def nt(a, b):
    return lax.dot_general(a, b, (((1,), (1,)), ((), ())), preferred_element_type=f32)


def tn(a, b):
    return lax.dot_general(a, b, (((0,), (0,)), ((), ())), preferred_element_type=f32)


def exact_nt(a, b):
    return lax.dot_general(a, b, (((1,), (1,)), ((), ())), precision=EXACT, preferred_element_type=f32)


def split2(a):
    high = a.astype(bf16)
    return high, (a - high.astype(f32)).astype(bf16)


def thrice(a, b):
    a_high, a_low = split2(a)
    b_high, b_low = split2(b)
    return nn(jnp.concatenate([a_high, a_high, a_low], axis=1), jnp.concatenate([b_high, b_low, b_high], axis=0))


def split3(a):
    high = a.astype(bf16)
    rest = a - high.astype(f32)
    mid = rest.astype(bf16)
    return high, mid, (rest - mid.astype(f32)).astype(bf16)


def summed3(ones, a):
    parts = nn(ones, jnp.concatenate(split3(a), axis=1))
    width = a.shape[1]
    return parts[:, :width] + (parts[:, width : 2 * width] + parts[:, 2 * width :])


def stacked(a):
    return jnp.concatenate(split2(a), axis=0)


def folded(a):
    half = a.shape[0] // 2
    return a[:half] + a[half:]


def head_forward(q, f):
    q_gate = 1.0 / (1.0 + jnp.exp(-q))
    query = q * q_gate
    small = jnp.exp(-jnp.abs(f))
    key = jnp.where(f >= 0, small, 1.0) / (1.0 + small)
    decay = jnp.where(f >= 0, 1.0, small) / (1.0 + small)
    log_decay = jnp.minimum(f, 0.0) - jnp.log1p(small)
    row = lax.broadcasted_iota(jnp.int32, (TOK, TOK), 0)
    col = lax.broadcasted_iota(jnp.int32, (TOK, TOK), 1)
    running = summed3(jnp.where(row >= col, 1.0, 0.0).astype(bf16), log_decay)
    differ = row ^ col
    scores = jnp.zeros((TOK, TOK), f32)
    levels = []
    for size in (128, 64, 32, 16, 8):
        blocks = running.reshape(TOK // (2 * size), 2 * size, DK)
        spread = (blocks - blocks[:, size - 1 : size, :]).reshape(TOK, DK)
        if size > 8:
            q_scale = jnp.exp(jnp.minimum(spread, 0.0))
            k_scale = jnp.exp(jnp.minimum(-spread, 0.0))
            mask = (differ >= size) & (differ < 2 * size) & (row > col)
        else:
            q_scale = jnp.exp(spread)
            k_scale = jnp.exp(-spread)
            mask = (differ < 2 * size) & (row >= col)
        q_high, q_low = split2(query * q_scale)
        k_high, k_low = split2(key * k_scale)
        level = nt(
            jnp.concatenate([q_high, q_high, q_low], axis=1),
            jnp.concatenate([k_high, k_low, k_high], axis=1),
        )
        scores = jnp.where(mask, level, scores)
        levels.append((q_scale, k_scale, q_high, q_low, k_high, k_low))
    return (query, key, decay, q_gate), levels, split2(scores)


def head_backward(gates, levels, scores, v, grad_o):
    query, key, decay, q_gate = gates
    row = lax.broadcasted_iota(jnp.int32, (TOK, TOK), 0)
    col = lax.broadcasted_iota(jnp.int32, (TOK, TOK), 1)
    differ = row ^ col
    grad_s = split2(nt(grad_o, v))
    grad_st = split2(nt(v, grad_o))
    grad_query = jnp.zeros((TOK, DK), f32)
    grad_key = jnp.zeros((TOK, DK), f32)
    for size, (q_scale, k_scale, q_high, q_low, k_high, k_low) in zip((128, 64, 32, 16, 8), levels):
        if size > 8:
            within = (differ >= size) & (differ < 2 * size)
            mask, mask_t = within & (row > col), within & (row < col)
        else:
            within = differ < 2 * size
            mask, mask_t = within & (row >= col), within & (row <= col)
        keep = jnp.where(mask, 1.0, 0.0).astype(bf16)
        keep_t = jnp.where(mask_t, 1.0, 0.0).astype(bf16)
        both = nn(grad_s[0] * keep, jnp.concatenate([k_high, k_low], axis=1))
        grad_query += q_scale * (both[:, :DK] + both[:, DK:] + nn(grad_s[1] * keep, k_high))
        both = nn(grad_st[0] * keep_t, jnp.concatenate([q_high, q_low], axis=1))
        grad_key += k_scale * (both[:, :DK] + both[:, DK:] + nn(grad_st[1] * keep_t, q_high))
    grad_v = tn(scores[0], grad_o) + tn(scores[1], grad_o)
    upper = jnp.where(row <= col, 1.0, 0.0).astype(bf16)
    grad_decay = summed3(upper, query * grad_query - key * grad_key)
    grad_q = grad_query * (q_gate + query * (1.0 - q_gate))
    return grad_q, key * (grad_decay - grad_key * decay), grad_v


def recurrence_kernel(q_hbm, f_hbm, v_hbm, gy_hbm, w_hbm, *refs):
    sources, (hid_ref, grad_ref), kept, (q_scr, f_scr, v_scr, gy_scr, w_scr, sem) = (
        refs[:4],
        refs[4:6],
        refs[6:10],
        refs[10:],
    )
    pairs = list(zip((q_hbm, f_hbm, v_hbm, gy_hbm, w_hbm), (q_scr, f_scr, v_scr, gy_scr, w_scr)))
    copies = [pltpu.make_async_copy(a, b, sem.at[i]) for i, (a, b) in enumerate(pairs + list(zip(sources, kept)))]
    for copy in copies:
        copy.start()
    for copy in copies[:3]:
        copy.wait()
    for h in range(HEADS):
        mine = slice(DK * h, DK * (h + 1))
        gates, levels, scores = head_forward(q_scr[:, mine].astype(f32), f_scr[:, mine].astype(f32))
        v = v_scr[:, mine]
        hid_ref[:, mine] = (nn(scores[0], v) + nn(scores[1], v)).astype(bf16)
        if h == 0:
            for copy in copies[3:5]:
                copy.wait()
            grad_o = nt(gy_scr[...], w_scr[...]).astype(bf16)
        for p, grad in enumerate(head_backward(gates, levels, scores, v, grad_o[:, mine])):
            grad_ref[p, :, mine] = grad.astype(bf16)
    for copy in copies[5:]:
        copy.wait()


def held(*arrays):
    return [pltpu.with_memory_space_constraint(a, pltpu.VMEM) for a in arrays]


def streamed(*arrays):
    return [pltpu.with_memory_space_constraint(a, pltpu.HBM) for a in arrays]


ANY = pl.BlockSpec(memory_space=pl.ANY)


def fetched(step, steps, column, width, sources, slots, sem):
    def copies(j):
        at = pl.ds(pl.multiple_of(column(j) * width, width), width)
        for i, (axis, source) in enumerate(sources):
            index = [slice(None)] * len(source.shape)
            index[axis] = at
            yield pltpu.make_async_copy(source.at[tuple(index)], slots[i].at[j], sem.at[i, j])

    @pl.when(step == 0)
    def _():
        for j in range(steps):
            for copy in copies(j):
                copy.start()

    for copy in copies(step):
        copy.wait()
    return [slot.at[step] for slot in slots]


def recurrence(grad_y, w_out, q_pre, f_pre, v_pre, keep):
    operands = (q_pre, f_pre, v_pre, grad_y, w_out) + keep
    whole = pl.BlockSpec(memory_space=pltpu.VMEM)
    return pl.pallas_call(
        recurrence_kernel,
        in_specs=[ANY] * len(operands),
        out_specs=[whole] * 2 + [ANY] * len(keep),
        out_shape=[
            jax.ShapeDtypeStruct((TOK, COLS), bf16),
            jax.ShapeDtypeStruct((3, TOK, COLS), bf16),
        ]
        + [pltpu.VMEM(a.shape, a.dtype) for a in keep],
        scratch_shapes=[pltpu.VMEM(a.shape, a.dtype) for a in operands[:5]]
        + [pltpu.SemaphoreType.DMA((len(operands),))],
        cost_estimate=cost(8),
        compiler_params=pltpu.CompilerParams(vmem_limit_bytes=VMEM),
        name="recurrence",
    )(*streamed(*operands))


def tiles_of(a):
    return [a[:, 128 * i : 128 * (i + 1)] for i in range(a.shape[1] // 128)]


def left_tiles(half_ref, x_ref, grads_ref, err_in_ref, basis_in_ref):
    bases = [stacked(basis_in_ref[p]) for p in range(3)]
    tokens = jnp.concatenate([stacked(folded(nt(bases[p], grads_ref[p]))) for p in range(3)], axis=0)
    for step in range(STEPS):
        at = pl.ds(pl.multiple_of(half_ref[0] * HALF + step * TILE, TILE), TILE)
        from_tokens = nn(tokens, x_ref[:, at])
        for p in range(3):
            part = from_tokens[2 * RANK * p : 2 * RANK * (p + 1)] + nt(bases[p], err_in_ref[p, at, :])
            for i, tile in enumerate(tiles_of(folded(part))):
                yield step * L_STEP + (3 * i + p) * RANK, tile


def left_send_kernel(half_ref, x_ref, grads_ref, err_in_ref, basis_in_ref, left_ref):
    for at, tile in left_tiles(half_ref, x_ref, grads_ref, err_in_ref, basis_in_ref):
        left_ref[at : at + RANK, :] = tile


def left_keep_kernel(half_ref, x_ref, grads_ref, err_in_ref, basis_in_ref, arrived_ref, left_out_ref, rows_hbm, rows_scr, sem):
    parts = [slice(L_STEP * step, L_STEP * (step + 1)) for step in range(STEPS)] + [slice(L_ROWS, ROWS1)]
    copies = [pltpu.make_async_copy(rows_scr.at[part], rows_hbm.at[part], sem.at[i]) for i, part in enumerate(parts)]
    rows_scr[L_ROWS : L_ROWS + LO_ROWS, :] = left_out_ref[...]
    rows_scr[L_ROWS + LO_ROWS :, :] = jnp.zeros((ROWS1 - L_ROWS - LO_ROWS, 128), f32)
    copies[STEPS].start()
    for i, (at, tile) in enumerate(left_tiles(half_ref, x_ref, grads_ref, err_in_ref, basis_in_ref)):
        rows_scr[at : at + RANK, :] = tile + arrived_ref[at : at + RANK, :]
        if (i + 1) % (3 * CT) == 0:
            copies[i // (3 * CT)].start()
    for copy in copies:
        copy.wait()


def left(half, inputs, grads, err_in, basis_in, *arrived):
    keep = {}
    if arrived:
        keep = dict(
            out_specs=ANY, scratch_shapes=[pltpu.VMEM((ROWS1, 128), f32), pltpu.SemaphoreType.DMA((STEPS + 1,))]
        )
    return pl.pallas_call(
        left_keep_kernel if arrived else left_send_kernel,
        in_specs=[pl.BlockSpec(memory_space=pltpu.SMEM)] + [pl.BlockSpec(memory_space=pltpu.VMEM)] * (4 + len(arrived)),
        out_shape=pltpu.HBM((ROWS1, 128), f32) if arrived else jax.ShapeDtypeStruct((L_ROWS, 128), f32),
        cost_estimate=cost(3),
        compiler_params=pltpu.CompilerParams(vmem_limit_bytes=VMEM),
        name="left_keep" if arrived else "left_send",
        **keep,
    )(half, *held(inputs), grads, *held(err_in), basis_in, *arrived)


def left_out_kernel(gy_ref, hid_ref, err_out_ref, basis_out_ref, left_out_ref):
    basis = stacked(basis_out_ref[...])
    tokens = stacked(folded(nt(basis, gy_ref[...])))
    part = folded(nt(basis, err_out_ref[...]) + nn(tokens, hid_ref[...]))
    for i, tile in enumerate(tiles_of(part)):
        left_out_ref[RANK * i : RANK * (i + 1), :] = tile


def left_out(grad_y, hidden, err_out, basis_out):
    return pl.pallas_call(
        left_out_kernel,
        out_shape=jax.ShapeDtypeStruct((LO_ROWS, 128), f32),
        cost_estimate=cost(4),
        compiler_params=pltpu.CompilerParams(vmem_limit_bytes=VMEM),
        name="left_out",
    )(*held(grad_y), hidden, *held(err_out), basis_out)


def ahead_kernel(x_ref, grads_ref, err_in_ref, hid_ref, gy_ref, err_out_ref, x_later_ref, turned_ref, moment_in_ref,
                 moment_out_ref):
    turned_ref[...] = x_ref[...].astype(f32).T.astype(bf16)
    later = x_later_ref[...].astype(f32).T.astype(bf16)
    moments = nn(later, jnp.concatenate([grads_ref[p] for p in range(3)], axis=1))
    for p in range(3):
        moment_in_ref[p] = moments[:, COLS * p : COLS * (p + 1)] + err_in_ref[p].astype(f32)
    moment_out_ref[...] = tn(hid_ref[...], gy_ref[...]) + err_out_ref[...].astype(f32)


def ahead(inputs, grads, err_in, hidden, grad_y, err_out):
    wide_tile = D // STEPS
    return pl.pallas_call(
        ahead_kernel,
        grid=(STEPS,),
        in_specs=[
            pl.BlockSpec((TOK, TILE), lambda j: (0, j)),
            pl.BlockSpec((3, TOK, COLS), lambda j: (0, 0, 0)),
            pl.BlockSpec((3, TILE, COLS), lambda j: (0, j + STEPS, 0)),
            pl.BlockSpec((TOK, COLS), lambda j: (0, 0)),
            pl.BlockSpec((TOK, wide_tile), lambda j: (0, j)),
            pl.BlockSpec((COLS, wide_tile), lambda j: (0, j)),
            pl.BlockSpec((TOK, TILE), lambda j: (0, j + STEPS)),
        ],
        out_specs=[
            pl.BlockSpec((TILE, TOK), lambda j: (j, 0)),
            pl.BlockSpec((3, TILE, COLS), lambda j: (0, j, 0)),
            pl.BlockSpec((COLS, wide_tile), lambda j: (0, j)),
        ],
        out_shape=[
            pltpu.HBM((HALF, TOK), bf16),
            pltpu.HBM((3, HALF, COLS), f32),
            pltpu.HBM((COLS, D), f32),
        ],
        cost_estimate=cost(9),
        compiler_params=pltpu.CompilerParams(vmem_limit_bytes=VMEM),
        name="ahead",
    )(*streamed(inputs, grads, err_in, hidden, grad_y, err_out, inputs))


def wide(block, rows):
    return jnp.concatenate([block[i * rows : (i + 1) * rows] for i in range(block.shape[0] // rows)], axis=1)


def answer_left_kernel(me_ref, received_ref, answer_ref):
    over_xy = []
    for z in range(4):
        total = received_ref[z]
        for i in range(1, N_DP):
            total += received_ref[4 * i + z]
        over_xy.append(total)
    total = (over_xy[0] + over_xy[1]) + (over_xy[2] + over_xy[3])
    row = me_ref[0] * EACH1 + lax.broadcasted_iota(jnp.int32, (EACH1, 128), 0)
    for z in range(4):
        answer = jnp.where(row >= L_ROWS, over_xy[z], total)
        for i in range(N_DP):
            answer_ref[4 * i + z] = answer


def answer_left(me, received):
    whole = pl.BlockSpec((CHIPS, EACH1, 128), lambda j, m: (0, 0, 0))
    return pl.pallas_call(
        answer_left_kernel,
        grid_spec=pltpu.PrefetchScalarGridSpec(num_scalar_prefetch=1, grid=(1,), in_specs=[whole], out_specs=whole),
        out_shape=jax.ShapeDtypeStruct((CHIPS, EACH1, 128), f32),
        cost_estimate=cost(2),
        compiler_params=pltpu.CompilerParams(vmem_limit_bytes=VMEM),
        name="answer_left",
    )(me, received)


def answer_right_kernel(received_ref, answer_ref):
    total = received_ref[0]
    for i in range(1, N_DP):
        total += received_ref[i]
    for i in range(N_DP):
        answer_ref[i] = total


def answer_right(received):
    return pl.pallas_call(
        answer_right_kernel,
        out_shape=jax.ShapeDtypeStruct((N_DP, EACH2, 128), f32),
        cost_estimate=cost(1),
        compiler_params=pltpu.CompilerParams(vmem_limit_bytes=VMEM),
        name="answer_right",
    )(received)


def right_out_kernel(place_ref, left_out_ref, hid_ref, gy_hbm, err_out_hbm, x_hbm, err_in_hbm, send_ref, keep_ref, x_out,
                     err_in_out, gy_scr, err_out_scr, sem, near_sem):
    def column(j):
        at = lax.rem(place_ref[0] + 1 + j // 4, 2) * 4 + lax.rem(place_ref[1] + j % 4, 4)
        return pl.ds(pl.multiple_of(at * COLS, COLS), COLS)

    copies = [
        (
            pltpu.make_async_copy(gy_hbm.at[:, column(j)], gy_scr.at[j], sem.at[0, j]),
            pltpu.make_async_copy(err_out_hbm.at[:, column(j)], err_out_scr.at[j], sem.at[1, j]),
        )
        for j in range(8)
    ]
    near = near_copies(place_ref[0], x_hbm, err_in_hbm, x_out, err_in_out, near_sem)
    for pair in copies + [near]:
        for copy in pair:
            copy.start()
    left_out = wide(left_out_ref[...], RANK)
    factor = stacked(left_out)
    both = jnp.concatenate([factor, stacked(folded(nt(factor, hid_ref[...])))], axis=1)
    send_ref[RO_ROWS:, :] = jnp.concatenate([exact_nt(left_out, left_out), jnp.zeros((RANK, RANK), f32)], axis=1)
    for j in range(0, 8, 2):
        for pair in copies[j : j + 2]:
            for copy in pair:
                copy.wait()
        err_out = jnp.concatenate([err_out_scr[j], err_out_scr[j + 1]], axis=1)
        gy = jnp.concatenate([gy_scr[j], gy_scr[j + 1]], axis=1)
        part = folded(nn(both, jnp.concatenate([err_out, gy], axis=0)))
        ref = send_ref if j < 4 else keep_ref
        for i, tile in enumerate(tiles_of(part)):
            at = (j % 4) * PIECE + i * RANK
            ref[at : at + RANK, :] = tile
    for copy in near:
        copy.wait()


def right_out(place, left_out_sum, grad_y, hidden, err_out, inputs, err_in):
    whole = pl.BlockSpec(memory_space=pltpu.VMEM)
    return pl.pallas_call(
        right_out_kernel,
        in_specs=[pl.BlockSpec(memory_space=pltpu.SMEM), whole, whole, ANY, ANY, ANY, ANY],
        out_specs=[whole, whole, ANY, ANY],
        out_shape=[
            jax.ShapeDtypeStruct((RO_ROWS + RANK, 128), f32),
            jax.ShapeDtypeStruct((RO_ROWS, 128), f32),
            pltpu.VMEM((TOK, HALF), bf16),
            pltpu.VMEM((3, HALF, COLS), bf16),
        ],
        scratch_shapes=[
            pltpu.VMEM((8, TOK, COLS), bf16),
            pltpu.VMEM((8, COLS, COLS), bf16),
            pltpu.SemaphoreType.DMA((2, 8)),
            pltpu.SemaphoreType.DMA((2, STEPS)),
        ],
        cost_estimate=cost(3),
        compiler_params=pltpu.CompilerParams(vmem_limit_bytes=VMEM),
        name="right_out",
    )(place, left_out_sum, hidden, *streamed(grad_y, err_out, inputs, err_in))


def right_tile(rows, x, err_in, rights):
    high, low = split2(rows)
    for p in range(3):
        mine = slice(RANK * p, RANK * (p + 1))
        rights[p] += folded(nn(jnp.concatenate([high[mine], low[mine]], axis=0), err_in[p]))
    return folded(nt(jnp.concatenate([high, low], axis=0), x))


def near_copies(half, x_hbm, err_in_hbm, x_out, err_in_out, sem):
    copies = []
    for j in range(STEPS):
        at = pl.ds(pl.multiple_of(half * HALF + j * TILE, TILE), TILE)
        to = slice(j * TILE, (j + 1) * TILE)
        copies.append(pltpu.make_async_copy(x_hbm.at[:, at], x_out.at[:, to], sem.at[0, j]))
        copies.append(pltpu.make_async_copy(err_in_hbm.at[:, at], err_in_out.at[:, to], sem.at[1, j]))
    return copies


def right_sums(left_ref, x_ref, err_in_ref, tokens, rights):
    for j in range(STEPS):
        mine = slice(j * TILE, (j + 1) * TILE)
        rows = wide(left_ref[L_STEP * j : L_STEP * (j + 1), :], 3 * RANK)
        tokens += right_tile(rows, x_ref[:, mine], err_in_ref.at[:, mine], rights)
    return tokens


def right_own_kernel(half_ref, own_ref, x_ref, err_in_ref, x_hbm, err_in_hbm, right_ref, token_ref, x_out, err_in_out, sem):
    copies = near_copies(half_ref[0], x_hbm, err_in_hbm, x_out, err_in_out, sem)
    for copy in copies:
        copy.start()
    rights = [jnp.zeros((RANK, COLS), f32)] * 3
    token_ref[...] = right_sums(own_ref, x_ref, err_in_ref, jnp.zeros((3 * RANK, TOK), f32), rights)
    for p in range(3):
        right_ref[p] = rights[p]
    for copy in copies:
        copy.wait()


def right_own(other_half, own, near_inputs, near_err_in, inputs, err_in):
    whole = pl.BlockSpec(memory_space=pltpu.VMEM)
    return pl.pallas_call(
        right_own_kernel,
        in_specs=[pl.BlockSpec(memory_space=pltpu.SMEM), whole, whole, whole, ANY, ANY],
        out_specs=[whole, whole, ANY, ANY],
        out_shape=[
            jax.ShapeDtypeStruct((3, RANK, COLS), f32),
            jax.ShapeDtypeStruct((3 * RANK, TOK), f32),
            pltpu.VMEM((TOK, HALF), bf16),
            pltpu.VMEM((3, HALF, COLS), bf16),
        ],
        scratch_shapes=[pltpu.SemaphoreType.DMA((2, STEPS))],
        cost_estimate=cost(3),
        compiler_params=pltpu.CompilerParams(vmem_limit_bytes=VMEM),
        name="right_own",
    )(other_half, own, *held(near_inputs, near_err_in), *streamed(inputs, err_in))


def right_other_kernel(other_ref, right_ref, token_ref, x_ref, err_in_ref, grads_ref, rows_ref):
    rights = [right_ref[p] for p in range(3)]
    tokens = right_sums(other_ref, x_ref, err_in_ref, token_ref[...], rights)
    for p in range(3):
        total = rights[p] + folded(nn(stacked(tokens[RANK * p : RANK * (p + 1)]), grads_ref[p]))
        for i, tile in enumerate(tiles_of(total)):
            at = (HEADS * p + i) * RANK
            rows_ref[at : at + RANK, :] = tile


def right_other(other, right_part, token_part, inputs, err_in, grads):
    return pl.pallas_call(
        right_other_kernel,
        out_shape=jax.ShapeDtypeStruct((RI_ROWS, 128), f32),
        cost_estimate=cost(4),
        compiler_params=pltpu.CompilerParams(vmem_limit_bytes=VMEM),
        name="right_other",
    )(other, right_part, token_part, *held(inputs, err_in), grads)


def join_kernel(right_ref, own_ref, first_ref, second_ref, third_ref, rows_ref, gram_ref):
    piece = (own_ref[...] + first_ref[...]) + (second_ref[...] + third_ref[...])
    rows_ref[:RI_ROWS, :] = right_ref[...]
    rows_ref[RI_ROWS:, :] = piece[:PIECE]
    gram_ref[...] = piece[PIECE:]


def join(*operands):
    return pl.pallas_call(
        join_kernel,
        out_shape=[jax.ShapeDtypeStruct((ROWS2, 128), f32), jax.ShapeDtypeStruct((RANK, 128), f32)],
        cost_estimate=cost(1),
        compiler_params=pltpu.CompilerParams(vmem_limit_bytes=VMEM),
        name="join",
    )(*operands)


def gram_kernel(own_ref, other_ref, gram_ref):
    gram = jnp.zeros((3 * RANK, 3 * RANK), f32)
    for ref in (own_ref, other_ref):
        for i in range(STEPS):
            rows = wide(ref[L_STEP * i : L_STEP * (i + 1), :], 3 * RANK)
            gram += exact_nt(rows, rows)
    gram_ref[...] = gram


def gram(own, other):
    return pl.pallas_call(
        gram_kernel,
        out_shape=jax.ShapeDtypeStruct((3 * RANK, 3 * RANK), f32),
        cost_estimate=cost(2),
        compiler_params=pltpu.CompilerParams(vmem_limit_bytes=VMEM),
        name="gram",
    )(own, other)


def invert_kernel(gram_in_ref, left_out_ref, gram_out_ref, inverse_ref, ortho_out_ref):
    eye = jnp.where(
        lax.broadcasted_iota(jnp.int32, (RANK, RANK), 0) == lax.broadcasted_iota(jnp.int32, (RANK, RANK), 1),
        1.0,
        0.0,
    )
    gram = gram_in_ref[...]
    for p in range(3):
        mine = slice(RANK * p, RANK * (p + 1))
        inverse_ref[p] = jnp.concatenate([gram[mine, mine], eye], axis=1)
    inverse_ref[3] = jnp.concatenate([gram_out_ref[:, :RANK], eye], axis=1)
    rows8 = lax.broadcasted_iota(jnp.int32, (1, 8, 1), 1)
    tiles = [inverse_ref[:, 8 * t : 8 * t + 8, :] for t in range(RANK // 8)]
    for j in range(RANK):
        top, at = divmod(j, 8)
        pivot_row = tiles[top][:, at : at + 1, :]
        scaled = pivot_row * (1.0 / pivot_row[:, :, j : j + 1])
        for t in range(top, RANK // 8):
            column = tiles[t][:, :, j : j + 1]
            if t == top:
                column = jnp.where(rows8 > at, column, 0.0)
            tiles[t] = tiles[t] - column * scaled
    work = jnp.concatenate(tiles, axis=1)
    lane = lax.broadcasted_iota(jnp.int32, (4, RANK, 128), 2)
    sub = lax.broadcasted_iota(jnp.int32, (4, RANK, 128), 1)
    diagonal = jnp.sum(jnp.where(lane == sub, work, 0.0), axis=2, keepdims=True)
    inverse = work * lax.rsqrt(diagonal)
    inverse_ref[...] = inverse
    ortho_out_ref[...] = thrice(inverse[3, :, RANK:], wide(left_out_ref[...], RANK))


def invert(gram_in, left_out_sum, gram_out):
    return pl.pallas_call(
        invert_kernel,
        out_shape=[
            jax.ShapeDtypeStruct((4, RANK, 128), f32),
            jax.ShapeDtypeStruct((RANK, COLS), f32),
        ],
        cost_estimate=cost(10),
        compiler_params=pltpu.CompilerParams(vmem_limit_bytes=VMEM),
        name="invert",
    )(gram_in, left_out_sum, gram_out)


def turn_kernel(half_ref, own_ref, other_ref, inverse_ref, ortho_ref):
    step = pl.program_id(0)

    def turn(ref):
        rows = wide(ref[...], 3 * RANK)
        for p in range(3):
            high, low = split2(thrice(inverse_ref[p, :, RANK:], rows[RANK * p : RANK * (p + 1)]))
            both = jnp.concatenate([high.astype(f32), low.astype(f32)], axis=0)
            ortho_ref[p] = both.T.astype(bf16)

    @pl.when(step < STEPS)
    def _():
        turn(own_ref)

    @pl.when(step >= STEPS)
    def _():
        turn(other_ref)


def turn(half, own, other, inverse):
    def column(j, h):
        return lax.rem(j // STEPS + h[0], 2) * STEPS + lax.rem(j, STEPS)

    return pl.pallas_call(
        turn_kernel,
        grid_spec=pltpu.PrefetchScalarGridSpec(
            num_scalar_prefetch=1,
            grid=(2 * STEPS,),
            in_specs=[
                pl.BlockSpec((CT * 3 * RANK, 128), lambda j, h: (jnp.minimum(j, STEPS - 1), 0)),
                pl.BlockSpec((CT * 3 * RANK, 128), lambda j, h: (jnp.maximum(j - STEPS, 0), 0)),
                pl.BlockSpec((4, RANK, 128), lambda j, h: (0, 0, 0)),
            ],
            out_specs=pl.BlockSpec((3, TILE, 128), lambda j, h: (0, column(j, h), 0)),
        ),
        out_shape=pltpu.HBM((3, D, 128), bf16),
        cost_estimate=cost(6),
        compiler_params=pltpu.CompilerParams(vmem_limit_bytes=VMEM),
        name="turn",
    )(half, own, other, inverse)


def rest_in_kernel(summed_in_ref, inverse_hbm, grads_hbm, turned_hbm, err_in_hbm, ortho_hbm, moment_hbm, rest_hbm,
                   factor_in_ref, inverse_scr, grads_scr, turned_scr, err_in_scr, ortho_scr, moment_scr, rest_scr, in_sem,
                   out_sem):
    def rows(j):
        return slice(TILE * j, TILE * (j + 1))

    tiles = range(2 * STEPS)
    first = [
        pltpu.make_async_copy(inverse_hbm, inverse_scr, in_sem.at[0, len(tiles)]),
        pltpu.make_async_copy(grads_hbm, grads_scr, in_sem.at[1, len(tiles)]),
    ]
    into = [[pltpu.make_async_copy(ortho_hbm.at[:, rows(j)], ortho_scr.at[j], in_sem.at[0, j])] for j in tiles]
    for j in range(STEPS):
        into[j].append(pltpu.make_async_copy(turned_hbm.at[rows(j)], turned_scr.at[j], in_sem.at[1, j]))
        into[j].append(pltpu.make_async_copy(err_in_hbm.at[:, rows(j)], err_in_scr.at[j], in_sem.at[2, j]))
        into[j + STEPS].append(
            pltpu.make_async_copy(moment_hbm.at[:, rows(j)], moment_scr.at[j], in_sem.at[1, j + STEPS])
        )
    out = [pltpu.make_async_copy(rest_scr.at[j], rest_hbm.at[:, rows(j)], out_sem.at[j]) for j in tiles]
    for copy in first:
        copy.start()
    order = [j + half for j in range(STEPS) for half in (0, STEPS)]
    for j in order:
        for copy in into[j]:
            copy.start()
    for copy in first:
        copy.wait()
    grads = jnp.concatenate([grads_scr[p] for p in range(3)], axis=1)
    weights = []
    for p in range(3):
        right = wide(summed_in_ref[HEADS * RANK * p : HEADS * RANK * (p + 1), :], RANK) * (1.0 / N_DP)
        factor = thrice(inverse_scr[p, :, RANK:], right)
        factor_in_ref[p] = factor
        high, low = split2(-factor)
        weights.append(jnp.concatenate([high, high, low, jnp.zeros_like(low)], axis=0))
    for j in order:
        for copy in into[j]:
            copy.wait()
        moments = nn(turned_scr[j], grads) if j < STEPS else None
        for p in range(3):
            if j < STEPS:
                moment = moments[:, COLS * p : COLS * (p + 1)] + err_in_scr[j, p].astype(f32)
            else:
                moment = moment_scr[j - STEPS, p]
            both = jnp.concatenate([ortho_scr[j, p], ortho_scr[j, p]], axis=1)
            rest_scr[j, p] = (moment + nn(both, weights[p])).astype(bf16)
        out[j].start()
    for copy in out:
        copy.wait()


def rest_in(summed, inverse, grads, turned, err_in, ortho_in, moment_in):
    whole = pl.BlockSpec(memory_space=pltpu.VMEM)
    tiles = 2 * STEPS
    return pl.pallas_call(
        rest_in_kernel,
        in_specs=[whole] + [ANY] * 6,
        out_specs=[ANY, whole],
        scratch_shapes=[
            pltpu.VMEM((4, RANK, 128), f32),
            pltpu.VMEM((3, TOK, COLS), bf16),
            pltpu.VMEM((STEPS, TILE, TOK), bf16),
            pltpu.VMEM((STEPS, 3, TILE, COLS), bf16),
            pltpu.VMEM((tiles, 3, TILE, 128), bf16),
            pltpu.VMEM((STEPS, 3, TILE, COLS), f32),
            pltpu.VMEM((tiles, 3, TILE, COLS), bf16),
            pltpu.SemaphoreType.DMA((3, tiles + 1)),
            pltpu.SemaphoreType.DMA((tiles,)),
        ],
        out_shape=[
            pltpu.HBM((3, D, COLS), bf16),
            jax.ShapeDtypeStruct((3, RANK, COLS), f32),
        ],
        cost_estimate=cost(9),
        compiler_params=pltpu.CompilerParams(vmem_limit_bytes=VMEM_LAST),
        name="rest_in",
    )(summed, *streamed(inverse, grads, turned, err_in, ortho_in, moment_in))


def rest_out_kernel(place_ref, *refs):
    piece_refs, (inverse_hbm, ortho_out_hbm, moment_hbm) = refs[:4], refs[4:7]
    rest_hbm, factor_hbm, inverse_scr, ortho_out_scr, moment_scr, rest_scr, factor_scr, first_sem, in_sem, out_sem = refs[7:]
    small = zip((inverse_hbm.at[3], ortho_out_hbm), (inverse_scr, ortho_out_scr))
    first = [pltpu.make_async_copy(a, b, first_sem.at[i]) for i, (a, b) in enumerate(small)]

    def column(j):
        at = lax.rem(place_ref[0] + j // 4, 2) * 4 + lax.rem(place_ref[1] + 4 - j % 4, 4)
        return pl.ds(pl.multiple_of(at * COLS, COLS), COLS)

    into = [pltpu.make_async_copy(moment_hbm.at[:, column(j)], moment_scr.at[j], in_sem.at[j]) for j in range(8)]
    out = [
        (
            pltpu.make_async_copy(rest_scr.at[j], rest_hbm.at[:, column(j)], out_sem.at[0, j]),
            pltpu.make_async_copy(factor_scr.at[j], factor_hbm.at[:, column(j)], out_sem.at[1, j]),
        )
        for j in range(8)
    ]
    for copy in first:
        copy.start()
    for copy in into:
        copy.start()
    for copy in first:
        copy.wait()
    high, low = split2(ortho_out_scr[...])
    stack = jnp.concatenate([high, high, low, jnp.zeros_like(low)], axis=0)
    both = stack.astype(f32).T.astype(bf16)
    inverse = inverse_scr[:, RANK:]
    for j in range(0, 8, 2):
        mine = slice(PIECE * (j // 4), PIECE * (j // 4 + 1))
        right = jnp.concatenate([wide(piece_refs[k % 4][mine, :], RANK) for k in (j, j + 1)], axis=1)
        factor = thrice(inverse, right * (1.0 / N_DP))
        high, low = split2(-factor)
        for k in (j, j + 1):
            into[k].wait()
        total = nn(both, jnp.concatenate([high, low, high, jnp.zeros_like(low)], axis=0))
        for i, k in enumerate((j, j + 1)):
            mine = slice(COLS * i, COLS * (i + 1))
            factor_scr[k] = factor[:, mine]
            rest_scr[k] = (total[:, mine] + moment_scr[k]).astype(bf16)
            for copy in out[k]:
                copy.start()
    for pair in out:
        for copy in pair:
            copy.wait()


def rest_out(place, pieces, inverse, ortho_out, moment_out):
    whole = pl.BlockSpec(memory_space=pltpu.VMEM)
    return pl.pallas_call(
        rest_out_kernel,
        in_specs=[pl.BlockSpec(memory_space=pltpu.SMEM)] + [whole] * 4 + [ANY] * 3,
        out_specs=[ANY, ANY],
        scratch_shapes=[
            pltpu.VMEM((RANK, 128), f32),
            pltpu.VMEM((RANK, COLS), f32),
            pltpu.VMEM((8, COLS, COLS), f32),
            pltpu.VMEM((8, COLS, COLS), bf16),
            pltpu.VMEM((8, RANK, COLS), f32),
            pltpu.SemaphoreType.DMA((2,)),
            pltpu.SemaphoreType.DMA((8,)),
            pltpu.SemaphoreType.DMA((2, 8)),
        ],
        out_shape=[pltpu.HBM((COLS, D), bf16), pltpu.HBM((RANK, D), f32)],
        cost_estimate=cost(6),
        compiler_params=pltpu.CompilerParams(vmem_limit_bytes=VMEM),
        name="rest_out",
    )(place, *pieces, *streamed(inverse, ortho_out, moment_out))


CHIP = ("x", "y", "z")
SWAP = [(0, 1), (1, 0)]
OTHERS = (2, 1, 3)


def ring(shift):
    return [(a, (a + shift) % 4) for a in range(4)]


def shards(inputs, grad_y, q_pre, f_pre, v_pre, w_out, err_in, err_out, basis_in, basis_out):
    keep = (err_in[0], err_out[0], inputs, grad_y)
    core = lax.axis_index("c").astype(jnp.int32)
    z = lax.axis_index("z").astype(jnp.int32)
    me = (lax.axis_index("x") * 4 + lax.axis_index("y")).astype(jnp.int32) * 4 + z
    mine = core[None]
    theirs = 1 - mine
    place = jnp.stack([core, z])
    q_pre, place, mine, theirs, me = lax.optimization_barrier((q_pre, place, mine, theirs, me[None]))
    hidden, grads, near_err_in, near_err_out, near_inputs, near_grad_y = recurrence(
        grad_y, w_out, q_pre, f_pre, v_pre, keep
    )
    err_in, err_out = keep[:2]
    send = left(theirs, near_inputs, grads, near_err_in, basis_in)
    arrived = lax.ppermute(send, "c", SWAP)
    left_out_part = left_out(near_grad_y, hidden, near_err_out, basis_out)
    rows = left(mine, near_inputs, grads, near_err_in, basis_in, arrived, left_out_part)

    rows, hidden_now = lax.optimization_barrier((rows, hidden))
    received = lax.all_to_all(rows.reshape(CHIPS, EACH1, 128), CHIP, 0, 0)
    inputs_turned, moment_in, moment_out = ahead(inputs, grads, err_in, hidden_now, grad_y, err_out)
    received, inputs_turned = lax.optimization_barrier((received, inputs_turned))
    own = lax.all_to_all(answer_left(me, received), CHIP, 0, 0).reshape(ROWS1, 128)
    other = lax.ppermute(own, "c", SWAP)
    left_out_sum = own[L_ROWS : L_ROWS + LO_ROWS]

    send, keep_out, near_inputs, near_err_in = right_out(
        place, left_out_sum, grad_y, hidden, err_out, inputs, err_in
    )
    arrived = lax.ppermute(send, "c", SWAP)
    gram_in = gram(own, other)
    arrived, gram_in, near_inputs = lax.optimization_barrier((arrived, gram_in, near_inputs))
    gram_out = send[RO_ROWS:] + arrived[RO_ROWS:]
    quarters = (keep_out + arrived[:RO_ROWS]).reshape(4, PIECE, 128)
    pieces = [jnp.concatenate([quarters[shift], gram_out]) for shift in range(4)]
    pieces = [pieces[0]] + [lax.ppermute(pieces[shift], "z", ring(shift)) for shift in OTHERS]
    right_part = right_own(theirs, own, near_inputs, near_err_in, inputs, err_in)
    rows, gram_out = join(right_other(other, *right_part, grads), *pieces)

    received = lax.all_to_all(rows.reshape(N_DP, EACH2, 128), ("x", "y"), 0, 0)
    inverse, ortho_out = invert(gram_in, left_out_sum, gram_out)
    received, inverse, ortho_out = lax.optimization_barrier((received, inverse, ortho_out))
    everywhere = answer_right(received)
    everywhere, inverse = lax.optimization_barrier((everywhere, inverse))
    summed = lax.all_to_all(everywhere, ("x", "y"), 0, 0).reshape(ROWS2, 128)
    ortho_in = turn(mine, own, other, inverse)
    summed, ortho_in = lax.optimization_barrier((summed, ortho_in))

    piece = summed[RI_ROWS:]
    pieces = [jnp.concatenate([piece, lax.ppermute(piece, "c", SWAP)])]
    pieces += [lax.ppermute(pieces[0], "z", ring(shift)) for shift in (1, 2, 3)]
    new_in, factor_in = rest_in(summed, inverse, grads, inputs_turned, err_in, ortho_in, moment_in)
    new_out, factor_out = rest_out(place, pieces, inverse, ortho_out, moment_out)
    return new_in[None], new_out[None], factor_in, factor_out


def solution(mesh):
    fine = Mesh(mesh.devices.reshape(4, 4, 4, 2), ("x", "y", "z", "c"))
    dp, head = ("x", "y"), ("z", "c")
    placed = (
        P(dp, None),
        P(dp, None),
        P(dp, head),
        P(dp, head),
        P(dp, head),
        P(head, None),
        P(dp, None, None, head),
        P(dp, head, None),
        P(None, None, head),
        P(),
    )
    return jax.shard_map(
        shards,
        mesh=fine,
        in_specs=placed,
        out_specs=(P(dp, None, None, head), P(dp, head, None), P(None, None, head), P()),
        check_vma=False,
    )
```

```python
import functools

import jax
import jax.numpy as jnp
from jax import lax
from jax.experimental import pallas as pl
from jax.experimental.pallas import tpu as pltpu
from jax.sharding import Mesh, PartitionSpec as P

TOK = 256
DK = 128
HEADS = 3
COLS = HEADS * DK
RANK = 64
D = 3072
HALF = D // 2
TILE = 512
STEPS = HALF // TILE
CT = TILE // 128
N_DP = 16
CHIPS = 64
L_ROWS = 12 * 3 * RANK
LO_ROWS = HEADS * RANK
ROWS1 = 2560
EACH1 = 40
L_STEP = CT * 3 * RANK
RI_ROWS = 9 * RANK
RO_ROWS = 12 * RANK
ROWS2 = 768
EACH2 = 48
PIECE = HEADS * RANK
GRAM_ROWS = RANK // 2

f32 = jnp.float32
bf16 = jnp.bfloat16
EXACT = lax.Precision.HIGHEST
VMEM = 24 * 1024 * 1024
VMEM_LAST = 40 * 1024 * 1024


def cost(us):
    return pl.CostEstimate(flops=int(us * 1e9), bytes_accessed=int(us * 3e6), transcendentals=0)


def nn(a, b):
    return lax.dot_general(a, b, (((1,), (0,)), ((), ())), preferred_element_type=f32)


def nt(a, b):
    return lax.dot_general(a, b, (((1,), (1,)), ((), ())), preferred_element_type=f32)


def tn(a, b):
    return lax.dot_general(a, b, (((0,), (0,)), ((), ())), preferred_element_type=f32)


def exact_nt(a, b):
    return lax.dot_general(a, b, (((1,), (1,)), ((), ())), precision=EXACT, preferred_element_type=f32)


def split2(a):
    high = a.astype(bf16)
    return high, (a - high.astype(f32)).astype(bf16)


def thrice(a, b):
    a_high, a_low = split2(a)
    b_high, b_low = split2(b)
    return nn(jnp.concatenate([a_high, a_high, a_low], axis=1), jnp.concatenate([b_high, b_low, b_high], axis=0))


def split3(a):
    high = a.astype(bf16)
    rest = a - high.astype(f32)
    mid = rest.astype(bf16)
    return high, mid, (rest - mid.astype(f32)).astype(bf16)


def summed3(ones, a):
    parts = nn(ones, jnp.concatenate(split3(a), axis=1))
    width = a.shape[1]
    return parts[:, :width] + (parts[:, width : 2 * width] + parts[:, 2 * width :])


def stacked(a):
    return jnp.concatenate(split2(a), axis=0)


def folded(a):
    half = a.shape[0] // 2
    return a[:half] + a[half:]


def head_forward(q, f):
    q_gate = 1.0 / (1.0 + jnp.exp(-q))
    query = q * q_gate
    small = jnp.exp(-jnp.abs(f))
    key = jnp.where(f >= 0, small, 1.0) / (1.0 + small)
    decay = jnp.where(f >= 0, 1.0, small) / (1.0 + small)
    log_decay = jnp.minimum(f, 0.0) - jnp.log1p(small)
    row = lax.broadcasted_iota(jnp.int32, (TOK, TOK), 0)
    col = lax.broadcasted_iota(jnp.int32, (TOK, TOK), 1)
    running = summed3(jnp.where(row >= col, 1.0, 0.0).astype(bf16), log_decay)
    differ = row ^ col
    scores = jnp.zeros((TOK, TOK), f32)
    levels = []
    for size in (128, 64, 32, 16, 8):
        blocks = running.reshape(TOK // (2 * size), 2 * size, DK)
        spread = (blocks - blocks[:, size - 1 : size, :]).reshape(TOK, DK)
        if size > 8:
            q_scale = jnp.exp(jnp.minimum(spread, 0.0))
            k_scale = jnp.exp(jnp.minimum(-spread, 0.0))
            mask = (differ >= size) & (differ < 2 * size) & (row > col)
        else:
            q_scale = jnp.exp(spread)
            k_scale = jnp.exp(-spread)
            mask = (differ < 2 * size) & (row >= col)
        q_high, q_low = split2(query * q_scale)
        k_high, k_low = split2(key * k_scale)
        level = nt(
            jnp.concatenate([q_high, q_high, q_low], axis=1),
            jnp.concatenate([k_high, k_low, k_high], axis=1),
        )
        scores = jnp.where(mask, level, scores)
        levels.append((q_scale, k_scale, q_high, q_low, k_high, k_low))
    return (query, key, decay, q_gate), levels, split2(scores)


def head_backward(gates, levels, scores, v, grad_o):
    query, key, decay, q_gate = gates
    row = lax.broadcasted_iota(jnp.int32, (TOK, TOK), 0)
    col = lax.broadcasted_iota(jnp.int32, (TOK, TOK), 1)
    differ = row ^ col
    grad_s = split2(nt(grad_o, v))
    grad_st = split2(nt(v, grad_o))
    grad_query = jnp.zeros((TOK, DK), f32)
    grad_key = jnp.zeros((TOK, DK), f32)
    for size, (q_scale, k_scale, q_high, q_low, k_high, k_low) in zip((128, 64, 32, 16, 8), levels):
        if size > 8:
            within = (differ >= size) & (differ < 2 * size)
            mask, mask_t = within & (row > col), within & (row < col)
        else:
            within = differ < 2 * size
            mask, mask_t = within & (row >= col), within & (row <= col)
        keep = jnp.where(mask, 1.0, 0.0).astype(bf16)
        keep_t = jnp.where(mask_t, 1.0, 0.0).astype(bf16)
        both = nn(grad_s[0] * keep, jnp.concatenate([k_high, k_low], axis=1))
        grad_query += q_scale * (both[:, :DK] + both[:, DK:] + nn(grad_s[1] * keep, k_high))
        both = nn(grad_st[0] * keep_t, jnp.concatenate([q_high, q_low], axis=1))
        grad_key += k_scale * (both[:, :DK] + both[:, DK:] + nn(grad_st[1] * keep_t, q_high))
    grad_v = tn(scores[0], grad_o) + tn(scores[1], grad_o)
    upper = jnp.where(row <= col, 1.0, 0.0).astype(bf16)
    grad_decay = summed3(upper, query * grad_query - key * grad_key)
    grad_q = grad_query * (q_gate + query * (1.0 - q_gate))
    return grad_q, key * (grad_decay - grad_key * decay), grad_v


def recurrence_kernel(q_hbm, f_hbm, v_hbm, gy_hbm, w_hbm, *refs):
    sources, (hid_ref, grad_ref), kept, (q_scr, f_scr, v_scr, gy_scr, w_scr, sem) = (
        refs[:4],
        refs[4:6],
        refs[6:10],
        refs[10:],
    )
    pairs = list(zip((q_hbm, f_hbm, v_hbm, gy_hbm, w_hbm), (q_scr, f_scr, v_scr, gy_scr, w_scr)))
    copies = [pltpu.make_async_copy(a, b, sem.at[i]) for i, (a, b) in enumerate(pairs + list(zip(sources, kept)))]
    for copy in copies:
        copy.start()
    for copy in copies[:3]:
        copy.wait()
    for h in range(HEADS):
        mine = slice(DK * h, DK * (h + 1))
        gates, levels, scores = head_forward(q_scr[:, mine].astype(f32), f_scr[:, mine].astype(f32))
        v = v_scr[:, mine]
        hid_ref[:, mine] = (nn(scores[0], v) + nn(scores[1], v)).astype(bf16)
        if h == 0:
            for copy in copies[3:5]:
                copy.wait()
            grad_o = nt(gy_scr[...], w_scr[...]).astype(bf16)
        for p, grad in enumerate(head_backward(gates, levels, scores, v, grad_o[:, mine])):
            grad_ref[p, :, mine] = grad.astype(bf16)
    for copy in copies[5:]:
        copy.wait()


def held(*arrays):
    return [pltpu.with_memory_space_constraint(a, pltpu.VMEM) for a in arrays]


def streamed(*arrays):
    return [pltpu.with_memory_space_constraint(a, pltpu.HBM) for a in arrays]


ANY = pl.BlockSpec(memory_space=pl.ANY)


def fetched(step, steps, column, width, sources, slots, sem):
    def copies(j):
        at = pl.ds(pl.multiple_of(column(j) * width, width), width)
        for i, (axis, source) in enumerate(sources):
            index = [slice(None)] * len(source.shape)
            index[axis] = at
            yield pltpu.make_async_copy(source.at[tuple(index)], slots[i].at[j], sem.at[i, j])

    @pl.when(step == 0)
    def _():
        for j in range(steps):
            for copy in copies(j):
                copy.start()

    for copy in copies(step):
        copy.wait()
    return [slot.at[step] for slot in slots]


def recurrence(grad_y, w_out, q_pre, f_pre, v_pre, keep):
    operands = (q_pre, f_pre, v_pre, grad_y, w_out) + keep
    whole = pl.BlockSpec(memory_space=pltpu.VMEM)
    return pl.pallas_call(
        recurrence_kernel,
        in_specs=[ANY] * len(operands),
        out_specs=[whole] * 2 + [ANY] * len(keep),
        out_shape=[
            jax.ShapeDtypeStruct((TOK, COLS), bf16),
            jax.ShapeDtypeStruct((3, TOK, COLS), bf16),
        ]
        + [pltpu.VMEM(a.shape, a.dtype) for a in keep],
        scratch_shapes=[pltpu.VMEM(a.shape, a.dtype) for a in operands[:5]]
        + [pltpu.SemaphoreType.DMA((len(operands),))],
        cost_estimate=cost(8),
        compiler_params=pltpu.CompilerParams(vmem_limit_bytes=VMEM),
        name="recurrence",
    )(*streamed(*operands))


def tiles_of(a):
    return [a[:, 128 * i : 128 * (i + 1)] for i in range(a.shape[1] // 128)]


def left_tiles(half_ref, x_ref, grads_ref, err_in_ref, basis_in_ref):
    bases = [stacked(basis_in_ref[p]) for p in range(3)]
    tokens = jnp.concatenate([stacked(folded(nt(bases[p], grads_ref[p]))) for p in range(3)], axis=0)
    for step in range(STEPS):
        at = pl.ds(pl.multiple_of(half_ref[0] * HALF + step * TILE, TILE), TILE)
        from_tokens = nn(tokens, x_ref[:, at])
        for p in range(3):
            part = from_tokens[2 * RANK * p : 2 * RANK * (p + 1)] + nt(bases[p], err_in_ref[p, at, :])
            for i, tile in enumerate(tiles_of(folded(part))):
                yield step * L_STEP + (3 * i + p) * RANK, tile


def left_send_kernel(half_ref, x_ref, grads_ref, err_in_ref, basis_in_ref, left_ref):
    for at, tile in left_tiles(half_ref, x_ref, grads_ref, err_in_ref, basis_in_ref):
        left_ref[at : at + RANK, :] = tile


def left_keep_kernel(half_ref, x_ref, grads_ref, err_in_ref, basis_in_ref, arrived_ref, left_out_ref, rows_hbm, rows_scr, sem):
    parts = [slice(L_STEP * step, L_STEP * (step + 1)) for step in range(STEPS)] + [slice(L_ROWS, ROWS1)]
    copies = [pltpu.make_async_copy(rows_scr.at[part], rows_hbm.at[part], sem.at[i]) for i, part in enumerate(parts)]
    rows_scr[L_ROWS : L_ROWS + LO_ROWS, :] = left_out_ref[...]
    rows_scr[L_ROWS + LO_ROWS :, :] = jnp.zeros((ROWS1 - L_ROWS - LO_ROWS, 128), f32)
    copies[STEPS].start()
    for i, (at, tile) in enumerate(left_tiles(half_ref, x_ref, grads_ref, err_in_ref, basis_in_ref)):
        rows_scr[at : at + RANK, :] = tile + arrived_ref[at : at + RANK, :]
        if (i + 1) % (3 * CT) == 0:
            copies[i // (3 * CT)].start()
    for copy in copies:
        copy.wait()


def left(half, inputs, grads, err_in, basis_in, *arrived):
    keep = {}
    if arrived:
        keep = dict(
            out_specs=ANY, scratch_shapes=[pltpu.VMEM((ROWS1, 128), f32), pltpu.SemaphoreType.DMA((STEPS + 1,))]
        )
    return pl.pallas_call(
        left_keep_kernel if arrived else left_send_kernel,
        in_specs=[pl.BlockSpec(memory_space=pltpu.SMEM)] + [pl.BlockSpec(memory_space=pltpu.VMEM)] * (4 + len(arrived)),
        out_shape=pltpu.HBM((ROWS1, 128), f32) if arrived else jax.ShapeDtypeStruct((L_ROWS, 128), f32),
        cost_estimate=cost(3),
        compiler_params=pltpu.CompilerParams(vmem_limit_bytes=VMEM),
        name="left_keep" if arrived else "left_send",
        **keep,
    )(half, *held(inputs), grads, *held(err_in), basis_in, *arrived)


def left_out_kernel(gy_ref, hid_ref, err_out_ref, basis_out_ref, left_out_ref):
    basis = stacked(basis_out_ref[...])
    tokens = stacked(folded(nt(basis, gy_ref[...])))
    part = folded(nt(basis, err_out_ref[...]) + nn(tokens, hid_ref[...]))
    for i, tile in enumerate(tiles_of(part)):
        left_out_ref[RANK * i : RANK * (i + 1), :] = tile


def left_out(grad_y, hidden, err_out, basis_out):
    return pl.pallas_call(
        left_out_kernel,
        out_shape=jax.ShapeDtypeStruct((LO_ROWS, 128), f32),
        cost_estimate=cost(4),
        compiler_params=pltpu.CompilerParams(vmem_limit_bytes=VMEM),
        name="left_out",
    )(*held(grad_y), hidden, *held(err_out), basis_out)


def ahead_kernel(x_ref, grads_ref, err_in_ref, hid_ref, gy_ref, err_out_ref, x_later_ref, turned_ref, moment_in_ref,
                 moment_out_ref):
    turned_ref[...] = x_ref[...].astype(f32).T.astype(bf16)
    later = x_later_ref[...].astype(f32).T.astype(bf16)
    moments = nn(later, jnp.concatenate([grads_ref[p] for p in range(3)], axis=1))
    for p in range(3):
        moment_in_ref[p] = moments[:, COLS * p : COLS * (p + 1)] + err_in_ref[p].astype(f32)
    moment_out_ref[...] = tn(hid_ref[...], gy_ref[...]) + err_out_ref[...].astype(f32)


def ahead(inputs, grads, err_in, hidden, grad_y, err_out):
    wide_tile = D // STEPS
    return pl.pallas_call(
        ahead_kernel,
        grid=(STEPS,),
        in_specs=[
            pl.BlockSpec((TOK, TILE), lambda j: (0, j)),
            pl.BlockSpec((3, TOK, COLS), lambda j: (0, 0, 0)),
            pl.BlockSpec((3, TILE, COLS), lambda j: (0, j + STEPS, 0)),
            pl.BlockSpec((TOK, COLS), lambda j: (0, 0)),
            pl.BlockSpec((TOK, wide_tile), lambda j: (0, j)),
            pl.BlockSpec((COLS, wide_tile), lambda j: (0, j)),
            pl.BlockSpec((TOK, TILE), lambda j: (0, j + STEPS)),
        ],
        out_specs=[
            pl.BlockSpec((TILE, TOK), lambda j: (j, 0)),
            pl.BlockSpec((3, TILE, COLS), lambda j: (0, j, 0)),
            pl.BlockSpec((COLS, wide_tile), lambda j: (0, j)),
        ],
        out_shape=[
            pltpu.HBM((HALF, TOK), bf16),
            pltpu.HBM((3, HALF, COLS), f32),
            pltpu.HBM((COLS, D), f32),
        ],
        cost_estimate=cost(9),
        compiler_params=pltpu.CompilerParams(vmem_limit_bytes=VMEM),
        name="ahead",
    )(*streamed(inputs, grads, err_in, hidden, grad_y, err_out, inputs))


def wide(block, rows):
    return jnp.concatenate([block[i * rows : (i + 1) * rows] for i in range(block.shape[0] // rows)], axis=1)


def answer_left_kernel(me_ref, received_ref, answer_ref):
    over_xy = []
    for z in range(4):
        total = received_ref[z]
        for i in range(1, N_DP):
            total += received_ref[4 * i + z]
        over_xy.append(total)
    total = (over_xy[0] + over_xy[1]) + (over_xy[2] + over_xy[3])
    row = me_ref[0] * EACH1 + lax.broadcasted_iota(jnp.int32, (EACH1, 128), 0)
    for z in range(4):
        answer = jnp.where(row >= L_ROWS, over_xy[z], total)
        for i in range(N_DP):
            answer_ref[4 * i + z] = answer


def answer_left(me, received):
    whole = pl.BlockSpec((CHIPS, EACH1, 128), lambda j, m: (0, 0, 0))
    return pl.pallas_call(
        answer_left_kernel,
        grid_spec=pltpu.PrefetchScalarGridSpec(num_scalar_prefetch=1, grid=(1,), in_specs=[whole], out_specs=whole),
        out_shape=jax.ShapeDtypeStruct((CHIPS, EACH1, 128), f32),
        cost_estimate=cost(2),
        compiler_params=pltpu.CompilerParams(vmem_limit_bytes=VMEM),
        name="answer_left",
    )(me, received)


def answer_right_kernel(received_ref, answer_ref):
    total = received_ref[0]
    for i in range(1, N_DP):
        total += received_ref[i]
    for i in range(N_DP):
        answer_ref[i] = total


def answer_right(received):
    return pl.pallas_call(
        answer_right_kernel,
        out_shape=jax.ShapeDtypeStruct((N_DP, EACH2, 128), f32),
        cost_estimate=cost(1),
        compiler_params=pltpu.CompilerParams(vmem_limit_bytes=VMEM),
        name="answer_right",
    )(received)


def right_out_kernel(place_ref, left_out_ref, hid_ref, gy_hbm, err_out_hbm, x_hbm, err_in_hbm, send_ref, keep_ref, x_out,
                     err_in_out, gy_scr, err_out_scr, sem, near_sem):
    def column(j):
        at = lax.rem(place_ref[0] + 1 + j // 4, 2) * 4 + lax.rem(place_ref[1] + j % 4, 4)
        return pl.ds(pl.multiple_of(at * COLS, COLS), COLS)

    copies = [
        (
            pltpu.make_async_copy(gy_hbm.at[:, column(j)], gy_scr.at[j], sem.at[0, j]),
            pltpu.make_async_copy(err_out_hbm.at[:, column(j)], err_out_scr.at[j], sem.at[1, j]),
        )
        for j in range(8)
    ]
    near = near_copies(place_ref[0], x_hbm, err_in_hbm, x_out, err_in_out, near_sem)
    for pair in copies + [near]:
        for copy in pair:
            copy.start()
    left_out = wide(left_out_ref[...], RANK)
    factor = stacked(left_out)
    both = jnp.concatenate([factor, stacked(folded(nt(factor, hid_ref[...])))], axis=1)
    gram = exact_nt(left_out, left_out)
    send_ref[RO_ROWS:, :] = jnp.concatenate([gram[:GRAM_ROWS], gram[GRAM_ROWS:]], axis=1)
    for j in range(0, 8, 2):
        for pair in copies[j : j + 2]:
            for copy in pair:
                copy.wait()
        err_out = jnp.concatenate([err_out_scr[j], err_out_scr[j + 1]], axis=1)
        gy = jnp.concatenate([gy_scr[j], gy_scr[j + 1]], axis=1)
        part = folded(nn(both, jnp.concatenate([err_out, gy], axis=0)))
        ref = send_ref if j < 4 else keep_ref
        for i, tile in enumerate(tiles_of(part)):
            at = (j % 4) * PIECE + i * RANK
            ref[at : at + RANK, :] = tile
    for copy in near:
        copy.wait()


def right_out(place, left_out_sum, grad_y, hidden, err_out, inputs, err_in):
    whole = pl.BlockSpec(memory_space=pltpu.VMEM)
    return pl.pallas_call(
        right_out_kernel,
        in_specs=[pl.BlockSpec(memory_space=pltpu.SMEM), whole, whole, ANY, ANY, ANY, ANY],
        out_specs=[whole, whole, ANY, ANY],
        out_shape=[
            jax.ShapeDtypeStruct((RO_ROWS + GRAM_ROWS, 128), f32),
            jax.ShapeDtypeStruct((RO_ROWS, 128), f32),
            pltpu.VMEM((TOK, HALF), bf16),
            pltpu.VMEM((3, HALF, COLS), bf16),
        ],
        scratch_shapes=[
            pltpu.VMEM((8, TOK, COLS), bf16),
            pltpu.VMEM((8, COLS, COLS), bf16),
            pltpu.SemaphoreType.DMA((2, 8)),
            pltpu.SemaphoreType.DMA((2, STEPS)),
        ],
        cost_estimate=cost(3),
        compiler_params=pltpu.CompilerParams(vmem_limit_bytes=VMEM),
        name="right_out",
    )(place, left_out_sum, hidden, *streamed(grad_y, err_out, inputs, err_in))


def right_tile(rows, x, err_in, rights):
    high, low = split2(rows)
    for p in range(3):
        mine = slice(RANK * p, RANK * (p + 1))
        rights[p] += folded(nn(jnp.concatenate([high[mine], low[mine]], axis=0), err_in[p]))
    return folded(nt(jnp.concatenate([high, low], axis=0), x))


def near_copies(half, x_hbm, err_in_hbm, x_out, err_in_out, sem):
    copies = []
    for j in range(STEPS):
        at = pl.ds(pl.multiple_of(half * HALF + j * TILE, TILE), TILE)
        to = slice(j * TILE, (j + 1) * TILE)
        copies.append(pltpu.make_async_copy(x_hbm.at[:, at], x_out.at[:, to], sem.at[0, j]))
        copies.append(pltpu.make_async_copy(err_in_hbm.at[:, at], err_in_out.at[:, to], sem.at[1, j]))
    return copies


def right_sums(left_ref, x_ref, err_in_ref, tokens, rights):
    for j in range(STEPS):
        mine = slice(j * TILE, (j + 1) * TILE)
        rows = wide(left_ref[L_STEP * j : L_STEP * (j + 1), :], 3 * RANK)
        tokens += right_tile(rows, x_ref[:, mine], err_in_ref.at[:, mine], rights)
    return tokens


def right_own_kernel(half_ref, own_ref, x_ref, err_in_ref, x_hbm, err_in_hbm, right_ref, token_ref, x_out, err_in_out, sem):
    copies = near_copies(half_ref[0], x_hbm, err_in_hbm, x_out, err_in_out, sem)
    for copy in copies:
        copy.start()
    rights = [jnp.zeros((RANK, COLS), f32)] * 3
    token_ref[...] = right_sums(own_ref, x_ref, err_in_ref, jnp.zeros((3 * RANK, TOK), f32), rights)
    for p in range(3):
        right_ref[p] = rights[p]
    for copy in copies:
        copy.wait()


def right_own(other_half, own, near_inputs, near_err_in, inputs, err_in):
    whole = pl.BlockSpec(memory_space=pltpu.VMEM)
    return pl.pallas_call(
        right_own_kernel,
        in_specs=[pl.BlockSpec(memory_space=pltpu.SMEM), whole, whole, whole, ANY, ANY],
        out_specs=[whole, whole, ANY, ANY],
        out_shape=[
            jax.ShapeDtypeStruct((3, RANK, COLS), f32),
            jax.ShapeDtypeStruct((3 * RANK, TOK), f32),
            pltpu.VMEM((TOK, HALF), bf16),
            pltpu.VMEM((3, HALF, COLS), bf16),
        ],
        scratch_shapes=[pltpu.SemaphoreType.DMA((2, STEPS))],
        cost_estimate=cost(3),
        compiler_params=pltpu.CompilerParams(vmem_limit_bytes=VMEM),
        name="right_own",
    )(other_half, own, *held(near_inputs, near_err_in), *streamed(inputs, err_in))


def right_other_kernel(other_ref, right_ref, token_ref, x_ref, err_in_ref, grads_ref, rows_ref):
    rights = [right_ref[p] for p in range(3)]
    tokens = right_sums(other_ref, x_ref, err_in_ref, token_ref[...], rights)
    for p in range(3):
        total = rights[p] + folded(nn(stacked(tokens[RANK * p : RANK * (p + 1)]), grads_ref[p]))
        for i, tile in enumerate(tiles_of(total)):
            at = (HEADS * p + i) * RANK
            rows_ref[at : at + RANK, :] = tile


def right_other(other, right_part, token_part, inputs, err_in, grads):
    return pl.pallas_call(
        right_other_kernel,
        out_shape=jax.ShapeDtypeStruct((RI_ROWS, 128), f32),
        cost_estimate=cost(4),
        compiler_params=pltpu.CompilerParams(vmem_limit_bytes=VMEM),
        name="right_other",
    )(other, right_part, token_part, *held(inputs, err_in), grads)


def join_kernel(right_ref, own_ref, first_ref, second_ref, third_ref, rows_ref, gram_ref):
    piece = (own_ref[...] + first_ref[...]) + (second_ref[...] + third_ref[...])
    rows_ref[:RI_ROWS, :] = right_ref[...]
    rows_ref[RI_ROWS:, :] = piece[:PIECE]
    gram_ref[...] = piece[PIECE:]


def join(*operands):
    return pl.pallas_call(
        join_kernel,
        out_shape=[jax.ShapeDtypeStruct((ROWS2, 128), f32), jax.ShapeDtypeStruct((GRAM_ROWS, 128), f32)],
        cost_estimate=cost(1),
        compiler_params=pltpu.CompilerParams(vmem_limit_bytes=VMEM),
        name="join",
    )(*operands)


def gram_kernel(own_ref, other_ref, gram_ref):
    gram = jnp.zeros((3 * RANK, 3 * RANK), f32)
    for ref in (own_ref, other_ref):
        for i in range(STEPS):
            rows = wide(ref[L_STEP * i : L_STEP * (i + 1), :], 3 * RANK)
            gram += exact_nt(rows, rows)
    gram_ref[...] = gram


def gram(own, other):
    return pl.pallas_call(
        gram_kernel,
        out_shape=jax.ShapeDtypeStruct((3 * RANK, 3 * RANK), f32),
        cost_estimate=cost(2),
        compiler_params=pltpu.CompilerParams(vmem_limit_bytes=VMEM),
        name="gram",
    )(own, other)


def invert_kernel(gram_in_ref, left_out_ref, gram_out_ref, inverse_ref, ortho_out_ref):
    eye = jnp.where(
        lax.broadcasted_iota(jnp.int32, (RANK, RANK), 0) == lax.broadcasted_iota(jnp.int32, (RANK, RANK), 1),
        1.0,
        0.0,
    )
    gram = gram_in_ref[...]
    for p in range(3):
        mine = slice(RANK * p, RANK * (p + 1))
        inverse_ref[p] = jnp.concatenate([gram[mine, mine], eye], axis=1)
    gram_out = jnp.concatenate([gram_out_ref[:, :RANK], gram_out_ref[:, RANK:]], axis=0)
    inverse_ref[3] = jnp.concatenate([gram_out, eye], axis=1)
    rows8 = lax.broadcasted_iota(jnp.int32, (1, 8, 1), 1)
    tiles = [inverse_ref[:, 8 * t : 8 * t + 8, :] for t in range(RANK // 8)]
    for j in range(RANK):
        top, at = divmod(j, 8)
        pivot_row = tiles[top][:, at : at + 1, :]
        scaled = pivot_row * (1.0 / pivot_row[:, :, j : j + 1])
        for t in range(top, RANK // 8):
            column = tiles[t][:, :, j : j + 1]
            if t == top:
                column = jnp.where(rows8 > at, column, 0.0)
            tiles[t] = tiles[t] - column * scaled
    work = jnp.concatenate(tiles, axis=1)
    lane = lax.broadcasted_iota(jnp.int32, (4, RANK, 128), 2)
    sub = lax.broadcasted_iota(jnp.int32, (4, RANK, 128), 1)
    diagonal = jnp.sum(jnp.where(lane == sub, work, 0.0), axis=2, keepdims=True)
    inverse = work * lax.rsqrt(diagonal)
    inverse_ref[...] = inverse
    ortho_out_ref[...] = thrice(inverse[3, :, RANK:], wide(left_out_ref[...], RANK))


def invert(gram_in, left_out_sum, gram_out):
    return pl.pallas_call(
        invert_kernel,
        out_shape=[
            jax.ShapeDtypeStruct((4, RANK, 128), f32),
            jax.ShapeDtypeStruct((RANK, COLS), f32),
        ],
        cost_estimate=cost(10),
        compiler_params=pltpu.CompilerParams(vmem_limit_bytes=VMEM),
        name="invert",
    )(gram_in, left_out_sum, gram_out)


def turn_kernel(half_ref, own_ref, other_ref, inverse_ref, ortho_ref):
    step = pl.program_id(0)

    def turn(ref):
        rows = wide(ref[...], 3 * RANK)
        for p in range(3):
            high, low = split2(thrice(inverse_ref[p, :, RANK:], rows[RANK * p : RANK * (p + 1)]))
            both = jnp.concatenate([high.astype(f32), low.astype(f32)], axis=0)
            ortho_ref[p] = both.T.astype(bf16)

    @pl.when(step < STEPS)
    def _():
        turn(own_ref)

    @pl.when(step >= STEPS)
    def _():
        turn(other_ref)


def turn(half, own, other, inverse):
    def column(j, h):
        return lax.rem(j // STEPS + h[0], 2) * STEPS + lax.rem(j, STEPS)

    return pl.pallas_call(
        turn_kernel,
        grid_spec=pltpu.PrefetchScalarGridSpec(
            num_scalar_prefetch=1,
            grid=(2 * STEPS,),
            in_specs=[
                pl.BlockSpec((CT * 3 * RANK, 128), lambda j, h: (jnp.minimum(j, STEPS - 1), 0)),
                pl.BlockSpec((CT * 3 * RANK, 128), lambda j, h: (jnp.maximum(j - STEPS, 0), 0)),
                pl.BlockSpec((4, RANK, 128), lambda j, h: (0, 0, 0)),
            ],
            out_specs=pl.BlockSpec((3, TILE, 128), lambda j, h: (0, column(j, h), 0)),
        ),
        out_shape=pltpu.HBM((3, D, 128), bf16),
        cost_estimate=cost(6),
        compiler_params=pltpu.CompilerParams(vmem_limit_bytes=VMEM),
        name="turn",
    )(half, own, other, inverse)


def rest_in_kernel(summed_in_ref, inverse_hbm, grads_hbm, turned_hbm, err_in_hbm, ortho_hbm, moment_hbm, rest_hbm,
                   factor_in_ref, inverse_scr, grads_scr, turned_scr, err_in_scr, ortho_scr, moment_scr, rest_scr, in_sem,
                   out_sem):
    def rows(j):
        return slice(TILE * j, TILE * (j + 1))

    tiles = range(2 * STEPS)
    first = [
        pltpu.make_async_copy(inverse_hbm, inverse_scr, in_sem.at[0, len(tiles)]),
        pltpu.make_async_copy(grads_hbm, grads_scr, in_sem.at[1, len(tiles)]),
    ]
    into = [[pltpu.make_async_copy(ortho_hbm.at[:, rows(j)], ortho_scr.at[j], in_sem.at[0, j])] for j in tiles]
    for j in range(STEPS):
        into[j].append(pltpu.make_async_copy(turned_hbm.at[rows(j)], turned_scr.at[j], in_sem.at[1, j]))
        into[j].append(pltpu.make_async_copy(err_in_hbm.at[:, rows(j)], err_in_scr.at[j], in_sem.at[2, j]))
        into[j + STEPS].append(
            pltpu.make_async_copy(moment_hbm.at[:, rows(j)], moment_scr.at[j], in_sem.at[1, j + STEPS])
        )
    out = [pltpu.make_async_copy(rest_scr.at[j], rest_hbm.at[:, rows(j)], out_sem.at[j]) for j in tiles]
    for copy in first:
        copy.start()
    order = [j + half for j in range(STEPS) for half in (0, STEPS)]
    for j in order:
        for copy in into[j]:
            copy.start()
    for copy in first:
        copy.wait()
    grads = jnp.concatenate([grads_scr[p] for p in range(3)], axis=1)
    weights = []
    for p in range(3):
        right = wide(summed_in_ref[HEADS * RANK * p : HEADS * RANK * (p + 1), :], RANK) * (1.0 / N_DP)
        factor = thrice(inverse_scr[p, :, RANK:], right)
        factor_in_ref[p] = factor
        high, low = split2(-factor)
        weights.append(jnp.concatenate([high, high, low, jnp.zeros_like(low)], axis=0))
    for j in order:
        for copy in into[j]:
            copy.wait()
        moments = nn(turned_scr[j], grads) if j < STEPS else None
        for p in range(3):
            if j < STEPS:
                moment = moments[:, COLS * p : COLS * (p + 1)] + err_in_scr[j, p].astype(f32)
            else:
                moment = moment_scr[j - STEPS, p]
            both = jnp.concatenate([ortho_scr[j, p], ortho_scr[j, p]], axis=1)
            rest_scr[j, p] = (moment + nn(both, weights[p])).astype(bf16)
        out[j].start()
    for copy in out:
        copy.wait()


def rest_in(summed, inverse, grads, turned, err_in, ortho_in, moment_in):
    whole = pl.BlockSpec(memory_space=pltpu.VMEM)
    tiles = 2 * STEPS
    return pl.pallas_call(
        rest_in_kernel,
        in_specs=[whole] + [ANY] * 6,
        out_specs=[ANY, whole],
        scratch_shapes=[
            pltpu.VMEM((4, RANK, 128), f32),
            pltpu.VMEM((3, TOK, COLS), bf16),
            pltpu.VMEM((STEPS, TILE, TOK), bf16),
            pltpu.VMEM((STEPS, 3, TILE, COLS), bf16),
            pltpu.VMEM((tiles, 3, TILE, 128), bf16),
            pltpu.VMEM((STEPS, 3, TILE, COLS), f32),
            pltpu.VMEM((tiles, 3, TILE, COLS), bf16),
            pltpu.SemaphoreType.DMA((3, tiles + 1)),
            pltpu.SemaphoreType.DMA((tiles,)),
        ],
        out_shape=[
            pltpu.HBM((3, D, COLS), bf16),
            jax.ShapeDtypeStruct((3, RANK, COLS), f32),
        ],
        cost_estimate=cost(9),
        compiler_params=pltpu.CompilerParams(vmem_limit_bytes=VMEM_LAST),
        name="rest_in",
    )(summed, *streamed(inverse, grads, turned, err_in, ortho_in, moment_in))


def rest_out_kernel(place_ref, *refs):
    piece_refs, (inverse_hbm, ortho_out_hbm, moment_hbm) = refs[:4], refs[4:7]
    rest_hbm, factor_hbm, inverse_scr, ortho_out_scr, moment_scr, rest_scr, factor_scr, first_sem, in_sem, out_sem = refs[7:]
    small = zip((inverse_hbm.at[3], ortho_out_hbm), (inverse_scr, ortho_out_scr))
    first = [pltpu.make_async_copy(a, b, first_sem.at[i]) for i, (a, b) in enumerate(small)]

    def column(j):
        at = lax.rem(place_ref[0] + j // 4, 2) * 4 + lax.rem(place_ref[1] + 4 - j % 4, 4)
        return pl.ds(pl.multiple_of(at * COLS, COLS), COLS)

    into = [pltpu.make_async_copy(moment_hbm.at[:, column(j)], moment_scr.at[j], in_sem.at[j]) for j in range(8)]
    out = [
        (
            pltpu.make_async_copy(rest_scr.at[j], rest_hbm.at[:, column(j)], out_sem.at[0, j]),
            pltpu.make_async_copy(factor_scr.at[j], factor_hbm.at[:, column(j)], out_sem.at[1, j]),
        )
        for j in range(8)
    ]
    for copy in first:
        copy.start()
    for copy in into:
        copy.start()
    for copy in first:
        copy.wait()
    high, low = split2(ortho_out_scr[...])
    stack = jnp.concatenate([high, high, low, jnp.zeros_like(low)], axis=0)
    both = stack.astype(f32).T.astype(bf16)
    inverse = inverse_scr[:, RANK:]
    for j in range(0, 8, 2):
        mine = slice(PIECE * (j // 4), PIECE * (j // 4 + 1))
        right = jnp.concatenate([wide(piece_refs[k % 4][mine, :], RANK) for k in (j, j + 1)], axis=1)
        factor = thrice(inverse, right * (1.0 / N_DP))
        high, low = split2(-factor)
        for k in (j, j + 1):
            into[k].wait()
        total = nn(both, jnp.concatenate([high, low, high, jnp.zeros_like(low)], axis=0))
        for i, k in enumerate((j, j + 1)):
            mine = slice(COLS * i, COLS * (i + 1))
            factor_scr[k] = factor[:, mine]
            rest_scr[k] = (total[:, mine] + moment_scr[k]).astype(bf16)
            for copy in out[k]:
                copy.start()
    for pair in out:
        for copy in pair:
            copy.wait()


def rest_out(place, pieces, inverse, ortho_out, moment_out):
    whole = pl.BlockSpec(memory_space=pltpu.VMEM)
    return pl.pallas_call(
        rest_out_kernel,
        in_specs=[pl.BlockSpec(memory_space=pltpu.SMEM)] + [whole] * 4 + [ANY] * 3,
        out_specs=[ANY, ANY],
        scratch_shapes=[
            pltpu.VMEM((RANK, 128), f32),
            pltpu.VMEM((RANK, COLS), f32),
            pltpu.VMEM((8, COLS, COLS), f32),
            pltpu.VMEM((8, COLS, COLS), bf16),
            pltpu.VMEM((8, RANK, COLS), f32),
            pltpu.SemaphoreType.DMA((2,)),
            pltpu.SemaphoreType.DMA((8,)),
            pltpu.SemaphoreType.DMA((2, 8)),
        ],
        out_shape=[pltpu.HBM((COLS, D), bf16), pltpu.HBM((RANK, D), f32)],
        cost_estimate=cost(6),
        compiler_params=pltpu.CompilerParams(vmem_limit_bytes=VMEM),
        name="rest_out",
    )(place, *pieces, *streamed(inverse, ortho_out, moment_out))


CHIP = ("x", "y", "z")
SWAP = [(0, 1), (1, 0)]
OTHERS = (2, 1, 3)


def ring(shift):
    return [(a, (a + shift) % 4) for a in range(4)]


def shards(inputs, grad_y, q_pre, f_pre, v_pre, w_out, err_in, err_out, basis_in, basis_out):
    keep = (err_in[0], err_out[0], inputs, grad_y)
    core = lax.axis_index("c").astype(jnp.int32)
    z = lax.axis_index("z").astype(jnp.int32)
    me = (lax.axis_index("x") * 4 + lax.axis_index("y")).astype(jnp.int32) * 4 + z
    mine = core[None]
    theirs = 1 - mine
    place = jnp.stack([core, z])
    q_pre, place, mine, theirs, me = lax.optimization_barrier((q_pre, place, mine, theirs, me[None]))
    hidden, grads, near_err_in, near_err_out, near_inputs, near_grad_y = recurrence(
        grad_y, w_out, q_pre, f_pre, v_pre, keep
    )
    err_in, err_out = keep[:2]
    send = left(theirs, near_inputs, grads, near_err_in, basis_in)
    arrived = lax.ppermute(send, "c", SWAP)
    left_out_part = left_out(near_grad_y, hidden, near_err_out, basis_out)
    rows = left(mine, near_inputs, grads, near_err_in, basis_in, arrived, left_out_part)

    rows, hidden_now = lax.optimization_barrier((rows, hidden))
    received = lax.all_to_all(rows.reshape(CHIPS, EACH1, 128), CHIP, 0, 0)
    inputs_turned, moment_in, moment_out = ahead(inputs, grads, err_in, hidden_now, grad_y, err_out)
    received, inputs_turned = lax.optimization_barrier((received, inputs_turned))
    own = lax.all_to_all(answer_left(me, received), CHIP, 0, 0).reshape(ROWS1, 128)
    other = lax.ppermute(own, "c", SWAP)
    left_out_sum = own[L_ROWS : L_ROWS + LO_ROWS]

    send, keep_out, near_inputs, near_err_in = right_out(
        place, left_out_sum, grad_y, hidden, err_out, inputs, err_in
    )
    arrived = lax.ppermute(send, "c", SWAP)
    gram_in = gram(own, other)
    arrived, gram_in, near_inputs = lax.optimization_barrier((arrived, gram_in, near_inputs))
    gram_out = send[RO_ROWS:] + arrived[RO_ROWS:]
    quarters = (keep_out + arrived[:RO_ROWS]).reshape(4, PIECE, 128)
    pieces = [jnp.concatenate([quarters[shift], gram_out]) for shift in range(4)]
    pieces = [pieces[0]] + [lax.ppermute(pieces[shift], "z", ring(shift)) for shift in OTHERS]
    right_part = right_own(theirs, own, near_inputs, near_err_in, inputs, err_in)
    rows, gram_out = join(right_other(other, *right_part, grads), *pieces)

    received = lax.all_to_all(rows.reshape(N_DP, EACH2, 128), ("x", "y"), 0, 0)
    inverse, ortho_out = invert(gram_in, left_out_sum, gram_out)
    received, inverse, ortho_out = lax.optimization_barrier((received, inverse, ortho_out))
    everywhere = answer_right(received)
    everywhere, inverse = lax.optimization_barrier((everywhere, inverse))
    summed = lax.all_to_all(everywhere, ("x", "y"), 0, 0).reshape(ROWS2, 128)
    ortho_in = turn(mine, own, other, inverse)
    summed, ortho_in = lax.optimization_barrier((summed, ortho_in))

    piece = summed[RI_ROWS:]
    pieces = [jnp.concatenate([piece, lax.ppermute(piece, "c", SWAP)])]
    pieces += [lax.ppermute(pieces[0], "z", ring(shift)) for shift in (1, 2, 3)]
    new_in, factor_in = rest_in(summed, inverse, grads, inputs_turned, err_in, ortho_in, moment_in)
    new_out, factor_out = rest_out(place, pieces, inverse, ortho_out, moment_out)
    return new_in[None], new_out[None], factor_in, factor_out


def solution(mesh):
    fine = Mesh(mesh.devices.reshape(4, 4, 4, 2), ("x", "y", "z", "c"))
    dp, head = ("x", "y"), ("z", "c")
    placed = (
        P(dp, None),
        P(dp, None),
        P(dp, head),
        P(dp, head),
        P(dp, head),
        P(head, None),
        P(dp, None, None, head),
        P(dp, head, None),
        P(None, None, head),
        P(),
    )
    return jax.shard_map(
        shards,
        mesh=fine,
        in_specs=placed,
        out_specs=(P(dp, None, None, head), P(dp, head, None), P(None, None, head), P()),
        check_vma=False,
    )
```

```python
import functools

import jax
import jax.numpy as jnp
from jax import lax
from jax.experimental import pallas as pl
from jax.experimental.pallas import tpu as pltpu
from jax.sharding import Mesh, PartitionSpec as P

TOK = 256
DK = 128
HEADS = 3
COLS = HEADS * DK
RANK = 64
D = 3072
HALF = D // 2
TILE = 512
STEPS = HALF // TILE
CT = TILE // 128
N_DP = 16
CHIPS = 64
L_ROWS = 12 * 3 * RANK
LO_ROWS = HEADS * RANK
ROWS1 = 2560
EACH1 = 40
L_STEP = CT * 3 * RANK
RI_ROWS = 9 * RANK
RO_ROWS = 12 * RANK
ROWS2 = 768
EACH2 = 48
PIECE = HEADS * RANK
GRAM_ROWS = RANK // 2

f32 = jnp.float32
bf16 = jnp.bfloat16
EXACT = lax.Precision.HIGHEST
VMEM = 24 * 1024 * 1024
VMEM_LAST = 40 * 1024 * 1024


def cost(us):
    return pl.CostEstimate(flops=int(us * 1e9), bytes_accessed=int(us * 3e6), transcendentals=0)


def nn(a, b):
    return lax.dot_general(a, b, (((1,), (0,)), ((), ())), preferred_element_type=f32)


def nt(a, b):
    return lax.dot_general(a, b, (((1,), (1,)), ((), ())), preferred_element_type=f32)


def tn(a, b):
    return lax.dot_general(a, b, (((0,), (0,)), ((), ())), preferred_element_type=f32)


def exact_nt(a, b):
    return lax.dot_general(a, b, (((1,), (1,)), ((), ())), precision=EXACT, preferred_element_type=f32)


def split2(a):
    high = a.astype(bf16)
    return high, (a - high.astype(f32)).astype(bf16)


def thrice(a, b):
    a_high, a_low = split2(a)
    b_high, b_low = split2(b)
    return nn(jnp.concatenate([a_high, a_high, a_low], axis=1), jnp.concatenate([b_high, b_low, b_high], axis=0))


def split3(a):
    high = a.astype(bf16)
    rest = a - high.astype(f32)
    mid = rest.astype(bf16)
    return high, mid, (rest - mid.astype(f32)).astype(bf16)


def summed3(ones, a):
    parts = nn(ones, jnp.concatenate(split3(a), axis=1))
    width = a.shape[1]
    return parts[:, :width] + (parts[:, width : 2 * width] + parts[:, 2 * width :])


def stacked(a):
    return jnp.concatenate(split2(a), axis=0)


def folded(a):
    half = a.shape[0] // 2
    return a[:half] + a[half:]


def head_forward(q, f):
    q_gate = 1.0 / (1.0 + jnp.exp(-q))
    query = q * q_gate
    small = jnp.exp(-jnp.abs(f))
    key = jnp.where(f >= 0, small, 1.0) / (1.0 + small)
    decay = jnp.where(f >= 0, 1.0, small) / (1.0 + small)
    log_decay = jnp.minimum(f, 0.0) - jnp.log1p(small)
    row = lax.broadcasted_iota(jnp.int32, (TOK, TOK), 0)
    col = lax.broadcasted_iota(jnp.int32, (TOK, TOK), 1)
    running = summed3(jnp.where(row >= col, 1.0, 0.0).astype(bf16), log_decay)
    differ = row ^ col
    scores = jnp.zeros((TOK, TOK), f32)
    levels = []
    for size in (128, 64, 32, 16, 8):
        blocks = running.reshape(TOK // (2 * size), 2 * size, DK)
        spread = (blocks - blocks[:, size - 1 : size, :]).reshape(TOK, DK)
        if size > 8:
            q_scale = jnp.exp(jnp.minimum(spread, 0.0))
            k_scale = jnp.exp(jnp.minimum(-spread, 0.0))
            mask = (differ >= size) & (differ < 2 * size) & (row > col)
        else:
            q_scale = jnp.exp(spread)
            k_scale = jnp.exp(-spread)
            mask = (differ < 2 * size) & (row >= col)
        q_high, q_low = split2(query * q_scale)
        k_high, k_low = split2(key * k_scale)
        level = nt(
            jnp.concatenate([q_high, q_high, q_low], axis=1),
            jnp.concatenate([k_high, k_low, k_high], axis=1),
        )
        scores = jnp.where(mask, level, scores)
        levels.append((q_scale, k_scale, q_high, q_low, k_high, k_low))
    return (query, key, decay, q_gate), levels, split2(scores)


def head_backward(gates, levels, scores, v, grad_o):
    query, key, decay, q_gate = gates
    row = lax.broadcasted_iota(jnp.int32, (TOK, TOK), 0)
    col = lax.broadcasted_iota(jnp.int32, (TOK, TOK), 1)
    differ = row ^ col
    grad_s = split2(nt(grad_o, v))
    grad_st = split2(nt(v, grad_o))
    grad_query = jnp.zeros((TOK, DK), f32)
    grad_key = jnp.zeros((TOK, DK), f32)
    for size, (q_scale, k_scale, q_high, q_low, k_high, k_low) in zip((128, 64, 32, 16, 8), levels):
        if size > 8:
            within = (differ >= size) & (differ < 2 * size)
            mask, mask_t = within & (row > col), within & (row < col)
        else:
            within = differ < 2 * size
            mask, mask_t = within & (row >= col), within & (row <= col)
        keep = jnp.where(mask, 1.0, 0.0).astype(bf16)
        keep_t = jnp.where(mask_t, 1.0, 0.0).astype(bf16)
        both = nn(grad_s[0] * keep, jnp.concatenate([k_high, k_low], axis=1))
        grad_query += q_scale * (both[:, :DK] + both[:, DK:] + nn(grad_s[1] * keep, k_high))
        both = nn(grad_st[0] * keep_t, jnp.concatenate([q_high, q_low], axis=1))
        grad_key += k_scale * (both[:, :DK] + both[:, DK:] + nn(grad_st[1] * keep_t, q_high))
    grad_v = tn(scores[0], grad_o) + tn(scores[1], grad_o)
    upper = jnp.where(row <= col, 1.0, 0.0).astype(bf16)
    grad_decay = summed3(upper, query * grad_query - key * grad_key)
    grad_q = grad_query * (q_gate + query * (1.0 - q_gate))
    return grad_q, key * (grad_decay - grad_key * decay), grad_v


def recurrence_kernel(q_hbm, f_hbm, v_hbm, gy_hbm, w_hbm, *refs):
    sources, (hid_ref, grad_ref), kept, (q_scr, f_scr, v_scr, gy_scr, w_scr, sem) = (
        refs[:4],
        refs[4:6],
        refs[6:10],
        refs[10:],
    )
    pairs = list(zip((q_hbm, f_hbm, v_hbm, gy_hbm, w_hbm), (q_scr, f_scr, v_scr, gy_scr, w_scr)))
    copies = [pltpu.make_async_copy(a, b, sem.at[i]) for i, (a, b) in enumerate(pairs + list(zip(sources, kept)))]
    for copy in copies:
        copy.start()
    for copy in copies[:3]:
        copy.wait()
    for h in range(HEADS):
        mine = slice(DK * h, DK * (h + 1))
        gates, levels, scores = head_forward(q_scr[:, mine].astype(f32), f_scr[:, mine].astype(f32))
        v = v_scr[:, mine]
        hid_ref[:, mine] = (nn(scores[0], v) + nn(scores[1], v)).astype(bf16)
        if h == 0:
            for copy in copies[3:5]:
                copy.wait()
            grad_o = nt(gy_scr[...], w_scr[...]).astype(bf16)
        for p, grad in enumerate(head_backward(gates, levels, scores, v, grad_o[:, mine])):
            grad_ref[p, :, mine] = grad.astype(bf16)
    for copy in copies[5:]:
        copy.wait()


def held(*arrays):
    return [pltpu.with_memory_space_constraint(a, pltpu.VMEM) for a in arrays]


def streamed(*arrays):
    return [pltpu.with_memory_space_constraint(a, pltpu.HBM) for a in arrays]


ANY = pl.BlockSpec(memory_space=pl.ANY)


def fetched(step, steps, column, width, sources, slots, sem):
    def copies(j):
        at = pl.ds(pl.multiple_of(column(j) * width, width), width)
        for i, (axis, source) in enumerate(sources):
            index = [slice(None)] * len(source.shape)
            index[axis] = at
            yield pltpu.make_async_copy(source.at[tuple(index)], slots[i].at[j], sem.at[i, j])

    @pl.when(step == 0)
    def _():
        for j in range(steps):
            for copy in copies(j):
                copy.start()

    for copy in copies(step):
        copy.wait()
    return [slot.at[step] for slot in slots]


def recurrence(grad_y, w_out, q_pre, f_pre, v_pre, keep):
    operands = (q_pre, f_pre, v_pre, grad_y, w_out) + keep
    whole = pl.BlockSpec(memory_space=pltpu.VMEM)
    return pl.pallas_call(
        recurrence_kernel,
        in_specs=[ANY] * len(operands),
        out_specs=[whole] * 2 + [ANY] * len(keep),
        out_shape=[
            jax.ShapeDtypeStruct((TOK, COLS), bf16),
            jax.ShapeDtypeStruct((3, TOK, COLS), bf16),
        ]
        + [pltpu.VMEM(a.shape, a.dtype) for a in keep],
        scratch_shapes=[pltpu.VMEM(a.shape, a.dtype) for a in operands[:5]]
        + [pltpu.SemaphoreType.DMA((len(operands),))],
        cost_estimate=cost(8),
        compiler_params=pltpu.CompilerParams(vmem_limit_bytes=VMEM),
        name="recurrence",
    )(*streamed(*operands))


def tiles_of(a):
    return [a[:, 128 * i : 128 * (i + 1)] for i in range(a.shape[1] // 128)]


def left_tiles(half_ref, x_ref, grads_ref, err_in_ref, basis_in_ref):
    bases = [stacked(basis_in_ref[p]) for p in range(3)]
    tokens = jnp.concatenate([stacked(folded(nt(bases[p], grads_ref[p]))) for p in range(3)], axis=0)
    for step in range(STEPS):
        at = pl.ds(pl.multiple_of(half_ref[0] * HALF + step * TILE, TILE), TILE)
        from_tokens = nn(tokens, x_ref[:, at])
        for p in range(3):
            part = from_tokens[2 * RANK * p : 2 * RANK * (p + 1)] + nt(bases[p], err_in_ref[p, at, :])
            for i, tile in enumerate(tiles_of(folded(part))):
                yield step * L_STEP + (3 * i + p) * RANK, tile


def left_send_kernel(half_ref, x_ref, grads_ref, err_in_ref, basis_in_ref, left_ref):
    for at, tile in left_tiles(half_ref, x_ref, grads_ref, err_in_ref, basis_in_ref):
        left_ref[at : at + RANK, :] = tile


def left_keep_kernel(half_ref, x_ref, grads_ref, err_in_ref, basis_in_ref, arrived_ref, left_out_ref, rows_hbm, rows_scr, sem):
    parts = [slice(L_STEP * step, L_STEP * (step + 1)) for step in range(STEPS)] + [slice(L_ROWS, ROWS1)]
    copies = [pltpu.make_async_copy(rows_scr.at[part], rows_hbm.at[part], sem.at[i]) for i, part in enumerate(parts)]
    rows_scr[L_ROWS : L_ROWS + LO_ROWS, :] = left_out_ref[...]
    rows_scr[L_ROWS + LO_ROWS :, :] = jnp.zeros((ROWS1 - L_ROWS - LO_ROWS, 128), f32)
    copies[STEPS].start()
    for i, (at, tile) in enumerate(left_tiles(half_ref, x_ref, grads_ref, err_in_ref, basis_in_ref)):
        rows_scr[at : at + RANK, :] = tile + arrived_ref[at : at + RANK, :]
        if (i + 1) % (3 * CT) == 0:
            copies[i // (3 * CT)].start()
    for copy in copies:
        copy.wait()


def left(half, inputs, grads, err_in, basis_in, *arrived):
    keep = {}
    if arrived:
        keep = dict(
            out_specs=ANY, scratch_shapes=[pltpu.VMEM((ROWS1, 128), f32), pltpu.SemaphoreType.DMA((STEPS + 1,))]
        )
    return pl.pallas_call(
        left_keep_kernel if arrived else left_send_kernel,
        in_specs=[pl.BlockSpec(memory_space=pltpu.SMEM)] + [pl.BlockSpec(memory_space=pltpu.VMEM)] * (4 + len(arrived)),
        out_shape=pltpu.HBM((ROWS1, 128), f32) if arrived else jax.ShapeDtypeStruct((L_ROWS, 128), f32),
        cost_estimate=cost(3),
        compiler_params=pltpu.CompilerParams(vmem_limit_bytes=VMEM),
        name="left_keep" if arrived else "left_send",
        **keep,
    )(half, *held(inputs), grads, *held(err_in), basis_in, *arrived)


def left_out_kernel(gy_ref, hid_ref, err_out_ref, basis_out_ref, left_out_ref):
    basis = stacked(basis_out_ref[...])
    tokens = stacked(folded(nt(basis, gy_ref[...])))
    part = folded(nt(basis, err_out_ref[...]) + nn(tokens, hid_ref[...]))
    for i, tile in enumerate(tiles_of(part)):
        left_out_ref[RANK * i : RANK * (i + 1), :] = tile


def left_out(grad_y, hidden, err_out, basis_out):
    return pl.pallas_call(
        left_out_kernel,
        out_shape=jax.ShapeDtypeStruct((LO_ROWS, 128), f32),
        cost_estimate=cost(4),
        compiler_params=pltpu.CompilerParams(vmem_limit_bytes=VMEM),
        name="left_out",
    )(*held(grad_y), hidden, *held(err_out), basis_out)


def ahead_kernel(x_ref, grads_ref, err_in_ref, hid_ref, gy_ref, err_out_ref, x_later_ref, turned_ref, moment_in_ref,
                 moment_out_ref):
    turned_ref[...] = x_ref[...].astype(f32).T.astype(bf16)
    later = x_later_ref[...].astype(f32).T.astype(bf16)
    moments = nn(later, jnp.concatenate([grads_ref[p] for p in range(3)], axis=1))
    for p in range(3):
        moment_in_ref[p] = moments[:, COLS * p : COLS * (p + 1)] + err_in_ref[p].astype(f32)
    moment_out_ref[...] = tn(hid_ref[...], gy_ref[...]) + err_out_ref[...].astype(f32)


def ahead(inputs, grads, err_in, hidden, grad_y, err_out):
    wide_tile = D // STEPS
    return pl.pallas_call(
        ahead_kernel,
        grid=(STEPS,),
        in_specs=[
            pl.BlockSpec((TOK, TILE), lambda j: (0, j)),
            pl.BlockSpec((3, TOK, COLS), lambda j: (0, 0, 0)),
            pl.BlockSpec((3, TILE, COLS), lambda j: (0, j + STEPS, 0)),
            pl.BlockSpec((TOK, COLS), lambda j: (0, 0)),
            pl.BlockSpec((TOK, wide_tile), lambda j: (0, j)),
            pl.BlockSpec((COLS, wide_tile), lambda j: (0, j)),
            pl.BlockSpec((TOK, TILE), lambda j: (0, j + STEPS)),
        ],
        out_specs=[
            pl.BlockSpec((TILE, TOK), lambda j: (j, 0)),
            pl.BlockSpec((3, TILE, COLS), lambda j: (0, j, 0)),
            pl.BlockSpec((COLS, wide_tile), lambda j: (0, j)),
        ],
        out_shape=[
            pltpu.HBM((HALF, TOK), bf16),
            pltpu.HBM((3, HALF, COLS), f32),
            pltpu.HBM((COLS, D), f32),
        ],
        cost_estimate=cost(9),
        compiler_params=pltpu.CompilerParams(vmem_limit_bytes=VMEM),
        name="ahead",
    )(*streamed(inputs, grads, err_in, hidden, grad_y, err_out, inputs))


def wide(block, rows):
    return jnp.concatenate([block[i * rows : (i + 1) * rows] for i in range(block.shape[0] // rows)], axis=1)


def answer_left_kernel(me_ref, received_ref, answer_ref):
    over_xy = []
    for z in range(4):
        total = received_ref[z]
        for i in range(1, N_DP):
            total += received_ref[4 * i + z]
        over_xy.append(total)
    total = (over_xy[0] + over_xy[1]) + (over_xy[2] + over_xy[3])
    row = me_ref[0] * EACH1 + lax.broadcasted_iota(jnp.int32, (EACH1, 128), 0)
    for z in range(4):
        answer = jnp.where(row >= L_ROWS, over_xy[z], total)
        for i in range(N_DP):
            answer_ref[4 * i + z] = answer


def answer_left(me, received):
    whole = pl.BlockSpec((CHIPS, EACH1, 128), lambda j, m: (0, 0, 0))
    return pl.pallas_call(
        answer_left_kernel,
        grid_spec=pltpu.PrefetchScalarGridSpec(num_scalar_prefetch=1, grid=(1,), in_specs=[whole], out_specs=whole),
        out_shape=jax.ShapeDtypeStruct((CHIPS, EACH1, 128), f32),
        cost_estimate=cost(2),
        compiler_params=pltpu.CompilerParams(vmem_limit_bytes=VMEM),
        name="answer_left",
    )(me, received)


def answer_right_kernel(received_ref, answer_ref):
    total = received_ref[0]
    for i in range(1, N_DP):
        total += received_ref[i]
    for i in range(N_DP):
        answer_ref[i] = total


def answer_right(received):
    return pl.pallas_call(
        answer_right_kernel,
        out_shape=jax.ShapeDtypeStruct((N_DP, EACH2, 128), f32),
        cost_estimate=cost(1),
        compiler_params=pltpu.CompilerParams(vmem_limit_bytes=VMEM),
        name="answer_right",
    )(received)


def right_out_kernel(place_ref, left_out_ref, hid_ref, gy_hbm, err_out_hbm, x_hbm, err_in_hbm, send_ref, keep_ref, x_out,
                     err_in_out, gy_scr, err_out_scr, sem, near_sem):
    def column(j):
        at = lax.rem(place_ref[0] + 1 + j // 4, 2) * 4 + lax.rem(place_ref[1] + j % 4, 4)
        return pl.ds(pl.multiple_of(at * COLS, COLS), COLS)

    copies = [
        (
            pltpu.make_async_copy(gy_hbm.at[:, column(j)], gy_scr.at[j], sem.at[0, j]),
            pltpu.make_async_copy(err_out_hbm.at[:, column(j)], err_out_scr.at[j], sem.at[1, j]),
        )
        for j in range(8)
    ]
    near = near_copies(place_ref[0], x_hbm, err_in_hbm, x_out, err_in_out, near_sem)
    for pair in copies + [near]:
        for copy in pair:
            copy.start()
    left_out = wide(left_out_ref[...], RANK)
    factor = stacked(left_out)
    both = jnp.concatenate([factor, stacked(folded(nt(factor, hid_ref[...])))], axis=1)
    gram = exact_nt(left_out, left_out)
    send_ref[RO_ROWS:, :] = jnp.concatenate([gram[:GRAM_ROWS], gram[GRAM_ROWS:]], axis=1)
    for j in range(0, 8, 2):
        for pair in copies[j : j + 2]:
            for copy in pair:
                copy.wait()
        err_out = jnp.concatenate([err_out_scr[j], err_out_scr[j + 1]], axis=1)
        gy = jnp.concatenate([gy_scr[j], gy_scr[j + 1]], axis=1)
        part = folded(nn(both, jnp.concatenate([err_out, gy], axis=0)))
        ref = send_ref if j < 4 else keep_ref
        for i, tile in enumerate(tiles_of(part)):
            at = (j % 4) * PIECE + i * RANK
            ref[at : at + RANK, :] = tile
    for copy in near:
        copy.wait()


def right_out(place, left_out_sum, grad_y, hidden, err_out, inputs, err_in):
    whole = pl.BlockSpec(memory_space=pltpu.VMEM)
    return pl.pallas_call(
        right_out_kernel,
        in_specs=[pl.BlockSpec(memory_space=pltpu.SMEM), whole, whole, ANY, ANY, ANY, ANY],
        out_specs=[whole, whole, ANY, ANY],
        out_shape=[
            jax.ShapeDtypeStruct((RO_ROWS + GRAM_ROWS, 128), f32),
            jax.ShapeDtypeStruct((RO_ROWS, 128), f32),
            pltpu.VMEM((TOK, HALF), bf16),
            pltpu.VMEM((3, HALF, COLS), bf16),
        ],
        scratch_shapes=[
            pltpu.VMEM((8, TOK, COLS), bf16),
            pltpu.VMEM((8, COLS, COLS), bf16),
            pltpu.SemaphoreType.DMA((2, 8)),
            pltpu.SemaphoreType.DMA((2, STEPS)),
        ],
        cost_estimate=cost(3),
        compiler_params=pltpu.CompilerParams(vmem_limit_bytes=VMEM),
        name="right_out",
    )(place, left_out_sum, hidden, *streamed(grad_y, err_out, inputs, err_in))


def right_tile(rows, x, err_in, rights):
    high, low = split2(rows)
    for p in range(3):
        mine = slice(RANK * p, RANK * (p + 1))
        rights[p] += folded(nn(jnp.concatenate([high[mine], low[mine]], axis=0), err_in[p]))
    return folded(nt(jnp.concatenate([high, low], axis=0), x))


def near_copies(half, x_hbm, err_in_hbm, x_out, err_in_out, sem):
    copies = []
    for j in range(STEPS):
        at = pl.ds(pl.multiple_of(half * HALF + j * TILE, TILE), TILE)
        to = slice(j * TILE, (j + 1) * TILE)
        copies.append(pltpu.make_async_copy(x_hbm.at[:, at], x_out.at[:, to], sem.at[0, j]))
        copies.append(pltpu.make_async_copy(err_in_hbm.at[:, at], err_in_out.at[:, to], sem.at[1, j]))
    return copies


def right_sums(left_ref, x_ref, err_in_ref, tokens, rights):
    for j in range(STEPS):
        mine = slice(j * TILE, (j + 1) * TILE)
        rows = wide(left_ref[L_STEP * j : L_STEP * (j + 1), :], 3 * RANK)
        tokens += right_tile(rows, x_ref[:, mine], err_in_ref.at[:, mine], rights)
    return tokens


def right_own_kernel(half_ref, own_ref, x_ref, err_in_ref, x_hbm, err_in_hbm, right_ref, token_ref, x_out, err_in_out, sem):
    copies = near_copies(half_ref[0], x_hbm, err_in_hbm, x_out, err_in_out, sem)
    for copy in copies:
        copy.start()
    rights = [jnp.zeros((RANK, COLS), f32)] * 3
    token_ref[...] = right_sums(own_ref, x_ref, err_in_ref, jnp.zeros((3 * RANK, TOK), f32), rights)
    for p in range(3):
        right_ref[p] = rights[p]
    for copy in copies:
        copy.wait()


def right_own(other_half, own, near_inputs, near_err_in, inputs, err_in):
    whole = pl.BlockSpec(memory_space=pltpu.VMEM)
    return pl.pallas_call(
        right_own_kernel,
        in_specs=[pl.BlockSpec(memory_space=pltpu.SMEM), whole, whole, whole, ANY, ANY],
        out_specs=[whole, whole, ANY, ANY],
        out_shape=[
            jax.ShapeDtypeStruct((3, RANK, COLS), f32),
            jax.ShapeDtypeStruct((3 * RANK, TOK), f32),
            pltpu.VMEM((TOK, HALF), bf16),
            pltpu.VMEM((3, HALF, COLS), bf16),
        ],
        scratch_shapes=[pltpu.SemaphoreType.DMA((2, STEPS))],
        cost_estimate=cost(3),
        compiler_params=pltpu.CompilerParams(vmem_limit_bytes=VMEM),
        name="right_own",
    )(other_half, own, *held(near_inputs, near_err_in), *streamed(inputs, err_in))


def right_other_kernel(other_ref, right_ref, token_ref, x_ref, err_in_ref, grads_ref, rows_ref):
    rights = [right_ref[p] for p in range(3)]
    tokens = right_sums(other_ref, x_ref, err_in_ref, token_ref[...], rights)
    for p in range(3):
        total = rights[p] + folded(nn(stacked(tokens[RANK * p : RANK * (p + 1)]), grads_ref[p]))
        for i, tile in enumerate(tiles_of(total)):
            at = (HEADS * p + i) * RANK
            rows_ref[at : at + RANK, :] = tile


def right_other(other, right_part, token_part, inputs, err_in, grads):
    return pl.pallas_call(
        right_other_kernel,
        out_shape=jax.ShapeDtypeStruct((RI_ROWS, 128), f32),
        cost_estimate=cost(4),
        compiler_params=pltpu.CompilerParams(vmem_limit_bytes=VMEM),
        name="right_other",
    )(other, right_part, token_part, *held(inputs, err_in), grads)


def join_kernel(right_ref, own_ref, first_ref, second_ref, third_ref, rows_ref, gram_ref):
    piece = (own_ref[...] + first_ref[...]) + (second_ref[...] + third_ref[...])
    rows_ref[:RI_ROWS, :] = right_ref[...]
    rows_ref[RI_ROWS:, :] = piece[:PIECE]
    gram_ref[...] = piece[PIECE:]


def join(*operands):
    return pl.pallas_call(
        join_kernel,
        out_shape=[jax.ShapeDtypeStruct((ROWS2, 128), f32), jax.ShapeDtypeStruct((GRAM_ROWS, 128), f32)],
        cost_estimate=cost(1),
        compiler_params=pltpu.CompilerParams(vmem_limit_bytes=VMEM),
        name="join",
    )(*operands)


def gram_kernel(own_ref, other_ref, gram_ref):
    gram = jnp.zeros((3 * RANK, 3 * RANK), f32)
    for ref in (own_ref, other_ref):
        for i in range(STEPS):
            rows = wide(ref[L_STEP * i : L_STEP * (i + 1), :], 3 * RANK)
            gram += exact_nt(rows, rows)
    gram_ref[...] = gram


def gram(own, other):
    return pl.pallas_call(
        gram_kernel,
        out_shape=jax.ShapeDtypeStruct((3 * RANK, 3 * RANK), f32),
        cost_estimate=cost(2),
        compiler_params=pltpu.CompilerParams(vmem_limit_bytes=VMEM),
        name="gram",
    )(own, other)


def invert_kernel(gram_in_ref, left_out_ref, gram_out_ref, inverse_ref, ortho_out_ref):
    eye = jnp.where(
        lax.broadcasted_iota(jnp.int32, (RANK, RANK), 0) == lax.broadcasted_iota(jnp.int32, (RANK, RANK), 1),
        1.0,
        0.0,
    )
    gram = gram_in_ref[...]
    for p in range(3):
        mine = slice(RANK * p, RANK * (p + 1))
        inverse_ref[p] = jnp.concatenate([gram[mine, mine], eye], axis=1)
    gram_out = jnp.concatenate([gram_out_ref[:, :RANK], gram_out_ref[:, RANK:]], axis=0)
    inverse_ref[3] = jnp.concatenate([gram_out, eye], axis=1)
    rows8 = lax.broadcasted_iota(jnp.int32, (1, 8, 1), 1)
    tiles = [inverse_ref[:, 8 * t : 8 * t + 8, :] for t in range(RANK // 8)]
    for j in range(RANK):
        top, at = divmod(j, 8)
        pivot_row = tiles[top][:, at : at + 1, :]
        scaled = pivot_row * (1.0 / pivot_row[:, :, j : j + 1])
        for t in range(top, RANK // 8):
            column = tiles[t][:, :, j : j + 1]
            if t == top:
                column = jnp.where(rows8 > at, column, 0.0)
            tiles[t] = tiles[t] - column * scaled
    work = jnp.concatenate(tiles, axis=1)
    lane = lax.broadcasted_iota(jnp.int32, (4, RANK, 128), 2)
    sub = lax.broadcasted_iota(jnp.int32, (4, RANK, 128), 1)
    diagonal = jnp.sum(jnp.where(lane == sub, work, 0.0), axis=2, keepdims=True)
    inverse = work * lax.rsqrt(diagonal)
    inverse_ref[...] = inverse
    ortho_out_ref[...] = thrice(inverse[3, :, RANK:], wide(left_out_ref[...], RANK))


def invert(gram_in, left_out_sum, gram_out):
    return pl.pallas_call(
        invert_kernel,
        out_shape=[
            jax.ShapeDtypeStruct((4, RANK, 128), f32),
            jax.ShapeDtypeStruct((RANK, COLS), f32),
        ],
        cost_estimate=cost(10),
        compiler_params=pltpu.CompilerParams(vmem_limit_bytes=VMEM),
        name="invert",
    )(gram_in, left_out_sum, gram_out)


def turn_kernel(half_ref, own_ref, other_ref, inverse_ref, ortho_ref):
    step = pl.program_id(0)

    def turn(ref):
        rows = wide(ref[...], 3 * RANK)
        for p in range(3):
            high, low = split2(thrice(inverse_ref[p, :, RANK:], rows[RANK * p : RANK * (p + 1)]))
            both = jnp.concatenate([high.astype(f32), low.astype(f32)], axis=0)
            ortho_ref[p] = both.T.astype(bf16)

    @pl.when(step < STEPS)
    def _():
        turn(own_ref)

    @pl.when(step >= STEPS)
    def _():
        turn(other_ref)


def turn(half, own, other, inverse):
    def column(j, h):
        return lax.rem(j // STEPS + h[0], 2) * STEPS + lax.rem(j, STEPS)

    return pl.pallas_call(
        turn_kernel,
        grid_spec=pltpu.PrefetchScalarGridSpec(
            num_scalar_prefetch=1,
            grid=(2 * STEPS,),
            in_specs=[
                pl.BlockSpec((CT * 3 * RANK, 128), lambda j, h: (jnp.minimum(j, STEPS - 1), 0)),
                pl.BlockSpec((CT * 3 * RANK, 128), lambda j, h: (jnp.maximum(j - STEPS, 0), 0)),
                pl.BlockSpec((4, RANK, 128), lambda j, h: (0, 0, 0)),
            ],
            out_specs=pl.BlockSpec((3, TILE, 128), lambda j, h: (0, column(j, h), 0)),
        ),
        out_shape=pltpu.HBM((3, D, 128), bf16),
        cost_estimate=cost(6),
        compiler_params=pltpu.CompilerParams(vmem_limit_bytes=VMEM),
        name="turn",
    )(half, own, other, inverse)


def rest_in_kernel(summed_in_ref, inverse_hbm, grads_hbm, turned_hbm, err_in_hbm, ortho_hbm, moment_hbm, rest_hbm,
                   factor_in_ref, inverse_scr, grads_scr, turned_scr, err_in_scr, ortho_scr, moment_scr, rest_scr, in_sem,
                   out_sem):
    def rows(j):
        return slice(TILE * j, TILE * (j + 1))

    tiles = range(2 * STEPS)
    first = [
        pltpu.make_async_copy(inverse_hbm, inverse_scr, in_sem.at[0, len(tiles)]),
        pltpu.make_async_copy(grads_hbm, grads_scr, in_sem.at[1, len(tiles)]),
    ]
    into = [[pltpu.make_async_copy(ortho_hbm.at[:, rows(j)], ortho_scr.at[j], in_sem.at[0, j])] for j in tiles]
    for j in range(STEPS):
        into[j].append(pltpu.make_async_copy(turned_hbm.at[rows(j)], turned_scr.at[j], in_sem.at[1, j]))
        into[j].append(pltpu.make_async_copy(err_in_hbm.at[:, rows(j)], err_in_scr.at[j], in_sem.at[2, j]))
        into[j + STEPS].append(
            pltpu.make_async_copy(moment_hbm.at[:, rows(j)], moment_scr.at[j], in_sem.at[1, j + STEPS])
        )
    out = [pltpu.make_async_copy(rest_scr.at[j], rest_hbm.at[:, rows(j)], out_sem.at[j]) for j in tiles]
    for copy in first:
        copy.start()
    order = [j + half for j in range(STEPS) for half in (0, STEPS)]
    for j in order:
        for copy in into[j]:
            copy.start()
    for copy in first:
        copy.wait()
    grads = jnp.concatenate([grads_scr[p] for p in range(3)], axis=1)
    weights = []
    for p in range(3):
        right = wide(summed_in_ref[HEADS * RANK * p : HEADS * RANK * (p + 1), :], RANK) * (1.0 / N_DP)
        factor = thrice(inverse_scr[p, :, RANK:], right)
        factor_in_ref[p] = factor
        high, low = split2(-factor)
        weights.append(jnp.concatenate([high, high, low, jnp.zeros_like(low)], axis=0))
    for j in order:
        for copy in into[j]:
            copy.wait()
        moments = nn(turned_scr[j], grads) if j < STEPS else None
        for p in range(3):
            if j < STEPS:
                moment = moments[:, COLS * p : COLS * (p + 1)] + err_in_scr[j, p].astype(f32)
            else:
                moment = moment_scr[j - STEPS, p]
            both = jnp.concatenate([ortho_scr[j, p], ortho_scr[j, p]], axis=1)
            rest_scr[j, p] = (moment + nn(both, weights[p])).astype(bf16)
        out[j].start()
    for copy in out:
        copy.wait()


def rest_in(summed, inverse, grads, turned, err_in, ortho_in, moment_in):
    whole = pl.BlockSpec(memory_space=pltpu.VMEM)
    tiles = 2 * STEPS
    return pl.pallas_call(
        rest_in_kernel,
        in_specs=[whole] + [ANY] * 6,
        out_specs=[ANY, whole],
        scratch_shapes=[
            pltpu.VMEM((4, RANK, 128), f32),
            pltpu.VMEM((3, TOK, COLS), bf16),
            pltpu.VMEM((STEPS, TILE, TOK), bf16),
            pltpu.VMEM((STEPS, 3, TILE, COLS), bf16),
            pltpu.VMEM((tiles, 3, TILE, 128), bf16),
            pltpu.VMEM((STEPS, 3, TILE, COLS), f32),
            pltpu.VMEM((tiles, 3, TILE, COLS), bf16),
            pltpu.SemaphoreType.DMA((3, tiles + 1)),
            pltpu.SemaphoreType.DMA((tiles,)),
        ],
        out_shape=[
            pltpu.HBM((3, D, COLS), bf16),
            jax.ShapeDtypeStruct((3, RANK, COLS), f32),
        ],
        cost_estimate=cost(9),
        compiler_params=pltpu.CompilerParams(vmem_limit_bytes=VMEM_LAST),
        name="rest_in",
    )(summed, *streamed(inverse, grads, turned, err_in, ortho_in, moment_in))


def rest_out_kernel(place_ref, *refs):
    piece_refs, (inverse_hbm, ortho_out_hbm, moment_hbm) = refs[:4], refs[4:7]
    rest_hbm, factor_hbm, inverse_scr, ortho_out_scr, moment_scr, rest_scr, factor_scr, first_sem, in_sem, out_sem = refs[7:]
    small = zip((inverse_hbm.at[3], ortho_out_hbm), (inverse_scr, ortho_out_scr))
    first = [pltpu.make_async_copy(a, b, first_sem.at[i]) for i, (a, b) in enumerate(small)]

    def column(j):
        at = lax.rem(place_ref[0] + j // 4, 2) * 4 + lax.rem(place_ref[1] + 4 - j % 4, 4)
        return pl.ds(pl.multiple_of(at * COLS, COLS), COLS)

    into = [pltpu.make_async_copy(moment_hbm.at[:, column(j)], moment_scr.at[j], in_sem.at[j]) for j in range(8)]
    out = [
        (
            pltpu.make_async_copy(rest_scr.at[j], rest_hbm.at[:, column(j)], out_sem.at[0, j]),
            pltpu.make_async_copy(factor_scr.at[j], factor_hbm.at[:, column(j)], out_sem.at[1, j]),
        )
        for j in range(8)
    ]
    for copy in first:
        copy.start()
    for copy in into:
        copy.start()
    for copy in first:
        copy.wait()
    high, low = split2(ortho_out_scr[...])
    stack = jnp.concatenate([high, high, low, jnp.zeros_like(low)], axis=0)
    both = stack.astype(f32).T.astype(bf16)
    inverse = inverse_scr[:, RANK:]
    for j in range(0, 8, 2):
        mine = slice(PIECE * (j // 4), PIECE * (j // 4 + 1))
        right = jnp.concatenate([wide(piece_refs[k % 4][mine, :], RANK) for k in (j, j + 1)], axis=1)
        factor = thrice(inverse, right * (1.0 / N_DP))
        high, low = split2(-factor)
        for k in (j, j + 1):
            into[k].wait()
        total = nn(both, jnp.concatenate([high, low, high, jnp.zeros_like(low)], axis=0))
        for i, k in enumerate((j, j + 1)):
            mine = slice(COLS * i, COLS * (i + 1))
            factor_scr[k] = factor[:, mine]
            rest_scr[k] = (total[:, mine] + moment_scr[k]).astype(bf16)
            for copy in out[k]:
                copy.start()
    for pair in out:
        for copy in pair:
            copy.wait()


def rest_out(place, pieces, inverse, ortho_out, moment_out):
    whole = pl.BlockSpec(memory_space=pltpu.VMEM)
    return pl.pallas_call(
        rest_out_kernel,
        in_specs=[pl.BlockSpec(memory_space=pltpu.SMEM)] + [whole] * 4 + [ANY] * 3,
        out_specs=[ANY, ANY],
        scratch_shapes=[
            pltpu.VMEM((RANK, 128), f32),
            pltpu.VMEM((RANK, COLS), f32),
            pltpu.VMEM((8, COLS, COLS), f32),
            pltpu.VMEM((8, COLS, COLS), bf16),
            pltpu.VMEM((8, RANK, COLS), f32),
            pltpu.SemaphoreType.DMA((2,)),
            pltpu.SemaphoreType.DMA((8,)),
            pltpu.SemaphoreType.DMA((2, 8)),
        ],
        out_shape=[pltpu.HBM((COLS, D), bf16), pltpu.HBM((RANK, D), f32)],
        cost_estimate=cost(6),
        compiler_params=pltpu.CompilerParams(vmem_limit_bytes=VMEM),
        name="rest_out",
    )(place, *pieces, *streamed(inverse, ortho_out, moment_out))


CHIP = ("x", "y", "z")
SWAP = [(0, 1), (1, 0)]
OTHERS = (2, 1, 3)


def ring(shift):
    return [(a, (a + shift) % 4) for a in range(4)]


def shards(inputs, grad_y, q_pre, f_pre, v_pre, w_out, err_in, err_out, basis_in, basis_out):
    keep = (err_in[0], err_out[0], inputs, grad_y)
    core = lax.axis_index("c").astype(jnp.int32)
    z = lax.axis_index("z").astype(jnp.int32)
    me = (lax.axis_index("x") * 4 + lax.axis_index("y")).astype(jnp.int32) * 4 + z
    mine = core[None]
    theirs = 1 - mine
    place = jnp.stack([core, z])
    q_pre, place, mine, theirs, me = lax.optimization_barrier((q_pre, place, mine, theirs, me[None]))
    hidden, grads, near_err_in, near_err_out, near_inputs, near_grad_y = recurrence(
        grad_y, w_out, q_pre, f_pre, v_pre, keep
    )
    err_in, err_out = keep[:2]
    send = left(theirs, near_inputs, grads, near_err_in, basis_in)
    arrived = lax.ppermute(send, "c", SWAP)
    left_out_part = left_out(near_grad_y, hidden, near_err_out, basis_out)
    rows = left(mine, near_inputs, grads, near_err_in, basis_in, arrived, left_out_part)

    rows, hidden_now = lax.optimization_barrier((rows, hidden))
    received = lax.all_to_all(rows.reshape(CHIPS, EACH1, 128), CHIP, 0, 0)
    inputs_turned, moment_in, moment_out = ahead(inputs, grads, err_in, hidden_now, grad_y, err_out)
    received, inputs_turned = lax.optimization_barrier((received, inputs_turned))
    own = lax.all_to_all(answer_left(me, received), CHIP, 0, 0).reshape(ROWS1, 128)
    other = lax.ppermute(own, "c", SWAP)
    left_out_sum = own[L_ROWS : L_ROWS + LO_ROWS]

    send, keep_out, near_inputs, near_err_in = right_out(
        place, left_out_sum, grad_y, hidden, err_out, inputs, err_in
    )
    arrived = lax.ppermute(send, "c", SWAP)
    arrived, near_inputs = lax.optimization_barrier((arrived, near_inputs))
    gram_out = send[RO_ROWS:] + arrived[RO_ROWS:]
    quarters = (keep_out + arrived[:RO_ROWS]).reshape(4, PIECE, 128)
    pieces = [jnp.concatenate([quarters[shift], gram_out]) for shift in range(4)]
    pieces = [pieces[0]] + [lax.ppermute(pieces[shift], "z", ring(shift)) for shift in OTHERS]
    right_part = right_own(theirs, own, near_inputs, near_err_in, inputs, err_in)
    right_part, own = lax.optimization_barrier((right_part, own))
    gram_in = gram(own, other)
    rows, gram_out = join(right_other(other, *right_part, grads), *pieces)
    rows, gram_in = lax.optimization_barrier((rows, gram_in))

    received = lax.all_to_all(rows.reshape(N_DP, EACH2, 128), ("x", "y"), 0, 0)
    inverse, ortho_out = invert(gram_in, left_out_sum, gram_out)
    received, inverse, ortho_out = lax.optimization_barrier((received, inverse, ortho_out))
    everywhere = answer_right(received)
    everywhere, inverse = lax.optimization_barrier((everywhere, inverse))
    summed = lax.all_to_all(everywhere, ("x", "y"), 0, 0).reshape(ROWS2, 128)
    ortho_in = turn(mine, own, other, inverse)
    summed, ortho_in = lax.optimization_barrier((summed, ortho_in))

    piece = summed[RI_ROWS:]
    pieces = [jnp.concatenate([piece, lax.ppermute(piece, "c", SWAP)])]
    pieces += [lax.ppermute(pieces[0], "z", ring(shift)) for shift in (1, 2, 3)]
    new_in, factor_in = rest_in(summed, inverse, grads, inputs_turned, err_in, ortho_in, moment_in)
    new_out, factor_out = rest_out(place, pieces, inverse, ortho_out, moment_out)
    return new_in[None], new_out[None], factor_in, factor_out


def solution(mesh):
    fine = Mesh(mesh.devices.reshape(4, 4, 4, 2), ("x", "y", "z", "c"))
    dp, head = ("x", "y"), ("z", "c")
    placed = (
        P(dp, None),
        P(dp, None),
        P(dp, head),
        P(dp, head),
        P(dp, head),
        P(head, None),
        P(dp, None, None, head),
        P(dp, head, None),
        P(None, None, head),
        P(),
    )
    return jax.shard_map(
        shards,
        mesh=fine,
        in_specs=placed,
        out_specs=(P(dp, None, None, head), P(dp, head, None), P(None, None, head), P()),
        check_vma=False,
    )
```
